32 devices in a mesh: grp: 4 (over z), sub: 8 (over y, x, core).
Axes of the slice: x: 2, y: 2, z: 4, core: 2. Of those that a mesh axis runs over, the one named last changes fastest.
Arguments:
- residual: float32 [8, 24576], P(None, 'sub'), may hold values from -6 to 6
- margin: int32 [8, 8], replicated, may hold values from 0 to 191, as said below
- aggregate: int32 [192], P('sub'), may hold values from 0 to 63
- local_factor: bfloat16 [8, 4096, 4096], P('sub', 'grp'), may hold values from -0.09375 to 0.09375
- coarse_factor: bfloat16 [8192, 8192], P('sub'), may hold values from -0.0625 to 0.0625
Outputs:
- preconditioned: float32 [8, 24576], P('grp', 'sub')
The draws below stay inside these ranges and needn't reach their ends.
Inputs may be any that keep to these rules, and one draw needn't show every extreme that they name: `margin`: for subdomain s, every entry names a block owned by another subdomain (block b is owned by subdomain b // 24); the entries of one row are distinct. Up to 8 entries of one row may name blocks of the same owner, and in every draw some row takes all of its entries from a single owner. `aggregate`: the counts of global blocks for each coarse block are whole numbers and may cross devices as int32.
All inputs are finite; a program needn't handle non-finite values.
Results may differ from the reference program's by a relative error of at most 0.0033.
Values sent between devices are 32-bit elements; how exact they have to be, the bound alone decides.
No kernel may reach another device: no remote copies, remote signals or barrier semaphores. Data moves between devices by JAX's collectives and lax.ppermute only.
A program may use at most 64 MiB of HBM per device.

```python
import math
import jax
import jax.numpy as jnp
import numpy as np
from jax import lax

BLK = 128
SUBB = 32
HALO = 8
NCB = 64
NRHS = 8
OWN = 24
SUBN = 4096
NC = 8192
NFB = 192
NCELL = 24576
N_SUB = 8


def draw_margin(key, part):
    base = jax.random.fold_in(key, 11)
    first_key, second_key, third_key, fourth_key, fifth_key = jax.random.split(base, 5)
    distance = jax.random.randint(first_key, (N_SUB, HALO), 1, N_SUB)
    far_slot = jax.random.randint(third_key, (N_SUB, 1), 0, HALO)
    slot_ids = jnp.arange(HALO, dtype=jnp.int32)[None, :]
    distance = jnp.where(slot_ids == far_slot, N_SUB // 2, distance)
    full_row = jax.random.randint(fourth_key, (), 0, N_SUB)
    full_distance = jax.random.randint(fifth_key, (), 1, N_SUB)
    row_ids = jnp.arange(N_SUB, dtype=jnp.int32)[:, None]
    distance = jnp.where(row_ids == full_row, full_distance, distance)
    owners = (jnp.arange(N_SUB, dtype=jnp.int32)[:, None] + distance) % N_SUB
    subkeys = jax.random.split(second_key, N_SUB)

    def slot_row(row_key):
        return jax.random.permutation(row_key, OWN)[:HALO]
    in_slot = jax.vmap(slot_row)(subkeys)
    return (owners * OWN + in_slot).astype(jnp.int32)


def with_ends(drawn, own_key, low, high):
    longest = drawn.shape.index(max(drawn.shape))
    spots = []
    for shift in (0, 1):
        where = [jax.random.randint(jax.random.fold_in(own_key, axis), (), 0, length) for axis, length in enumerate(drawn.shape)]
        where[longest] = (where[longest] + shift) % drawn.shape[longest]
        spots.append(tuple(where))
    return drawn.at[spots[0]].set(low).at[spots[1]].set(high)


def level_of(rng, extent, shards, low, top_value):
    level, own = 1.0, jax.random.fold_in(rng, 6)
    for axis_at, shards_of in shards:
        heights = jnp.exp(jax.random.uniform(jax.random.fold_in(own, axis_at), (shards_of,), jnp.float32, low / len(shards), top_value / len(shards)))
        level = level * jnp.repeat(heights, extent[axis_at] // shards_of).reshape([-1 if axis == axis_at else 1 for axis in range(len(extent))])
    return level


def rank_table(count, slope):
    weights = [(1 << 20) // math.isqrt(grade ** slope) + 1 for grade in range(1, count + 1)]
    width = 1 + sum(weights) // (1 << 30)
    return np.cumsum(np.array([max(1, weight // width) for weight in weights]))


def ranked_ids(key, shape, number_of, slope):
    listing = rank_table(number_of, slope)
    pick = jax.random.randint(jax.random.fold_in(key, 1), shape, 0, int(listing[number_of - 1]))
    standing = jnp.searchsorted(jnp.asarray(listing, jnp.int32), pick, side="right")
    return jax.random.permutation(jax.random.fold_in(key, 2), number_of)[standing].astype(jnp.int32)


def noise(stream_key, dims, width, limit, cuts=(), kind=jnp.bfloat16):
    array = jax.random.normal(stream_key, dims, jnp.float32) * width
    if len(cuts) > 0:
        array = level_of(stream_key, dims, cuts, -0.22, 0.18) * array
    return jnp.clip(array, min=-limit, max=limit).astype(kind)


def setup_inputs(seed: int = 0) -> dict:
    key_of = jax.random.split(jax.random.key(seed), 6)
    return {
        "residual": noise(key_of[0], (NRHS, NCELL), 1.0, 6.0, ((1, 8),), jnp.float32),
        "margin": draw_margin(jax.random.fold_in(key_of[5], 71), 0),
        "aggregate": with_ends(ranked_ids(key_of[2], (NFB,), NCB, 2), jax.random.fold_in(key_of[2], 3), 0, NCB - 1).astype(jnp.int32),
        "local_factor": noise(key_of[3], (N_SUB, SUBN, SUBN), SUBN ** -0.5, 0.09375, ((0, 8), (1, 4))),
        "coarse_factor": noise(key_of[4], (NC, NC), NC ** -0.5, 0.0625, ((0, 8),)),
    }


def reference(residual, margin, aggregate, local_factor, coarse_factor):
    blocks = residual.reshape(NRHS, NFB, BLK)
    own_ids = jnp.arange(NFB, dtype=jnp.int32).reshape(N_SUB, OWN)
    block_ids = jnp.concatenate([own_ids, margin.astype(jnp.int32)], axis=1)

    def subdomain(summed, pieces):
        chosen, factor = pieces
        local_rhs = blocks[:, chosen, :].reshape(NRHS, SUBN).astype(jnp.bfloat16)
        inner_term = jnp.dot(local_rhs, factor.T, preferred_element_type=jnp.float32).astype(jnp.bfloat16)
        local_sol = jnp.dot(inner_term, factor, preferred_element_type=jnp.float32)
        summed = summed.at[:, chosen, :].add(local_sol.reshape(NRHS, SUBB, BLK))
        return summed, None

    summed, _ = lax.scan(subdomain, jnp.zeros((NRHS, NFB, BLK), jnp.float32), (block_ids, local_factor))
    catalog = jnp.arange(NCB, dtype=jnp.int32)
    member = (aggregate[:, None] == catalog[None, :]).astype(jnp.float32)
    sums = jnp.einsum('rbk,bj->rjk', blocks, member, precision=lax.Precision.HIGHEST)
    counts = jnp.sum(member, axis=0)
    coarse_rhs = (sums / jnp.maximum(counts, 1.0)[None, :, None]).reshape(NRHS, NC).astype(jnp.bfloat16)
    inner_coarse = jnp.dot(coarse_rhs, coarse_factor.T, preferred_element_type=jnp.float32).astype(jnp.bfloat16)
    coarse_sol = jnp.dot(inner_coarse, coarse_factor, preferred_element_type=jnp.float32)
    prolonged = jnp.einsum('rjk,bj->rbk', coarse_sol.reshape(NRHS, NCB, BLK), member, precision=lax.Precision.HIGHEST)
    return (summed + prolonged).reshape(NRHS, NCELL)
```

```python
import functools

import jax
import jax.numpy as jnp
from jax import lax
from jax.experimental import pallas as pl
from jax.experimental.pallas import tpu as pltpu
from jax.sharding import PartitionSpec as P

BLK = 128
MIB = 1024 * 1024
VMEM = pl.BlockSpec(memory_space=pltpu.VMEM)
SMEM = pl.BlockSpec(memory_space=pltpu.SMEM)
NT = (((1,), (1,)), ((), ()))
TN = (((0,), (0,)), ((), ()))


def call(kernel, out, specs, scratch=(), limit=12 * MIB, flops=0, moved=0, **options):
    return pl.pallas_call(
        kernel,
        out_shape=out,
        in_specs=specs,
        out_specs=VMEM,
        scratch_shapes=scratch,
        compiler_params=pltpu.CompilerParams(vmem_limit_bytes=limit),
        cost_estimate=pl.CostEstimate(flops=flops, bytes_accessed=moved, transcendentals=0),
        **options,
    )


def mm(left, right, dims=(((1,), (0,)), ((), ()))):
    return lax.dot_general(left, right, dims, preferred_element_type=jnp.float32)


def split3(value):
    high = value.astype(jnp.bfloat16)
    rest = value - high.astype(jnp.float32)
    middle = rest.astype(jnp.bfloat16)
    low = (rest - middle.astype(jnp.float32)).astype(jnp.bfloat16)
    return [high, middle, low]


def pack_kernel(own, rows, pad, margin, aggregate, residual, out, block_rows):
    targets, halo = margin.shape
    rhs = residual.shape[0]
    me = lax.axis_index("sub")
    first = lax.axis_index("grp") * rows
    for b in range(own):
        block_rows[pl.ds(b, rhs, stride=own), :] = residual[:, b * BLK : (b + 1) * BLK]
    mine = block_rows[pl.ds(pl.multiple_of(first * own, 8), rows * own), :]
    names = aggregate[...].astype(jnp.float32)
    at = own * rows
    for t in range(targets):
        out[t, :at, :] = mine
        out[t, at : at + pad, :] = jnp.zeros((pad, BLK), jnp.float32)
        out[t, at : at + 1, :own] = names
        for k in range(halo):
            slot = jnp.clip(margin[t, k] - me * own, 0, own - 1)
            out[t, at + pad + k * rhs : at + pad + (k + 1) * rhs, :] = residual[
                :, pl.ds(pl.multiple_of(slot * BLK, BLK), BLK)
            ]


def fine_kernel(own, start, chunk, margin, residual, arrived, factor, out, inner):
    rhs = residual.shape[0]
    halo = margin.shape[1]
    depth, width = factor.shape[1:]
    blocks = width // BLK
    me = lax.axis_index("sub")
    tiles = [residual[...].astype(jnp.bfloat16)]
    for k in range(halo):
        owner = margin[me, k] // own
        tiles.append(arrived[owner, start + k * rhs : start + (k + 1) * rhs, :].astype(jnp.bfloat16))
    local = jnp.concatenate(tiles, axis=1)
    for n in range(depth // chunk):
        span = slice(n * chunk, (n + 1) * chunk)
        inner[:, span] = mm(local, factor[0, span, :], NT)
    mid = inner[...].astype(jnp.bfloat16)
    for n in range(width // chunk):
        part = mm(mid, factor[0, :, n * chunk : (n + 1) * chunk])
        for i in range(chunk // BLK):
            b = n * (chunk // BLK) + i
            out[pl.ds(b, rhs, stride=blocks), :] = part[:, i * BLK : (i + 1) * BLK]


def coarse_kernel(own, rows, chunk, arrived, factor, out, table, inner):
    sources = arrived.shape[0]
    depth, width = factor.shape
    coarse = width // BLK
    names = arrived[:, own * rows, :].T
    catalog = lax.broadcasted_iota(jnp.int32, (own, coarse), 1).astype(jnp.float32)
    member = jnp.concatenate(
        [(names[:own, s : s + 1] == catalog).astype(jnp.float32) for s in range(sources)], axis=0
    ).astype(jnp.bfloat16)
    whole = jnp.concatenate(
        [
            jnp.concatenate([arrived[s, r * own : (r + 1) * own, :] for s in range(sources)], axis=0)
            for r in range(rows)
        ],
        axis=1,
    )
    ones = jnp.ones((own * sources, BLK), jnp.bfloat16)
    span = rows * BLK
    found = mm(member, jnp.concatenate(split3(whole) + [ones], axis=1), TN)
    sums = found[:, :span] + found[:, span : 2 * span] + found[:, 2 * span : 3 * span]
    counts = jnp.maximum(found[:, 3 * span :], 1.0)
    for r in range(rows):
        table[r * coarse : (r + 1) * coarse, :] = sums[:, r * BLK : (r + 1) * BLK] / counts
    right = jnp.concatenate(
        [table[pl.ds(j, rows, stride=coarse), :] for j in range(coarse)], axis=1
    ).astype(jnp.bfloat16)
    for n in range(depth // chunk):
        inner[:, n * chunk : (n + 1) * chunk] = mm(right, factor[n * chunk : (n + 1) * chunk, :], NT)
    mid = inner[...].astype(jnp.bfloat16)
    for n in range(width // chunk):
        part = mm(mid, factor[:, n * chunk : (n + 1) * chunk])
        for i in range(chunk // BLK):
            j = n * (chunk // BLK) + i
            table[pl.ds(j, rows, stride=coarse), :] = part[:, i * BLK : (i + 1) * BLK]
    solved = jnp.concatenate([table[r * coarse : (r + 1) * coarse, :] for r in range(rows)], axis=1)
    spread = mm(member, jnp.concatenate(split3(solved), axis=1))
    spread = spread[:, :span] + spread[:, span : 2 * span] + spread[:, 2 * span :]
    for s in range(sources):
        for r in range(rows):
            out[s, r * own : (r + 1) * own, :] = spread[
                s * own : (s + 1) * own, r * BLK : (r + 1) * BLK
            ]


def merge_kernel(own, rows, margin, arrived, spread, out, total):
    halo = margin.shape[1]
    blocks = own + halo
    me = lax.axis_index("sub")
    summed = arrived[0]
    for g in range(1, arrived.shape[0]):
        summed = summed + arrived[g]
    total[...] = summed
    out[...] = spread[...]
    for r in range(rows):
        here = out[me, r * own : (r + 1) * own, :]
        out[me, r * own : (r + 1) * own, :] = here + total[r * blocks : r * blocks + own, :]
    for k in range(halo):
        block = margin[me, k]
        owner = block // own
        slot = block - owner * own
        where = pl.ds(slot, rows, stride=own)
        out[owner, where, :] = out[owner, where, :] + total[pl.ds(own + k, rows, stride=blocks), :]


def last_kernel(own, rows, arrived, out, total):
    summed = arrived[0]
    for s in range(1, arrived.shape[0]):
        summed = summed + arrived[s]
    total[...] = summed
    for b in range(own):
        out[:, b * BLK : (b + 1) * BLK] = total[pl.ds(b, rows, stride=own), :]


def on_device(residual, margin, aggregate, local_factor, coarse_factor):
    sub_count = lax.axis_size("sub")
    grp_count = lax.axis_size("grp")
    rhs, own_width = residual.shape
    own = own_width // BLK
    rows = rhs // grp_count
    halo = margin.shape[1]
    pad = 8
    start = own * rows + pad
    f32 = jnp.float32
    sds = jax.ShapeDtypeStruct
    _, depth, width = local_factor.shape
    coarse_depth, coarse_width = coarse_factor.shape
    blocks = width // BLK

    local_factor = pltpu.with_memory_space_constraint(local_factor, pltpu.VMEM)
    coarse_factor = pltpu.with_memory_space_constraint(coarse_factor, pltpu.VMEM)

    outgoing = call(
        functools.partial(pack_kernel, own, rows, pad),
        sds((sub_count, start + halo * rhs, BLK), f32),
        [SMEM, VMEM, VMEM],
        [pltpu.VMEM((own * rhs, BLK), f32)],
    )(margin, aggregate.reshape(1, own), residual)
    arrived = lax.all_to_all(outgoing, "sub", split_axis=0, concat_axis=0, tiled=True)
    fine = call(
        functools.partial(fine_kernel, own, start, 256),
        sds((rhs * blocks, BLK), f32),
        [SMEM, VMEM, VMEM, VMEM],
        [pltpu.VMEM((rhs, depth), f32)],
        flops=4 * rhs * depth * width,
        moved=2 * depth * width,
    )(margin, residual, arrived, local_factor)
    panels = lax.all_to_all(
        fine.reshape(grp_count, rows * blocks, BLK), "grp", split_axis=0, concat_axis=0, tiled=True
    )
    spread = call(
        functools.partial(coarse_kernel, own, rows, 256),
        sds((sub_count, own * rows, BLK), f32),
        [VMEM, VMEM],
        [pltpu.VMEM((rows * (coarse_width // BLK), BLK), f32), pltpu.VMEM((rows, coarse_depth), f32)],
        flops=4 * rows * coarse_depth * coarse_width,
        moved=2 * coarse_depth * coarse_width,
    )(arrived, coarse_factor)
    merged = call(
        functools.partial(merge_kernel, own, rows),
        sds((sub_count, own * rows, BLK), f32),
        [SMEM, VMEM, VMEM],
        [pltpu.VMEM((rows * blocks, BLK), f32)],
    )(margin, panels, spread)
    back = lax.all_to_all(merged, "sub", split_axis=0, concat_axis=0, tiled=True)
    return call(
        functools.partial(last_kernel, own, rows),
        sds((rows, own_width), f32),
        [VMEM],
        [pltpu.VMEM((own * rows, BLK), f32)],
    )(back)


def solution(mesh):
    placed = (P(None, "sub"), P(), P("sub"), P("sub", "grp", None), P("sub", None))
    return jax.shard_map(
        on_device, mesh=mesh, in_specs=placed, out_specs=P("grp", "sub"), check_vma=False
    )
```

```python
import functools

import jax
import jax.numpy as jnp
from jax import lax
from jax.experimental import pallas as pl
from jax.experimental.pallas import tpu as pltpu
from jax.sharding import PartitionSpec as P

BLK = 128
MIB = 1024 * 1024
VMEM = pl.BlockSpec(memory_space=pltpu.VMEM)
SMEM = pl.BlockSpec(memory_space=pltpu.SMEM)
HBM = pl.BlockSpec(memory_space=pltpu.HBM)
NT = (((1,), (1,)), ((), ()))
TN = (((0,), (0,)), ((), ()))


def call(kernel, out, specs, scratch=(), limit=12 * MIB, flops=0, moved=0, **options):
    return pl.pallas_call(
        kernel,
        out_shape=out,
        in_specs=specs,
        out_specs=jax.tree.map(lambda _: VMEM, out),
        scratch_shapes=scratch,
        compiler_params=pltpu.CompilerParams(vmem_limit_bytes=limit),
        cost_estimate=pl.CostEstimate(flops=flops, bytes_accessed=moved, transcendentals=0),
        **options,
    )


def mm(left, right, dims=(((1,), (0,)), ((), ()))):
    return lax.dot_general(left, right, dims, preferred_element_type=jnp.float32)


def split3(value):
    high = value.astype(jnp.bfloat16)
    rest = value - high.astype(jnp.float32)
    middle = rest.astype(jnp.bfloat16)
    low = (rest - middle.astype(jnp.float32)).astype(jnp.bfloat16)
    return [high, middle, low]


def pack_kernel(
    own, rows, pad, margin_hbm, aggregate_hbm, residual_hbm, out, block_rows, margin, aggregate, residual, sems
):
    pairs = ((residual_hbm, residual), (margin_hbm, margin), (aggregate_hbm, aggregate))
    copies = [pltpu.make_async_copy(a, b, sems.at[i]) for i, (a, b) in enumerate(pairs)]
    for copy in copies:
        copy.start()
    for copy in copies:
        copy.wait()
    targets, halo = margin.shape
    rhs = residual.shape[0]
    me = lax.axis_index("sub")
    first = lax.axis_index("grp") * rows
    for b in range(own):
        block_rows[pl.ds(b, rhs, stride=own), :] = residual[:, b * BLK : (b + 1) * BLK]
    mine = block_rows[pl.ds(pl.multiple_of(first * own, 8), rows * own), :]
    names = aggregate[...].astype(jnp.float32)
    at = own * rows
    for t in range(targets):
        out[t, :at, :] = mine
        out[t, at : at + pad, :] = jnp.zeros((pad, BLK), jnp.float32)
        out[t, at : at + 1, :own] = names
        for k in range(halo):
            slot = jnp.clip(margin[t, k] - me * own, 0, own - 1)
            out[t, at + pad + k * rhs : at + pad + (k + 1) * rhs, :] = residual[
                :, pl.ds(pl.multiple_of(slot * BLK, BLK), BLK)
            ]


def load_kernel(chunk, residual_hbm, fine_hbm, coarse_hbm, inner, fine, coarse, residual, sems):
    depth = fine.shape[1]
    own_width = residual.shape[1]
    first = pltpu.make_async_copy(residual_hbm, residual, sems.at[0])
    first.start()
    copies = []
    for n in range(depth // chunk):
        span = pl.ds(n * chunk, chunk)
        copies.append(
            pltpu.make_async_copy(fine_hbm.at[0, span], fine.at[0, span], sems.at[1 + n])
        )
    last = []
    for n in range(coarse.shape[0] // chunk):
        span = pl.ds(n * chunk, chunk)
        last.append(
            pltpu.make_async_copy(
                coarse_hbm.at[span], coarse.at[span], sems.at[1 + len(copies) + n]
            )
        )
    for copy in copies + last:
        copy.start()
    first.wait()
    local = residual[...].astype(jnp.bfloat16)
    for n, copy in enumerate(copies):
        copy.wait()
        span = slice(n * chunk, (n + 1) * chunk)
        inner[:, span] = mm(local, fine[0, span, :own_width], NT)
    for copy in last:
        copy.wait()


def fine_kernel(own, start, chunk, margin, begun, arrived, factor, out, inner):
    rhs = begun.shape[0]
    halo = margin.shape[1]
    depth, width = factor.shape[1:]
    blocks = width // BLK
    me = lax.axis_index("sub")
    tiles = []
    for k in range(halo):
        owner = margin[me, k] // own
        tiles.append(arrived[owner, start + k * rhs : start + (k + 1) * rhs, :].astype(jnp.bfloat16))
    local = jnp.concatenate(tiles, axis=1)
    for n in range(depth // chunk):
        span = slice(n * chunk, (n + 1) * chunk)
        inner[:, span] = begun[:, span] + mm(local, factor[0, span, own * BLK :], NT)
    mid = inner[...].astype(jnp.bfloat16)
    for n in range(width // chunk):
        part = mm(mid, factor[0, :, n * chunk : (n + 1) * chunk])
        for i in range(chunk // BLK):
            b = n * (chunk // BLK) + i
            out[pl.ds(b, rhs, stride=blocks), :] = part[:, i * BLK : (i + 1) * BLK]


def coarse_kernel(own, rows, chunk, arrived, factor, out, table, inner):
    sources = arrived.shape[0]
    depth, width = factor.shape
    coarse = width // BLK
    names = arrived[:, own * rows, :].T
    catalog = lax.broadcasted_iota(jnp.int32, (own, coarse), 1).astype(jnp.float32)
    member = jnp.concatenate(
        [(names[:own, s : s + 1] == catalog).astype(jnp.float32) for s in range(sources)], axis=0
    ).astype(jnp.bfloat16)
    whole = jnp.concatenate(
        [
            jnp.concatenate([arrived[s, r * own : (r + 1) * own, :] for s in range(sources)], axis=0)
            for r in range(rows)
        ],
        axis=1,
    )
    ones = jnp.ones((own * sources, BLK), jnp.bfloat16)
    span = rows * BLK
    found = mm(member, jnp.concatenate(split3(whole) + [ones], axis=1), TN)
    sums = found[:, :span] + found[:, span : 2 * span] + found[:, 2 * span : 3 * span]
    counts = jnp.maximum(found[:, 3 * span :], 1.0)
    for r in range(rows):
        table[r * coarse : (r + 1) * coarse, :] = sums[:, r * BLK : (r + 1) * BLK] / counts
    right = jnp.concatenate(
        [table[pl.ds(j, rows, stride=coarse), :] for j in range(coarse)], axis=1
    ).astype(jnp.bfloat16)
    for n in range(depth // chunk):
        inner[:, n * chunk : (n + 1) * chunk] = mm(right, factor[n * chunk : (n + 1) * chunk, :], NT)
    mid = inner[...].astype(jnp.bfloat16)
    for n in range(width // chunk):
        part = mm(mid, factor[:, n * chunk : (n + 1) * chunk])
        for i in range(chunk // BLK):
            j = n * (chunk // BLK) + i
            table[pl.ds(j, rows, stride=coarse), :] = part[:, i * BLK : (i + 1) * BLK]
    solved = jnp.concatenate([table[r * coarse : (r + 1) * coarse, :] for r in range(rows)], axis=1)
    spread = mm(member, jnp.concatenate(split3(solved), axis=1))
    spread = spread[:, :span] + spread[:, span : 2 * span] + spread[:, 2 * span :]
    for s in range(sources):
        for r in range(rows):
            out[s, r * own : (r + 1) * own, :] = spread[
                s * own : (s + 1) * own, r * BLK : (r + 1) * BLK
            ]


def merge_kernel(own, rows, margin, arrived, spread, out, total):
    halo = margin.shape[1]
    blocks = own + halo
    me = lax.axis_index("sub")
    summed = arrived[0]
    for g in range(1, arrived.shape[0]):
        summed = summed + arrived[g]
    total[...] = summed
    out[...] = spread[...]
    for r in range(rows):
        here = out[me, r * own : (r + 1) * own, :]
        out[me, r * own : (r + 1) * own, :] = here + total[r * blocks : r * blocks + own, :]
    for k in range(halo):
        block = margin[me, k]
        owner = block // own
        slot = block - owner * own
        where = pl.ds(slot, rows, stride=own)
        out[owner, where, :] = out[owner, where, :] + total[pl.ds(own + k, rows, stride=blocks), :]


def last_kernel(own, rows, arrived, out, total):
    summed = arrived[0]
    for s in range(1, arrived.shape[0]):
        summed = summed + arrived[s]
    total[...] = summed
    for b in range(own):
        out[:, b * BLK : (b + 1) * BLK] = total[pl.ds(b, rows, stride=own), :]


def on_device(residual, margin, aggregate, local_factor, coarse_factor):
    sub_count = lax.axis_size("sub")
    grp_count = lax.axis_size("grp")
    rhs, own_width = residual.shape
    own = own_width // BLK
    rows = rhs // grp_count
    halo = margin.shape[1]
    pad = 8
    start = own * rows + pad
    f32 = jnp.float32
    sds = jax.ShapeDtypeStruct
    _, depth, width = local_factor.shape
    coarse_depth, coarse_width = coarse_factor.shape
    blocks = width // BLK

    in_hbm = functools.partial(pltpu.with_memory_space_constraint, memory_space=pltpu.HBM)
    outgoing = call(
        functools.partial(pack_kernel, own, rows, pad),
        sds((sub_count, start + halo * rhs, BLK), f32),
        [HBM, HBM, HBM],
        [
            pltpu.VMEM((own * rhs, BLK), f32),
            pltpu.SMEM(margin.shape, jnp.int32),
            pltpu.VMEM((1, own), jnp.int32),
            pltpu.VMEM(residual.shape, f32),
            pltpu.SemaphoreType.DMA((3,)),
        ],
    )(in_hbm(margin), in_hbm(aggregate.reshape(1, own)), in_hbm(residual))
    arrived = lax.all_to_all(outgoing, "sub", split_axis=0, concat_axis=0, tiled=True)
    chunk = 256
    begun, local_factor, coarse_factor = call(
        functools.partial(load_kernel, chunk),
        (
            sds((rhs, depth), f32),
            sds(local_factor.shape, local_factor.dtype),
            sds(coarse_factor.shape, coarse_factor.dtype),
        ),
        [HBM, HBM, HBM],
        [
            pltpu.VMEM(residual.shape, f32),
            pltpu.SemaphoreType.DMA((1 + depth // chunk + coarse_depth // chunk,)),
        ],
        flops=2 * rhs * depth * own_width,
        moved=2 * depth * width + 2 * coarse_depth * coarse_width,
    )(in_hbm(residual), in_hbm(local_factor), in_hbm(coarse_factor))
    fine = call(
        functools.partial(fine_kernel, own, start, chunk),
        sds((rhs * blocks, BLK), f32),
        [SMEM, VMEM, VMEM, VMEM],
        [pltpu.VMEM((rhs, depth), f32)],
        flops=4 * rhs * depth * width,
        moved=2 * depth * width,
    )(margin, begun, arrived, local_factor)
    panels = lax.all_to_all(
        fine.reshape(grp_count, rows * blocks, BLK), "grp", split_axis=0, concat_axis=0, tiled=True
    )
    spread = call(
        functools.partial(coarse_kernel, own, rows, 256),
        sds((sub_count, own * rows, BLK), f32),
        [VMEM, VMEM],
        [pltpu.VMEM((rows * (coarse_width // BLK), BLK), f32), pltpu.VMEM((rows, coarse_depth), f32)],
        flops=4 * rows * coarse_depth * coarse_width,
        moved=2 * coarse_depth * coarse_width,
    )(arrived, coarse_factor)
    merged = call(
        functools.partial(merge_kernel, own, rows),
        sds((sub_count, own * rows, BLK), f32),
        [SMEM, VMEM, VMEM],
        [pltpu.VMEM((rows * blocks, BLK), f32)],
    )(margin, panels, spread)
    back = lax.all_to_all(merged, "sub", split_axis=0, concat_axis=0, tiled=True)
    return call(
        functools.partial(last_kernel, own, rows),
        sds((rows, own_width), f32),
        [VMEM],
        [pltpu.VMEM((own * rows, BLK), f32)],
    )(back)


def solution(mesh):
    placed = (P(None, "sub"), P(), P("sub"), P("sub", "grp", None), P("sub", None))
    return jax.shard_map(
        on_device, mesh=mesh, in_specs=placed, out_specs=P("grp", "sub"), check_vma=False
    )
```

```python
import functools

import jax
import jax.numpy as jnp
from jax import lax
from jax.experimental import pallas as pl
from jax.experimental.pallas import tpu as pltpu
from jax.sharding import PartitionSpec as P

BLK = 128
MIB = 1024 * 1024
VMEM = pl.BlockSpec(memory_space=pltpu.VMEM)
SMEM = pl.BlockSpec(memory_space=pltpu.SMEM)
HBM = pl.BlockSpec(memory_space=pltpu.HBM)
NT = (((1,), (1,)), ((), ()))
TN = (((0,), (0,)), ((), ()))


def call(kernel, out, specs, scratch=(), limit=12 * MIB, flops=0, moved=0, **options):
    return pl.pallas_call(
        kernel,
        out_shape=out,
        in_specs=specs,
        out_specs=jax.tree.map(lambda _: VMEM, out),
        scratch_shapes=scratch,
        compiler_params=pltpu.CompilerParams(vmem_limit_bytes=limit),
        cost_estimate=pl.CostEstimate(flops=flops, bytes_accessed=moved, transcendentals=0),
        **options,
    )


def mm(left, right, dims=(((1,), (0,)), ((), ()))):
    return lax.dot_general(left, right, dims, preferred_element_type=jnp.float32)


def split3(value):
    high = value.astype(jnp.bfloat16)
    rest = value - high.astype(jnp.float32)
    middle = rest.astype(jnp.bfloat16)
    low = (rest - middle.astype(jnp.float32)).astype(jnp.bfloat16)
    return [high, middle, low]


def pack_kernel(own, rows, pad, margin_hbm, aggregate_hbm, residual_hbm, *refs):
    *outs, block_rows, margin, aggregate, residual, sems = refs
    pairs = ((residual_hbm, residual), (margin_hbm, margin), (aggregate_hbm, aggregate))
    copies = [pltpu.make_async_copy(a, b, sems.at[i]) for i, (a, b) in enumerate(pairs)]
    for copy in copies:
        copy.start()
    for copy in copies:
        copy.wait()
    halo = margin.shape[1]
    rhs = residual.shape[0]
    me = lax.axis_index("sub")
    first = lax.axis_index("grp") * rows
    for b in range(own):
        block_rows[pl.ds(b, rhs, stride=own), :] = residual[:, b * BLK : (b + 1) * BLK]
    mine = block_rows[pl.ds(pl.multiple_of(first * own, 8), rows * own), :]
    names = aggregate[...].astype(jnp.float32)
    at = own * rows
    for d, out in enumerate(outs):
        out[:at, :] = mine
        out[at : at + pad, :] = jnp.zeros((pad, BLK), jnp.float32)
        out[at : at + 1, :own] = names
        if d == 0:
            continue
        target = me ^ d
        for k in range(halo):
            slot = jnp.clip(margin[target, k] - me * own, 0, own - 1)
            out[at + pad + k * rhs : at + pad + (k + 1) * rhs, :] = residual[
                :, pl.ds(pl.multiple_of(slot * BLK, BLK), BLK)
            ]


def load_kernel(chunk, residual_hbm, fine_hbm, coarse_hbm, inner, fine, coarse, residual, sems):
    depth = fine.shape[1]
    own_width = residual.shape[1]
    first = pltpu.make_async_copy(residual_hbm, residual, sems.at[0])
    first.start()
    copies = []
    for n in range(depth // chunk):
        span = pl.ds(n * chunk, chunk)
        copies.append(
            pltpu.make_async_copy(fine_hbm.at[0, span], fine.at[0, span], sems.at[1 + n])
        )
    last = []
    for n in range(coarse.shape[0] // chunk):
        span = pl.ds(n * chunk, chunk)
        last.append(
            pltpu.make_async_copy(
                coarse_hbm.at[span], coarse.at[span], sems.at[1 + len(copies) + n]
            )
        )
    for copy in copies + last:
        copy.start()
    first.wait()
    local = residual[...].astype(jnp.bfloat16)
    for n, copy in enumerate(copies):
        copy.wait()
        span = slice(n * chunk, (n + 1) * chunk)
        inner[:, span] = mm(local, fine[0, span, :own_width], NT)
    for copy in last:
        copy.wait()


def fine_kernel(own, rows, start, chunk, sources, margin, begun, factor, *refs):
    arrived = (None, *refs[: sources - 1])
    *outs, inner, table = refs[sources - 1 :]
    rhs = begun.shape[0]
    halo = margin.shape[1]
    depth, width = factor.shape[1:]
    blocks = width // BLK
    me = lax.axis_index("sub")
    group = lax.axis_index("grp")
    tiles = []
    for k in range(halo):
        away = me ^ (margin[me, k] // own)
        span = slice(start + k * rhs, start + (k + 1) * rhs)
        tile = arrived[1][span, :]
        for d in range(2, sources):
            tile = jnp.where(away == d, arrived[d][span, :], tile)
        tiles.append(tile.astype(jnp.bfloat16))
    local = jnp.concatenate(tiles, axis=1)
    for n in range(depth // chunk):
        span = slice(n * chunk, (n + 1) * chunk)
        inner[:, span] = begun[:, span] + mm(local, factor[0, span, own * BLK :], NT)
    mid = inner[...].astype(jnp.bfloat16)
    for n in range(width // chunk):
        part = mm(mid, factor[0, :, n * chunk : (n + 1) * chunk])
        for i in range(chunk // BLK):
            b = n * (chunk // BLK) + i
            table[pl.ds(b, rhs, stride=blocks), :] = part[:, i * BLK : (i + 1) * BLK]
    size = rows * blocks
    for d, out in enumerate(outs):
        out[...] = table[pl.ds(pl.multiple_of((group ^ d) * size, 8), size), :]


def coarse_kernel(own, rows, chunk, sources, factor, *refs):
    arrived = refs[:sources]
    out, table, inner = refs[sources:]
    depth, width = factor.shape
    coarse = width // BLK
    names = [part[own * rows : own * rows + 1, :] for part in arrived]
    names = jnp.concatenate(names, axis=0).T
    catalog = lax.broadcasted_iota(jnp.int32, (own, coarse), 1).astype(jnp.float32)
    member = jnp.concatenate(
        [(names[:own, s : s + 1] == catalog).astype(jnp.float32) for s in range(sources)], axis=0
    ).astype(jnp.bfloat16)
    whole = jnp.concatenate(
        [
            jnp.concatenate([part[r * own : (r + 1) * own, :] for part in arrived], axis=0)
            for r in range(rows)
        ],
        axis=1,
    )
    ones = jnp.ones((own * sources, BLK), jnp.bfloat16)
    span = rows * BLK
    found = mm(member, jnp.concatenate(split3(whole) + [ones], axis=1), TN)
    sums = found[:, :span] + found[:, span : 2 * span] + found[:, 2 * span : 3 * span]
    counts = jnp.maximum(found[:, 3 * span :], 1.0)
    for r in range(rows):
        table[r * coarse : (r + 1) * coarse, :] = sums[:, r * BLK : (r + 1) * BLK] / counts
    right = jnp.concatenate(
        [table[pl.ds(j, rows, stride=coarse), :] for j in range(coarse)], axis=1
    ).astype(jnp.bfloat16)
    for n in range(depth // chunk):
        inner[:, n * chunk : (n + 1) * chunk] = mm(right, factor[n * chunk : (n + 1) * chunk, :], NT)
    mid = inner[...].astype(jnp.bfloat16)
    for n in range(width // chunk):
        part = mm(mid, factor[:, n * chunk : (n + 1) * chunk])
        for i in range(chunk // BLK):
            j = n * (chunk // BLK) + i
            table[pl.ds(j, rows, stride=coarse), :] = part[:, i * BLK : (i + 1) * BLK]
    solved = jnp.concatenate([table[r * coarse : (r + 1) * coarse, :] for r in range(rows)], axis=1)
    spread = mm(member, jnp.concatenate(split3(solved), axis=1))
    spread = spread[:, :span] + spread[:, span : 2 * span] + spread[:, 2 * span :]
    for s in range(sources):
        for r in range(rows):
            out[s, r * own : (r + 1) * own, :] = spread[
                s * own : (s + 1) * own, r * BLK : (r + 1) * BLK
            ]


def merge_kernel(own, rows, groups, margin, spread, *refs):
    arrived = refs[:groups]
    *outs, total, field = refs[groups:]
    halo = margin.shape[1]
    blocks = own + halo
    me = lax.axis_index("sub")
    summed = arrived[0][...]
    for part in arrived[1:]:
        summed = summed + part[...]
    total[...] = summed
    field[...] = spread[...]
    for r in range(rows):
        span = slice(r * own, (r + 1) * own)
        field[0, span, :] = field[0, span, :] + total[r * blocks : r * blocks + own, :]
    for k in range(halo):
        block = margin[me, k]
        owner = block // own
        where = pl.ds(block - owner * own, rows, stride=own)
        away = me ^ owner
        field[away, where, :] = field[away, where, :] + total[pl.ds(own + k, rows, stride=blocks), :]
    for d, out in enumerate(outs):
        out[...] = field[d]


def last_kernel(own, rows, *refs):
    *arrived, out, total = refs
    summed = arrived[0][...]
    for part in arrived[1:]:
        summed = summed + part[...]
    total[...] = summed
    for b in range(own):
        out[:, b * BLK : (b + 1) * BLK] = total[pl.ds(b, rows, stride=own), :]


def exchange(parts, axis):
    count = lax.axis_size(axis)
    return [parts[0]] + [
        lax.ppermute(parts[d], axis, [(i, i ^ d) for i in range(count)]) for d in range(1, count)
    ]


def on_device(residual, margin, aggregate, local_factor, coarse_factor):
    sub_count = lax.axis_size("sub")
    grp_count = lax.axis_size("grp")
    rhs, own_width = residual.shape
    own = own_width // BLK
    rows = rhs // grp_count
    halo = margin.shape[1]
    pad = 8
    start = own * rows + pad
    f32 = jnp.float32
    sds = jax.ShapeDtypeStruct
    _, depth, width = local_factor.shape
    coarse_depth, coarse_width = coarse_factor.shape
    blocks = width // BLK

    in_hbm = functools.partial(pltpu.with_memory_space_constraint, memory_space=pltpu.HBM)
    outgoing = call(
        functools.partial(pack_kernel, own, rows, pad),
        [sds((start, BLK), f32)] + [sds((start + halo * rhs, BLK), f32)] * (sub_count - 1),
        [HBM, HBM, HBM],
        [
            pltpu.VMEM((own * rhs, BLK), f32),
            pltpu.SMEM(margin.shape, jnp.int32),
            pltpu.VMEM((1, own), jnp.int32),
            pltpu.VMEM(residual.shape, f32),
            pltpu.SemaphoreType.DMA((3,)),
        ],
    )(in_hbm(margin), in_hbm(aggregate.reshape(1, own)), in_hbm(residual))
    arrived = exchange(outgoing, "sub")
    chunk = 256
    begun, local_factor, coarse_factor = call(
        functools.partial(load_kernel, chunk),
        (
            sds((rhs, depth), f32),
            sds(local_factor.shape, local_factor.dtype),
            sds(coarse_factor.shape, coarse_factor.dtype),
        ),
        [HBM, HBM, HBM],
        [
            pltpu.VMEM(residual.shape, f32),
            pltpu.SemaphoreType.DMA((1 + depth // chunk + coarse_depth // chunk,)),
        ],
        flops=2 * rhs * depth * own_width,
        moved=2 * depth * width + 2 * coarse_depth * coarse_width,
    )(in_hbm(residual), in_hbm(local_factor), in_hbm(coarse_factor))
    fine = call(
        functools.partial(fine_kernel, own, rows, start, chunk, sub_count),
        [sds((rows * blocks, BLK), f32)] * grp_count,
        [SMEM] + [VMEM] * (sub_count + 1),
        [pltpu.VMEM((rhs, depth), f32), pltpu.VMEM((rhs * blocks, BLK), f32)],
        flops=4 * rhs * depth * width,
        moved=2 * depth * width,
    )(margin, begun, local_factor, *arrived[1:])
    panels = exchange(fine, "grp")
    spread = call(
        functools.partial(coarse_kernel, own, rows, chunk, sub_count),
        sds((sub_count, own * rows, BLK), f32),
        [VMEM] * (1 + sub_count),
        [pltpu.VMEM((rows * (coarse_width // BLK), BLK), f32), pltpu.VMEM((rows, coarse_depth), f32)],
        flops=4 * rows * coarse_depth * coarse_width,
        moved=2 * coarse_depth * coarse_width,
    )(coarse_factor, *arrived)
    merged = call(
        functools.partial(merge_kernel, own, rows, grp_count),
        [sds((own * rows, BLK), f32)] * sub_count,
        [SMEM] + [VMEM] * (1 + grp_count),
        [pltpu.VMEM((rows * blocks, BLK), f32), pltpu.VMEM((sub_count, own * rows, BLK), f32)],
    )(margin, spread, *panels)
    back = exchange(merged, "sub")
    return call(
        functools.partial(last_kernel, own, rows),
        sds((rows, own_width), f32),
        [VMEM] * sub_count,
        [pltpu.VMEM((own * rows, BLK), f32)],
    )(*back)


def solution(mesh):
    placed = (P(None, "sub"), P(), P("sub"), P("sub", "grp", None), P("sub", None))
    return jax.shard_map(
        on_device, mesh=mesh, in_specs=placed, out_specs=P("grp", "sub"), check_vma=False
    )
```

```python
import functools

import jax
import jax.numpy as jnp
from jax import lax
from jax.experimental import pallas as pl
from jax.experimental.pallas import tpu as pltpu
from jax.sharding import PartitionSpec as P

BLK = 128
MIB = 1024 * 1024
VMEM = pl.BlockSpec(memory_space=pltpu.VMEM)
SMEM = pl.BlockSpec(memory_space=pltpu.SMEM)
HBM = pl.BlockSpec(memory_space=pltpu.HBM)
NT = (((1,), (1,)), ((), ()))
TN = (((0,), (0,)), ((), ()))


def call(kernel, out, specs, scratch=(), limit=12 * MIB, flops=0, moved=0, **options):
    return pl.pallas_call(
        kernel,
        out_shape=out,
        in_specs=specs,
        out_specs=jax.tree.map(lambda _: VMEM, out),
        scratch_shapes=scratch,
        compiler_params=pltpu.CompilerParams(vmem_limit_bytes=limit),
        cost_estimate=pl.CostEstimate(flops=flops, bytes_accessed=moved, transcendentals=0),
        **options,
    )


def mm(left, right, dims=(((1,), (0,)), ((), ()))):
    return lax.dot_general(left, right, dims, preferred_element_type=jnp.float32)


def split3(value):
    high = value.astype(jnp.bfloat16)
    rest = value - high.astype(jnp.float32)
    middle = rest.astype(jnp.bfloat16)
    low = (rest - middle.astype(jnp.float32)).astype(jnp.bfloat16)
    return [high, middle, low]


def pack_kernel(own, rows, pad, margin_hbm, aggregate_hbm, residual_hbm, *refs):
    *outs, block_rows, margin, aggregate, residual, sems = refs
    pairs = ((residual_hbm, residual), (margin_hbm, margin), (aggregate_hbm, aggregate))
    copies = [pltpu.make_async_copy(a, b, sems.at[i]) for i, (a, b) in enumerate(pairs)]
    for copy in copies:
        copy.start()
    for copy in copies:
        copy.wait()
    halo = margin.shape[1]
    rhs = residual.shape[0]
    me = lax.axis_index("sub")
    first = lax.axis_index("grp") * rows
    for b in range(own):
        block_rows[pl.ds(b, rhs, stride=own), :] = residual[:, b * BLK : (b + 1) * BLK]
    mine = block_rows[pl.ds(pl.multiple_of(first * own, 8), rows * own), :]
    names = aggregate[...].astype(jnp.float32)
    at = own * rows
    for d, out in enumerate(outs):
        out[:at, :] = mine
        out[at : at + pad, :] = jnp.zeros((pad, BLK), jnp.float32)
        out[at : at + 1, :own] = names
        if d == 0:
            continue
        target = me ^ d
        for k in range(halo):
            slot = jnp.clip(margin[target, k] - me * own, 0, own - 1)
            out[at + pad + k * rhs : at + pad + (k + 1) * rhs, :] = residual[
                :, pl.ds(pl.multiple_of(slot * BLK, BLK), BLK)
            ]


def panel_copies(source, target, chunk, sems, first=0):
    copies = []
    for n in range(target.shape[0] // chunk):
        span = pl.ds(first + n * chunk, chunk)
        copies.append(
            pltpu.make_async_copy(source.at[span], target.at[pl.ds(n * chunk, chunk)], sems.at[n])
        )
    return copies


def load_kernel(chunk, residual_hbm, fine_hbm, inner, fine, residual, sem, sems):
    own_width = residual.shape[1]
    first = pltpu.make_async_copy(residual_hbm, residual, sem)
    first.start()
    copies = panel_copies(fine_hbm.at[0], fine.at[0], chunk, sems)
    for copy in copies:
        copy.start()
    first.wait()
    local = residual[...].astype(jnp.bfloat16)
    for n, copy in enumerate(copies):
        copy.wait()
        span = slice(n * chunk, (n + 1) * chunk)
        inner[:, span] = mm(local, fine[0, span, :own_width], NT)


def fine_kernel(own, rows, start, chunk, sources, margin, begun, factor, coarse_hbm, *refs):
    arrived = (None, *refs[: sources - 1])
    *outs, coarse, inner, table, sems = refs[sources - 1 :]
    copies = panel_copies(coarse_hbm, coarse, chunk, sems)
    for copy in copies:
        copy.start()
    rhs = begun.shape[0]
    halo = margin.shape[1]
    depth, width = factor.shape[1:]
    blocks = width // BLK
    me = lax.axis_index("sub")
    group = lax.axis_index("grp")
    tiles = []
    for k in range(halo):
        away = me ^ (margin[me, k] // own)
        span = slice(start + k * rhs, start + (k + 1) * rhs)
        tile = arrived[1][span, :]
        for d in range(2, sources):
            tile = jnp.where(away == d, arrived[d][span, :], tile)
        tiles.append(tile.astype(jnp.bfloat16))
    local = jnp.concatenate(tiles, axis=1)
    for n in range(depth // chunk):
        span = slice(n * chunk, (n + 1) * chunk)
        inner[:, span] = begun[:, span] + mm(local, factor[0, span, own * BLK :], NT)
    mid = inner[...].astype(jnp.bfloat16)
    for n in range(width // chunk):
        part = mm(mid, factor[0, :, n * chunk : (n + 1) * chunk])
        for i in range(chunk // BLK):
            b = n * (chunk // BLK) + i
            table[pl.ds(b, rhs, stride=blocks), :] = part[:, i * BLK : (i + 1) * BLK]
    size = rows * blocks
    for d, out in enumerate(outs):
        out[...] = table[pl.ds(pl.multiple_of((group ^ d) * size, 8), size), :]
    for copy in copies:
        copy.wait()


def coarse_kernel(own, rows, chunk, sources, upper, factor_hbm, *refs):
    arrived = refs[:sources]
    out, table, total, lower, sems = refs[sources:]
    done = upper.shape[0]
    depth, width = factor_hbm.shape
    copies = panel_copies(factor_hbm, lower, chunk, sems, done)
    for copy in copies:
        copy.start()
    coarse = width // BLK
    names = [part[own * rows : own * rows + 1, :] for part in arrived]
    names = jnp.concatenate(names, axis=0).T
    catalog = lax.broadcasted_iota(jnp.int32, (own, coarse), 1).astype(jnp.float32)
    member = jnp.concatenate(
        [(names[:own, s : s + 1] == catalog).astype(jnp.float32) for s in range(sources)], axis=0
    ).astype(jnp.bfloat16)
    whole = jnp.concatenate(
        [
            jnp.concatenate([part[r * own : (r + 1) * own, :] for part in arrived], axis=0)
            for r in range(rows)
        ],
        axis=1,
    )
    ones = jnp.ones((own * sources, BLK), jnp.bfloat16)
    span = rows * BLK
    found = mm(member, jnp.concatenate(split3(whole) + [ones], axis=1), TN)
    sums = found[:, :span] + found[:, span : 2 * span] + found[:, 2 * span : 3 * span]
    counts = jnp.maximum(found[:, 3 * span :], 1.0)
    for r in range(rows):
        table[r * coarse : (r + 1) * coarse, :] = sums[:, r * BLK : (r + 1) * BLK] / counts
    right = jnp.concatenate(
        [table[pl.ds(j, rows, stride=coarse), :] for j in range(coarse)], axis=1
    ).astype(jnp.bfloat16)
    panels = [upper.at[pl.ds(n * chunk, chunk)] for n in range(done // chunk)]
    panels += [lower.at[pl.ds(n * chunk, chunk)] for n in range((depth - done) // chunk)]
    waits = [None] * (done // chunk) + copies
    step = 4 * chunk
    for p, (panel, copy) in enumerate(zip(panels, waits)):
        if copy is not None:
            copy.wait()
        mid = mm(right, panel[...], NT).astype(jnp.bfloat16)
        for n in range(width // step):
            where = slice(n * step, (n + 1) * step)
            part = mm(mid, panel[:, where])
            total[:, where] = part if p == 0 else total[:, where] + part
    for j in range(coarse):
        table[pl.ds(j, rows, stride=coarse), :] = total[:, j * BLK : (j + 1) * BLK]
    solved = jnp.concatenate([table[r * coarse : (r + 1) * coarse, :] for r in range(rows)], axis=1)
    spread = mm(member, jnp.concatenate(split3(solved), axis=1))
    spread = spread[:, :span] + spread[:, span : 2 * span] + spread[:, 2 * span :]
    for s in range(sources):
        for r in range(rows):
            out[s, r * own : (r + 1) * own, :] = spread[
                s * own : (s + 1) * own, r * BLK : (r + 1) * BLK
            ]


def merge_kernel(own, rows, groups, margin, spread, *refs):
    arrived = refs[:groups]
    out, total, field = refs[groups:]
    halo = margin.shape[1]
    blocks = own + halo
    me = lax.axis_index("sub")
    summed = arrived[0][...]
    for part in arrived[1:]:
        summed = summed + part[...]
    total[...] = summed
    field[...] = spread[...]
    for r in range(rows):
        span = slice(r * own, (r + 1) * own)
        field[0, span, :] = field[0, span, :] + total[r * blocks : r * blocks + own, :]
    for k in range(halo):
        block = margin[me, k]
        owner = block // own
        where = pl.ds(block - owner * own, rows, stride=own)
        away = me ^ owner
        field[away, where, :] = field[away, where, :] + total[pl.ds(own + k, rows, stride=blocks), :]
    for d in range(out.shape[0]):
        out[me ^ d] = field[d]


def last_kernel(own, rows, arrived, out, total):
    summed = arrived[0]
    for s in range(1, arrived.shape[0]):
        summed = summed + arrived[s]
    total[...] = summed
    for b in range(own):
        out[:, b * BLK : (b + 1) * BLK] = total[pl.ds(b, rows, stride=own), :]


def exchange(parts, axis):
    count = lax.axis_size(axis)
    return [parts[0]] + [
        lax.ppermute(parts[d], axis, [(i, i ^ d) for i in range(count)]) for d in range(1, count)
    ]


def on_device(residual, margin, aggregate, local_factor, coarse_factor):
    sub_count = lax.axis_size("sub")
    grp_count = lax.axis_size("grp")
    rhs, own_width = residual.shape
    own = own_width // BLK
    rows = rhs // grp_count
    halo = margin.shape[1]
    pad = 8
    start = own * rows + pad
    f32 = jnp.float32
    sds = jax.ShapeDtypeStruct
    _, depth, width = local_factor.shape
    coarse_depth, coarse_width = coarse_factor.shape
    blocks = width // BLK

    in_hbm = functools.partial(pltpu.with_memory_space_constraint, memory_space=pltpu.HBM)
    outgoing = call(
        functools.partial(pack_kernel, own, rows, pad),
        [sds((start, BLK), f32)] + [sds((start + halo * rhs, BLK), f32)] * (sub_count - 1),
        [HBM, HBM, HBM],
        [
            pltpu.VMEM((own * rhs, BLK), f32),
            pltpu.SMEM(margin.shape, jnp.int32),
            pltpu.VMEM((1, own), jnp.int32),
            pltpu.VMEM(residual.shape, f32),
            pltpu.SemaphoreType.DMA((3,)),
        ],
    )(in_hbm(margin), in_hbm(aggregate.reshape(1, own)), in_hbm(residual))
    arrived = exchange(outgoing, "sub")
    chunk = 256
    begun, local_factor = call(
        functools.partial(load_kernel, chunk),
        (sds((rhs, depth), f32), sds(local_factor.shape, local_factor.dtype)),
        [HBM, HBM],
        [
            pltpu.VMEM(residual.shape, f32),
            pltpu.SemaphoreType.DMA,
            pltpu.SemaphoreType.DMA((depth // chunk,)),
        ],
        flops=2 * rhs * depth * own_width,
        moved=2 * depth * width,
    )(in_hbm(residual), in_hbm(local_factor))
    coarse_factor = in_hbm(coarse_factor)
    panel = min(chunk, coarse_depth // 2)
    upper = coarse_depth // 2
    *fine, coarse_upper = call(
        functools.partial(fine_kernel, own, rows, start, panel, sub_count),
        [sds((rows * blocks, BLK), f32)] * grp_count
        + [sds((upper, coarse_width), coarse_factor.dtype)],
        [SMEM, VMEM, VMEM, HBM] + [VMEM] * (sub_count - 1),
        [
            pltpu.VMEM((rhs, depth), f32),
            pltpu.VMEM((rhs * blocks, BLK), f32),
            pltpu.SemaphoreType.DMA((upper // panel,)),
        ],
        flops=4 * rhs * depth * width,
        moved=2 * depth * width + 2 * upper * coarse_width,
    )(margin, begun, local_factor, coarse_factor, *arrived[1:])
    panels = exchange(fine, "grp")
    lower = coarse_depth - upper
    spread = call(
        functools.partial(coarse_kernel, own, rows, panel, sub_count),
        sds((sub_count, own * rows, BLK), f32),
        [VMEM, HBM] + [VMEM] * sub_count,
        [
            pltpu.VMEM((rows * (coarse_width // BLK), BLK), f32),
            pltpu.VMEM((rows, coarse_width), f32),
            pltpu.VMEM((lower, coarse_width), coarse_factor.dtype),
            pltpu.SemaphoreType.DMA((lower // panel,)),
        ],
        flops=4 * rows * coarse_depth * coarse_width,
        moved=2 * coarse_depth * coarse_width,
        limit=24 * MIB,
    )(coarse_upper, coarse_factor, *arrived)
    merged = call(
        functools.partial(merge_kernel, own, rows, grp_count),
        sds((sub_count, own * rows, BLK), f32),
        [SMEM] + [VMEM] * (1 + grp_count),
        [pltpu.VMEM((rows * blocks, BLK), f32), pltpu.VMEM((sub_count, own * rows, BLK), f32)],
    )(margin, spread, *panels)
    back = lax.all_to_all(merged, "sub", split_axis=0, concat_axis=0, tiled=True)
    return call(
        functools.partial(last_kernel, own, rows),
        sds((rows, own_width), f32),
        [VMEM],
        [pltpu.VMEM((own * rows, BLK), f32)],
    )(back)


def solution(mesh):
    placed = (P(None, "sub"), P(), P("sub"), P("sub", "grp", None), P("sub", None))
    return jax.shard_map(
        on_device, mesh=mesh, in_specs=placed, out_specs=P("grp", "sub"), check_vma=False
    )
```

```python
import functools

import jax
import jax.numpy as jnp
from jax import lax
from jax.experimental import pallas as pl
from jax.experimental.pallas import tpu as pltpu
from jax.sharding import PartitionSpec as P

BLK = 128
MIB = 1024 * 1024
VMEM = pl.BlockSpec(memory_space=pltpu.VMEM)
SMEM = pl.BlockSpec(memory_space=pltpu.SMEM)
HBM = pl.BlockSpec(memory_space=pltpu.HBM)
NT = (((1,), (1,)), ((), ()))
TN = (((0,), (0,)), ((), ()))


def call(kernel, out, specs, scratch=(), limit=12 * MIB, flops=0, moved=0, **options):
    return pl.pallas_call(
        kernel,
        out_shape=out,
        in_specs=specs,
        out_specs=jax.tree.map(lambda _: VMEM, out),
        scratch_shapes=scratch,
        compiler_params=pltpu.CompilerParams(vmem_limit_bytes=limit),
        cost_estimate=pl.CostEstimate(flops=flops, bytes_accessed=moved, transcendentals=0),
        **options,
    )


def mm(left, right, dims=(((1,), (0,)), ((), ()))):
    return lax.dot_general(left, right, dims, preferred_element_type=jnp.float32)


def split3(value):
    high = value.astype(jnp.bfloat16)
    rest = value - high.astype(jnp.float32)
    middle = rest.astype(jnp.bfloat16)
    low = (rest - middle.astype(jnp.float32)).astype(jnp.bfloat16)
    return [high, middle, low]


def pack_kernel(own, rows, pad, margin_hbm, aggregate_hbm, residual_hbm, *refs):
    *outs, block_rows, margin, aggregate, residual, sems = refs
    pairs = ((residual_hbm, residual), (margin_hbm, margin), (aggregate_hbm, aggregate))
    copies = [pltpu.make_async_copy(a, b, sems.at[i]) for i, (a, b) in enumerate(pairs)]
    for copy in copies:
        copy.start()
    for copy in copies:
        copy.wait()
    halo = margin.shape[1]
    rhs = residual.shape[0]
    me = lax.axis_index("sub")
    first = lax.axis_index("grp") * rows
    for b in range(own):
        block_rows[pl.ds(b, rhs, stride=own), :] = residual[:, b * BLK : (b + 1) * BLK]
    mine = block_rows[pl.ds(pl.multiple_of(first * own, 8), rows * own), :]
    names = aggregate[...].astype(jnp.float32)
    at = own * rows
    for d, out in enumerate(outs):
        out[:at, :] = mine
        out[at : at + pad, :] = jnp.zeros((pad, BLK), jnp.float32)
        out[at : at + 1, :own] = names
        if d == 0:
            continue
        target = me ^ d
        for k in range(halo):
            slot = jnp.clip(margin[target, k] - me * own, 0, own - 1)
            out[at + pad + k * rhs : at + pad + (k + 1) * rhs, :] = residual[
                :, pl.ds(pl.multiple_of(slot * BLK, BLK), BLK)
            ]


def panel_copies(source, target, chunk, sems, first=0):
    copies = []
    for n in range(target.shape[0] // chunk):
        span = pl.ds(first + n * chunk, chunk)
        copies.append(
            pltpu.make_async_copy(source.at[span], target.at[pl.ds(n * chunk, chunk)], sems.at[n])
        )
    for copy in copies:
        copy.start()
    return copies


def first_product(factor, right, tile, copies=()):
    depth = factor.shape[0]
    each = len(copies) * tile // depth
    parts = []
    for n in range(depth // tile):
        for copy in copies[n * each : (n + 1) * each]:
            copy.wait()
        parts.append(mm(factor[n * tile : (n + 1) * tile, :], right, NT).T)
    return jnp.concatenate(parts, axis=1)


def load_kernel(chunk, tile, residual_hbm, fine_hbm, inner, fine, residual, sem, sems):
    own_width = residual.shape[1]
    first = pltpu.make_async_copy(residual_hbm, residual, sem)
    first.start()
    copies = panel_copies(fine_hbm.at[0], fine.at[0], chunk, sems)
    first.wait()
    local = residual[...].astype(jnp.bfloat16)
    inner[...] = first_product(fine.at[0, :, pl.ds(0, own_width)], local, tile, copies)


def fine_kernel(own, rows, start, chunk, tile, sources, margin, begun, factor, coarse_hbm, *refs):
    arrived = (None, *refs[: sources - 1])
    *outs, coarse, table, sems = refs[sources - 1 :]
    copies = panel_copies(coarse_hbm, coarse, chunk, sems)
    rhs = begun.shape[0]
    halo = margin.shape[1]
    depth, width = factor.shape[1:]
    blocks = width // BLK
    me = lax.axis_index("sub")
    group = lax.axis_index("grp")
    tiles = []
    for k in range(halo):
        away = me ^ (margin[me, k] // own)
        span = slice(start + k * rhs, start + (k + 1) * rhs)
        part = arrived[1][span, :]
        for d in range(2, sources):
            part = jnp.where(away == d, arrived[d][span, :], part)
        tiles.append(part.astype(jnp.bfloat16))
    local = jnp.concatenate(tiles, axis=1)
    far = factor.at[0, :, pl.ds(own * BLK, halo * BLK)]
    mid = (begun[...] + first_product(far, local, tile)).astype(jnp.bfloat16)
    for n in range(width // 256):
        part = mm(mid, factor[0, :, n * 256 : (n + 1) * 256])
        for i in range(256 // BLK):
            b = n * (256 // BLK) + i
            table[pl.ds(b, rhs, stride=blocks), :] = part[:, i * BLK : (i + 1) * BLK]
    size = rows * blocks
    for d, out in enumerate(outs):
        out[...] = table[pl.ds(pl.multiple_of((group ^ d) * size, 8), size), :]
    for copy in copies:
        copy.wait()


def coarse_kernel(own, rows, chunk, tile, sources, upper, factor_hbm, *refs):
    arrived = refs[:sources]
    out, table, lower, sems = refs[sources:]
    done = upper.shape[0]
    width = upper.shape[1]
    copies = panel_copies(factor_hbm, lower, chunk, sems, done)
    coarse = width // BLK
    names = [part[own * rows : own * rows + 1, :] for part in arrived]
    names = jnp.concatenate(names, axis=0).T
    catalog = lax.broadcasted_iota(jnp.int32, (own, coarse), 1).astype(jnp.float32)
    member = jnp.concatenate(
        [(names[:own, s : s + 1] == catalog).astype(jnp.float32) for s in range(sources)], axis=0
    ).astype(jnp.bfloat16)
    whole = jnp.concatenate(
        [
            jnp.concatenate([part[r * own : (r + 1) * own, :] for part in arrived], axis=0)
            for r in range(rows)
        ],
        axis=1,
    )
    ones = jnp.ones((own * sources, BLK), jnp.bfloat16)
    span = rows * BLK
    found = mm(member, jnp.concatenate(split3(whole) + [ones], axis=1), TN)
    sums = found[:, :span] + found[:, span : 2 * span] + found[:, 2 * span : 3 * span]
    counts = jnp.maximum(found[:, 3 * span :], 1.0)
    for r in range(rows):
        table[r * coarse : (r + 1) * coarse, :] = sums[:, r * BLK : (r + 1) * BLK] / counts
    right = jnp.concatenate(
        [table[pl.ds(j, rows, stride=coarse), :] for j in range(coarse)], axis=1
    ).astype(jnp.bfloat16)
    high = first_product(upper, right, min(tile, done)).astype(jnp.bfloat16)
    low = first_product(lower, right, min(tile, done), copies).astype(jnp.bfloat16)
    for n in range(width // 256):
        where = slice(n * 256, (n + 1) * 256)
        part = mm(high, upper[:, where]) + mm(low, lower[:, where])
        for i in range(256 // BLK):
            j = n * (256 // BLK) + i
            table[pl.ds(j, rows, stride=coarse), :] = part[:, i * BLK : (i + 1) * BLK]
    solved = jnp.concatenate([table[r * coarse : (r + 1) * coarse, :] for r in range(rows)], axis=1)
    spread = mm(member, jnp.concatenate(split3(solved), axis=1))
    spread = spread[:, :span] + spread[:, span : 2 * span] + spread[:, 2 * span :]
    for s in range(sources):
        for r in range(rows):
            out[s, r * own : (r + 1) * own, :] = spread[
                s * own : (s + 1) * own, r * BLK : (r + 1) * BLK
            ]


def merge_kernel(own, rows, groups, margin, spread, *refs):
    arrived = refs[:groups]
    out, total, field = refs[groups:]
    halo = margin.shape[1]
    blocks = own + halo
    me = lax.axis_index("sub")
    summed = arrived[0][...]
    for part in arrived[1:]:
        summed = summed + part[...]
    total[...] = summed
    field[...] = spread[...]
    for r in range(rows):
        span = slice(r * own, (r + 1) * own)
        field[0, span, :] = field[0, span, :] + total[r * blocks : r * blocks + own, :]
    for k in range(halo):
        block = margin[me, k]
        owner = block // own
        where = pl.ds(block - owner * own, rows, stride=own)
        away = me ^ owner
        field[away, where, :] = field[away, where, :] + total[pl.ds(own + k, rows, stride=blocks), :]
    for d in range(out.shape[0]):
        out[me ^ d] = field[d]


def last_kernel(own, rows, arrived, out, total):
    summed = arrived[0]
    for s in range(1, arrived.shape[0]):
        summed = summed + arrived[s]
    total[...] = summed
    for b in range(own):
        out[:, b * BLK : (b + 1) * BLK] = total[pl.ds(b, rows, stride=own), :]


def exchange(parts, axis):
    count = lax.axis_size(axis)
    return [parts[0]] + [
        lax.ppermute(parts[d], axis, [(i, i ^ d) for i in range(count)]) for d in range(1, count)
    ]


def on_device(residual, margin, aggregate, local_factor, coarse_factor):
    sub_count = lax.axis_size("sub")
    grp_count = lax.axis_size("grp")
    rhs, own_width = residual.shape
    own = own_width // BLK
    rows = rhs // grp_count
    halo = margin.shape[1]
    pad = 8
    start = own * rows + pad
    f32 = jnp.float32
    sds = jax.ShapeDtypeStruct
    _, depth, width = local_factor.shape
    coarse_depth, coarse_width = coarse_factor.shape
    blocks = width // BLK

    in_hbm = functools.partial(pltpu.with_memory_space_constraint, memory_space=pltpu.HBM)
    outgoing = call(
        functools.partial(pack_kernel, own, rows, pad),
        [sds((start, BLK), f32)] + [sds((start + halo * rhs, BLK), f32)] * (sub_count - 1),
        [HBM, HBM, HBM],
        [
            pltpu.VMEM((own * rhs, BLK), f32),
            pltpu.SMEM(margin.shape, jnp.int32),
            pltpu.VMEM((1, own), jnp.int32),
            pltpu.VMEM(residual.shape, f32),
            pltpu.SemaphoreType.DMA((3,)),
        ],
    )(in_hbm(margin), in_hbm(aggregate.reshape(1, own)), in_hbm(residual))
    arrived = exchange(outgoing, "sub")
    chunk, tile = 64, 256
    begun, local_factor = call(
        functools.partial(load_kernel, chunk, tile),
        (sds((rhs, depth), f32), sds(local_factor.shape, local_factor.dtype)),
        [HBM, HBM],
        [
            pltpu.VMEM(residual.shape, f32),
            pltpu.SemaphoreType.DMA,
            pltpu.SemaphoreType.DMA((depth // chunk,)),
        ],
        flops=2 * rhs * depth * own_width,
        moved=2 * depth * width,
    )(in_hbm(residual), in_hbm(local_factor))
    coarse_factor = in_hbm(coarse_factor)
    upper = coarse_depth // 4
    *fine, coarse_upper = call(
        functools.partial(fine_kernel, own, rows, start, chunk, tile, sub_count),
        [sds((rows * blocks, BLK), f32)] * grp_count
        + [sds((upper, coarse_width), coarse_factor.dtype)],
        [SMEM, VMEM, VMEM, HBM] + [VMEM] * (sub_count - 1),
        [pltpu.VMEM((rhs * blocks, BLK), f32), pltpu.SemaphoreType.DMA((upper // chunk,))],
        flops=4 * rhs * depth * width,
        moved=2 * depth * width + 2 * upper * coarse_width,
    )(margin, begun, local_factor, coarse_factor, *arrived[1:])
    panels = exchange(fine, "grp")
    lower = coarse_depth - upper
    spread = call(
        functools.partial(coarse_kernel, own, rows, chunk, tile, sub_count),
        sds((sub_count, own * rows, BLK), f32),
        [VMEM, HBM] + [VMEM] * sub_count,
        [
            pltpu.VMEM((rows * (coarse_width // BLK), BLK), f32),
            pltpu.VMEM((lower, coarse_width), coarse_factor.dtype),
            pltpu.SemaphoreType.DMA((lower // chunk,)),
        ],
        flops=4 * rows * coarse_depth * coarse_width,
        moved=2 * coarse_depth * coarse_width,
        limit=24 * MIB,
    )(coarse_upper, coarse_factor, *arrived)
    merged = call(
        functools.partial(merge_kernel, own, rows, grp_count),
        sds((sub_count, own * rows, BLK), f32),
        [SMEM] + [VMEM] * (1 + grp_count),
        [pltpu.VMEM((rows * blocks, BLK), f32), pltpu.VMEM((sub_count, own * rows, BLK), f32)],
    )(margin, spread, *panels)
    back = lax.all_to_all(merged, "sub", split_axis=0, concat_axis=0, tiled=True)
    return call(
        functools.partial(last_kernel, own, rows),
        sds((rows, own_width), f32),
        [VMEM],
        [pltpu.VMEM((own * rows, BLK), f32)],
    )(back)


def solution(mesh):
    placed = (P(None, "sub"), P(), P("sub"), P("sub", "grp", None), P("sub", None))
    return jax.shard_map(
        on_device, mesh=mesh, in_specs=placed, out_specs=P("grp", "sub"), check_vma=False
    )
```

```python
import functools

import jax
import jax.numpy as jnp
from jax import lax
from jax.experimental import pallas as pl
from jax.experimental.pallas import tpu as pltpu
from jax.sharding import PartitionSpec as P

BLK = 128
MIB = 1024 * 1024
VMEM = pl.BlockSpec(memory_space=pltpu.VMEM)
SMEM = pl.BlockSpec(memory_space=pltpu.SMEM)
HBM = pl.BlockSpec(memory_space=pltpu.HBM)
NT = (((1,), (1,)), ((), ()))
TN = (((0,), (0,)), ((), ()))


def call(kernel, out, specs, scratch=(), limit=12 * MIB, flops=0, moved=0, **options):
    return pl.pallas_call(
        kernel,
        out_shape=out,
        in_specs=specs,
        out_specs=jax.tree.map(lambda _: VMEM, out),
        scratch_shapes=scratch,
        compiler_params=pltpu.CompilerParams(vmem_limit_bytes=limit),
        cost_estimate=pl.CostEstimate(flops=flops, bytes_accessed=moved, transcendentals=0),
        **options,
    )


def mm(left, right, dims=(((1,), (0,)), ((), ()))):
    return lax.dot_general(left, right, dims, preferred_element_type=jnp.float32)


def split3(value):
    high = value.astype(jnp.bfloat16)
    rest = value - high.astype(jnp.float32)
    middle = rest.astype(jnp.bfloat16)
    low = (rest - middle.astype(jnp.float32)).astype(jnp.bfloat16)
    return [high, middle, low]


def pack_kernel(own, rows, pad, margin_hbm, aggregate_hbm, residual_hbm, near_names, near, *refs):
    *outs, block_rows, margin, aggregate, residual, sems = refs
    pairs = ((residual_hbm, residual), (margin_hbm, margin), (aggregate_hbm, aggregate))
    copies = [pltpu.make_async_copy(a, b, sems.at[i]) for i, (a, b) in enumerate(pairs)]
    for copy in copies:
        copy.start()
    for copy in copies:
        copy.wait()
    halo = margin.shape[1]
    rhs = residual.shape[0]
    me = lax.axis_index("sub")
    first = lax.axis_index("grp") * rows
    size = own * rows
    mine = []
    for i, part in enumerate((residual, near)):
        for b in range(own):
            block_rows[i, pl.ds(b, rhs, stride=own), :] = part[:, b * BLK : (b + 1) * BLK]
        mine.append(block_rows[i, pl.ds(pl.multiple_of(first * own, 8), size), :])
    names = [aggregate[...].astype(jnp.float32), near_names[...].astype(jnp.float32)]
    at = 2 * size
    for e, out in enumerate(outs):
        out[at : at + pad, :] = jnp.zeros((pad, BLK), jnp.float32)
        for i in range(2):
            out[i * size : (i + 1) * size, :] = mine[i]
            out[at + i : at + i + 1, :own] = names[i]
        if e == 0:
            continue
        target = me ^ (2 * e)
        for k in range(halo):
            block = margin[target, k]
            owner = block // own
            where = pl.ds(pl.multiple_of((block - owner * own) * BLK, BLK), BLK)
            out[at + pad + k * rhs : at + pad + (k + 1) * rhs, :] = jnp.where(
                owner == me, residual[:, where], near[:, where]
            )


def panel_copies(source, target, chunk, sems, first=0):
    copies = []
    for n in range(target.shape[0] // chunk):
        span = pl.ds(first + n * chunk, chunk)
        copies.append(
            pltpu.make_async_copy(source.at[span], target.at[pl.ds(n * chunk, chunk)], sems.at[n])
        )
    return copies


def start(copies):
    for copy in copies:
        copy.start()


def first_product(factor, right, tile, copies=(), ahead=0):
    depth = factor.shape[0]
    each = len(copies) * tile // depth
    parts = []
    for n in range(depth // tile):
        for i in range(n * each, (n + 1) * each):
            copies[i].wait()
            if i + ahead < len(copies):
                copies[i + ahead].start()
        parts.append(mm(right, factor[n * tile : (n + 1) * tile, :], NT))
    return jnp.concatenate(parts, axis=1)


def load_kernel(chunk, tile, ahead, residual_hbm, fine_hbm, after, inner, fine, residual, sem, sems):
    own_width = residual.shape[1]
    first = pltpu.make_async_copy(residual_hbm, residual, sem)
    first.start()
    copies = panel_copies(fine_hbm.at[0], fine.at[0], chunk, sems)
    start(copies[:ahead])
    first.wait()
    local = residual[...].astype(jnp.bfloat16)
    inner[...] = first_product(fine.at[0, :, pl.ds(0, own_width)], local, tile, copies, ahead)


def fine_kernel(own, rows, begin, chunk, tile, pairs, margin, begun, factor, coarse_hbm, near, *refs):
    arrived = (None, *refs[: pairs - 1])
    *outs, coarse, table, sems = refs[pairs - 1 :]
    copies = panel_copies(coarse_hbm, coarse, chunk, sems)
    start(copies)
    rhs = begun.shape[0]
    halo = margin.shape[1]
    depth, width = factor.shape[1:]
    blocks = width // BLK
    me = lax.axis_index("sub")
    group = lax.axis_index("grp")
    tiles = []
    for k in range(halo):
        block = margin[me, k]
        owner = block // own
        away = (me ^ owner) // 2
        span = slice(begin + k * rhs, begin + (k + 1) * rhs)
        part = near[:, pl.ds(pl.multiple_of((block - owner * own) * BLK, BLK), BLK)]
        for e in range(1, pairs):
            part = jnp.where(away == e, arrived[e][span, :], part)
        tiles.append(part.astype(jnp.bfloat16))
    local = jnp.concatenate(tiles, axis=1)
    far = factor.at[0, :, pl.ds(own * BLK, halo * BLK)]
    mid = (begun[...] + first_product(far, local, tile)).astype(jnp.bfloat16)
    for n in range(width // 256):
        part = mm(mid, factor[0, :, n * 256 : (n + 1) * 256])
        for i in range(256 // BLK):
            b = n * (256 // BLK) + i
            table[pl.ds(b, rhs, stride=blocks), :] = part[:, i * BLK : (i + 1) * BLK]
    size = rows * blocks
    for d, out in enumerate(outs):
        out[...] = table[pl.ds(pl.multiple_of((group ^ d) * size, 8), size), :]
    for copy in copies:
        copy.wait()


def coarse_kernel(own, rows, chunk, tile, ahead, pairs, upper, factor_hbm, *refs):
    arrived = refs[:pairs]
    out, table, lower, sems = refs[pairs:]
    done = upper.shape[0]
    width = upper.shape[1]
    copies = panel_copies(factor_hbm, lower, chunk, sems, done)
    start(copies[:ahead])
    coarse = width // BLK
    size = own * rows
    sources = 2 * pairs
    parts = [(part, i) for part in arrived for i in range(2)]
    names = jnp.concatenate(
        [part[2 * size + i : 2 * size + i + 1, :] for part, i in parts], axis=0
    ).T
    catalog = lax.broadcasted_iota(jnp.int32, (own, coarse), 1).astype(jnp.float32)
    member = jnp.concatenate(
        [(names[:own, s : s + 1] == catalog).astype(jnp.float32) for s in range(sources)], axis=0
    ).astype(jnp.bfloat16)
    whole = jnp.concatenate(
        [
            jnp.concatenate(
                [part[i * size + r * own : i * size + (r + 1) * own, :] for part, i in parts],
                axis=0,
            )
            for r in range(rows)
        ],
        axis=1,
    )
    ones = jnp.ones((own * sources, BLK), jnp.bfloat16)
    span = rows * BLK
    found = mm(member, jnp.concatenate(split3(whole) + [ones], axis=1), TN)
    sums = found[:, :span] + found[:, span : 2 * span] + found[:, 2 * span : 3 * span]
    counts = jnp.maximum(found[:, 3 * span :], 1.0)
    for r in range(rows):
        table[r * coarse : (r + 1) * coarse, :] = sums[:, r * BLK : (r + 1) * BLK] / counts
    right = jnp.concatenate(
        [table[pl.ds(j, rows, stride=coarse), :] for j in range(coarse)], axis=1
    ).astype(jnp.bfloat16)
    high = first_product(upper, right, tile).astype(jnp.bfloat16)
    low = first_product(lower, right, tile, copies, ahead).astype(jnp.bfloat16)
    for n in range(width // 256):
        where = slice(n * 256, (n + 1) * 256)
        part = mm(high, upper[:, where]) + mm(low, lower[:, where])
        for i in range(256 // BLK):
            j = n * (256 // BLK) + i
            table[pl.ds(j, rows, stride=coarse), :] = part[:, i * BLK : (i + 1) * BLK]
    solved = jnp.concatenate([table[r * coarse : (r + 1) * coarse, :] for r in range(rows)], axis=1)
    spread = mm(member, jnp.concatenate(split3(solved), axis=1))
    spread = spread[:, :span] + spread[:, span : 2 * span] + spread[:, 2 * span :]
    for s in range(sources):
        for r in range(rows):
            out[s, r * own : (r + 1) * own, :] = spread[
                s * own : (s + 1) * own, r * BLK : (r + 1) * BLK
            ]


def merge_kernel(own, rows, groups, margin, spread, *refs):
    arrived = refs[:groups]
    kept, near, total, field = refs[groups:]
    halo = margin.shape[1]
    blocks = own + halo
    me = lax.axis_index("sub")
    summed = arrived[0][...]
    for part in arrived[1:]:
        summed = summed + part[...]
    total[...] = summed
    field[...] = spread[...]
    for r in range(rows):
        span = slice(r * own, (r + 1) * own)
        field[0, span, :] = field[0, span, :] + total[r * blocks : r * blocks + own, :]
    for k in range(halo):
        block = margin[me, k]
        owner = block // own
        where = pl.ds(block - owner * own, rows, stride=own)
        away = me ^ owner
        field[away, where, :] = field[away, where, :] + total[pl.ds(own + k, rows, stride=blocks), :]
    for e in range(kept.shape[0]):
        kept[e] = field[2 * e]
        near[e] = field[2 * e + 1]


def add_kernel(kept, arrived, *outs):
    for e, out in enumerate(outs):
        out[...] = kept[e] + arrived[e]


def last_kernel(own, rows, *refs):
    *arrived, out, total = refs
    summed = arrived[0][...]
    for part in arrived[1:]:
        summed = summed + part[...]
    total[...] = summed
    for b in range(own):
        out[:, b * BLK : (b + 1) * BLK] = total[pl.ds(b, rows, stride=own), :]


def swap(value, axis, distance):
    count = lax.axis_size(axis)
    return lax.ppermute(value, axis, [(i, i ^ distance) for i in range(count)])


def exchange(parts, axis, unit=1):
    return [parts[0]] + [swap(part, axis, d * unit) for d, part in enumerate(parts) if d > 0]


def on_device(residual, margin, aggregate, local_factor, coarse_factor):
    pairs = lax.axis_size("sub") // 2
    grp_count = lax.axis_size("grp")
    rhs, own_width = residual.shape
    own = own_width // BLK
    rows = rhs // grp_count
    halo = margin.shape[1]
    pad = 8
    begin = 2 * own * rows + pad
    f32 = jnp.float32
    sds = jax.ShapeDtypeStruct
    _, depth, width = local_factor.shape
    coarse_depth, coarse_width = coarse_factor.shape
    blocks = width // BLK
    in_hbm = functools.partial(pltpu.with_memory_space_constraint, memory_space=pltpu.HBM)
    aggregate = aggregate.reshape(1, own)
    local_factor = in_hbm(local_factor)
    coarse_factor = in_hbm(coarse_factor)

    near = swap(residual, "sub", 1)
    near_names = swap(aggregate, "sub", 1)
    outgoing = call(
        functools.partial(pack_kernel, own, rows, pad),
        [sds((begin, BLK), f32)] + [sds((begin + halo * rhs, BLK), f32)] * (pairs - 1),
        [HBM, HBM, HBM, VMEM, VMEM],
        [
            pltpu.VMEM((2, own * rhs, BLK), f32),
            pltpu.SMEM(margin.shape, jnp.int32),
            pltpu.VMEM((1, own), jnp.int32),
            pltpu.VMEM(residual.shape, f32),
            pltpu.SemaphoreType.DMA((3,)),
        ],
    )(in_hbm(margin), in_hbm(aggregate), in_hbm(residual), near_names, near)
    arrived = exchange(outgoing, "sub", 2)
    tile = min(256, coarse_depth // 2, depth // 2)
    chunk = tile // 4
    ahead = 2 * tile // chunk
    begun, local_factor = call(
        functools.partial(load_kernel, chunk, tile, ahead),
        (sds((rhs, depth), f32), sds(local_factor.shape, local_factor.dtype)),
        [HBM, HBM, pl.BlockSpec(memory_space=pl.ANY)],
        [
            pltpu.VMEM(residual.shape, f32),
            pltpu.SemaphoreType.DMA,
            pltpu.SemaphoreType.DMA((depth // chunk,)),
        ],
        flops=2 * rhs * depth * own_width,
        moved=2 * depth * width,
    )(in_hbm(residual), local_factor, arrived[0])
    chunk = tile // 8
    ahead = tile // chunk
    upper, lower = tile, coarse_depth - tile
    *fine, coarse_upper = call(
        functools.partial(fine_kernel, own, rows, begin, chunk, tile, pairs),
        [sds((rows * blocks, BLK), f32)] * grp_count
        + [sds((upper, coarse_width), coarse_factor.dtype)],
        [SMEM, VMEM, VMEM, HBM, VMEM] + [VMEM] * (pairs - 1),
        [pltpu.VMEM((rhs * blocks, BLK), f32), pltpu.SemaphoreType.DMA((upper // chunk,))],
        flops=4 * rhs * depth * width,
        moved=2 * depth * width + 2 * upper * coarse_width,
    )(margin, begun, local_factor, coarse_factor, near, *arrived[1:])
    panels = exchange(fine, "grp")
    spread = call(
        functools.partial(coarse_kernel, own, rows, chunk, tile, ahead, pairs),
        sds((2 * pairs, own * rows, BLK), f32),
        [VMEM, HBM] + [VMEM] * pairs,
        [
            pltpu.VMEM((rows * (coarse_width // BLK), BLK), f32),
            pltpu.VMEM((lower, coarse_width), coarse_factor.dtype),
            pltpu.SemaphoreType.DMA((lower // chunk,)),
        ],
        flops=4 * rows * coarse_depth * coarse_width,
        moved=2 * coarse_depth * coarse_width,
        limit=24 * MIB,
    )(coarse_upper, coarse_factor, *arrived)
    field = sds((pairs, own * rows, BLK), f32)
    kept, crossing = call(
        functools.partial(merge_kernel, own, rows, grp_count),
        [field, field],
        [SMEM] + [VMEM] * (1 + grp_count),
        [
            pltpu.VMEM((rows * blocks, BLK), f32),
            pltpu.VMEM((2 * pairs, own * rows, BLK), f32),
        ],
    )(margin, spread, *panels)
    back = call(add_kernel, [sds((own * rows, BLK), f32)] * pairs, [VMEM, VMEM])(
        kept, swap(crossing, "sub", 1)
    )
    return call(
        functools.partial(last_kernel, own, rows),
        sds((rows, own_width), f32),
        [VMEM] * pairs,
        [pltpu.VMEM((own * rows, BLK), f32)],
    )(*exchange(back, "sub", 2))


def solution(mesh):
    placed = (P(None, "sub"), P(), P("sub"), P("sub", "grp", None), P("sub", None))
    return jax.shard_map(
        on_device, mesh=mesh, in_specs=placed, out_specs=P("grp", "sub"), check_vma=False
    )
```

```python
import functools

import jax
import jax.numpy as jnp
from jax import lax
from jax.experimental import pallas as pl
from jax.experimental.pallas import tpu as pltpu
from jax.sharding import PartitionSpec as P

BLK = 128
MIB = 1024 * 1024
VMEM = pl.BlockSpec(memory_space=pltpu.VMEM)
SMEM = pl.BlockSpec(memory_space=pltpu.SMEM)
HBM = pl.BlockSpec(memory_space=pltpu.HBM)
NT = (((1,), (1,)), ((), ()))
TN = (((0,), (0,)), ((), ()))


def call(kernel, out, specs, scratch=(), limit=12 * MIB, flops=0, moved=0, **options):
    return pl.pallas_call(
        kernel,
        out_shape=out,
        in_specs=specs,
        out_specs=jax.tree.map(lambda _: VMEM, out),
        scratch_shapes=scratch,
        compiler_params=pltpu.CompilerParams(vmem_limit_bytes=limit),
        cost_estimate=pl.CostEstimate(flops=flops, bytes_accessed=moved, transcendentals=0),
        **options,
    )


def mm(left, right, dims=(((1,), (0,)), ((), ()))):
    return lax.dot_general(left, right, dims, preferred_element_type=jnp.float32)


def split3(value):
    high = value.astype(jnp.bfloat16)
    rest = value - high.astype(jnp.float32)
    middle = rest.astype(jnp.bfloat16)
    low = (rest - middle.astype(jnp.float32)).astype(jnp.bfloat16)
    return [high, middle, low]


def pack_kernel(own, rows, pad, margin_hbm, aggregate_hbm, residual_hbm, near_names, near, *refs):
    *outs, block_rows, margin, aggregate, residual, sems = refs
    pairs = ((residual_hbm, residual), (margin_hbm, margin), (aggregate_hbm, aggregate))
    copies = [pltpu.make_async_copy(a, b, sems.at[i]) for i, (a, b) in enumerate(pairs)]
    for copy in copies:
        copy.start()
    for copy in copies:
        copy.wait()
    halo = margin.shape[1]
    rhs = residual.shape[0]
    me = lax.axis_index("sub")
    first = lax.axis_index("grp") * rows
    size = own * rows
    mine = []
    for i, part in enumerate((residual, near)):
        for b in range(own):
            block_rows[i, pl.ds(b, rhs, stride=own), :] = part[:, b * BLK : (b + 1) * BLK]
        mine.append(block_rows[i, pl.ds(pl.multiple_of(first * own, 8), size), :])
    names = [aggregate[...].astype(jnp.float32), near_names[...].astype(jnp.float32)]
    at = 2 * size
    for e, out in enumerate(outs):
        out[at : at + pad, :] = jnp.zeros((pad, BLK), jnp.float32)
        for i in range(2):
            out[i * size : (i + 1) * size, :] = mine[i]
            out[at + i : at + i + 1, :own] = names[i]
        if e == 0:
            continue
        target = me ^ (2 * e)
        for k in range(halo):
            block = margin[target, k]
            owner = block // own
            where = pl.ds(pl.multiple_of((block - owner * own) * BLK, BLK), BLK)
            out[at + pad + k * rhs : at + pad + (k + 1) * rhs, :] = jnp.where(
                owner == me, residual[:, where], near[:, where]
            )


def panel_copies(source, target, chunk, sems, first=0):
    copies = []
    for n in range(target.shape[0] // chunk):
        span = pl.ds(first + n * chunk, chunk)
        copies.append(
            pltpu.make_async_copy(source.at[span], target.at[pl.ds(n * chunk, chunk)], sems.at[n])
        )
    return copies


def start(copies):
    for copy in copies:
        copy.start()


def first_product(factor, right, tile):
    parts = [
        mm(right, factor[n * tile : (n + 1) * tile, :], NT) for n in range(factor.shape[0] // tile)
    ]
    return jnp.concatenate(parts, axis=1)


def in_own_block(body):
    pl.when(lax.axis_index("sub") >= 0)(body)


def load_kernel(
    chunk, tile, residual_hbm, fine_hbm, coarse_hbm, after, inner, fine, coarse, residual, sem, sems, more
):
    depth = fine.shape[1]
    own_width = residual.shape[1]
    half = depth // 2
    each = half // chunk
    first = pltpu.make_async_copy(residual_hbm, residual, sem)
    first.start()
    start(panel_copies(fine_hbm.at[0], fine.at[0], chunk, sems))
    late = panel_copies(coarse_hbm, coarse, coarse.shape[0] // 4, more)
    first.wait()

    def step(n, carry):
        for i in range(each):
            span = pl.ds(pl.multiple_of(n * half + i * chunk, chunk), chunk)
            pltpu.make_async_copy(fine_hbm.at[0, span], fine.at[0, span], sems.at[n * each + i]).wait()
        pl.when(n == 0)(lambda: start(late))
        local = residual[...].astype(jnp.bfloat16)
        for i in range(half // tile):
            at = pl.multiple_of(n * half + i * tile, tile)
            rows = fine[0, pl.ds(at, tile), pl.ds(0, own_width)]
            inner[:, pl.ds(at, tile)] = mm(local, rows, NT)
        return carry

    lax.fori_loop(0, 2, step, 0)
    for copy in late:
        copy.wait()


def fine_kernel(own, rows, begin, chunk, tile, pairs, margin, begun, factor, coarse_hbm, near, *refs):
    arrived = (None, *refs[: pairs - 1])
    *outs, coarse, table, sems = refs[pairs - 1 :]
    done = coarse_hbm.shape[0] // 4
    copies = panel_copies(coarse_hbm, coarse, chunk, sems, done)
    start(copies)
    rhs = begun.shape[0]
    halo = margin.shape[1]
    depth, width = factor.shape[1:]
    blocks = width // BLK
    me = lax.axis_index("sub")
    group = lax.axis_index("grp")
    tiles = []
    for k in range(halo):
        block = margin[me, k]
        owner = block // own
        away = (me ^ owner) // 2
        span = slice(begin + k * rhs, begin + (k + 1) * rhs)
        part = near[:, pl.ds(pl.multiple_of((block - owner * own) * BLK, BLK), BLK)]
        for e in range(1, pairs):
            part = jnp.where(away == e, arrived[e][span, :], part)
        tiles.append(part.astype(jnp.bfloat16))
    local = jnp.concatenate(tiles, axis=1)
    far = factor.at[0, :, pl.ds(own * BLK, halo * BLK)]
    mid = (begun[...] + first_product(far, local, tile)).astype(jnp.bfloat16)
    for n in range(width // 256):
        part = mm(mid, factor[0, :, n * 256 : (n + 1) * 256])
        for i in range(256 // BLK):
            b = n * (256 // BLK) + i
            table[pl.ds(b, rhs, stride=blocks), :] = part[:, i * BLK : (i + 1) * BLK]
    size = rows * blocks
    for d, out in enumerate(outs):
        out[...] = table[pl.ds(pl.multiple_of((group ^ d) * size, 8), size), :]

    @in_own_block
    def _():
        for copy in copies:
            copy.wait()


def coarse_kernel(own, rows, chunk, tile, pairs, upper, middle, factor_hbm, *refs):
    arrived = refs[:pairs]
    out, table, lower, begun, field, sems = refs[pairs:]
    done = upper.shape[0] + middle.shape[0]
    width = upper.shape[1]
    copies = panel_copies(factor_hbm, lower, chunk, sems, done)
    start(copies)
    coarse = width // BLK
    size = own * rows
    sources = 2 * pairs
    parts = [(part, i) for part in arrived for i in range(2)]
    names = jnp.concatenate(
        [part[2 * size + i : 2 * size + i + 1, :] for part, i in parts], axis=0
    ).T
    catalog = lax.broadcasted_iota(jnp.int32, (own, coarse), 1).astype(jnp.float32)
    member = jnp.concatenate(
        [(names[:own, s : s + 1] == catalog).astype(jnp.float32) for s in range(sources)], axis=0
    ).astype(jnp.bfloat16)
    whole = jnp.concatenate(
        [
            jnp.concatenate(
                [part[i * size + r * own : i * size + (r + 1) * own, :] for part, i in parts],
                axis=0,
            )
            for r in range(rows)
        ],
        axis=1,
    )
    ones = jnp.ones((own * sources, BLK), jnp.bfloat16)
    span = rows * BLK
    found = mm(member, jnp.concatenate(split3(whole) + [ones], axis=1), TN)
    sums = found[:, :span] + found[:, span : 2 * span] + found[:, 2 * span : 3 * span]
    counts = jnp.maximum(found[:, 3 * span :], 1.0)
    for r in range(rows):
        table[r * coarse : (r + 1) * coarse, :] = sums[:, r * BLK : (r + 1) * BLK] / counts
    right = jnp.concatenate(
        [table[pl.ds(j, rows, stride=coarse), :] for j in range(coarse)], axis=1
    ).astype(jnp.bfloat16)
    field[...] = member.astype(jnp.float32)
    begun[:, : upper.shape[0]] = first_product(upper, right, tile)
    begun[:, upper.shape[0] : done] = first_product(middle, right, tile)

    @in_own_block
    def _():
        for copy in copies:
            copy.wait()
        right = jnp.concatenate(
            [table[pl.ds(j, rows, stride=coarse), :] for j in range(coarse)], axis=1
        ).astype(jnp.bfloat16)
        low = first_product(lower, right, tile).astype(jnp.bfloat16)
        mid = begun[...].astype(jnp.bfloat16)
        high = mid[:, : upper.shape[0]]
        mid = mid[:, upper.shape[0] :]
        for n in range(width // 256):
            where = slice(n * 256, (n + 1) * 256)
            part = mm(high, upper[:, where]) + mm(mid, middle[:, where]) + mm(low, lower[:, where])
            for i in range(256 // BLK):
                j = n * (256 // BLK) + i
                table[pl.ds(j, rows, stride=coarse), :] = part[:, i * BLK : (i + 1) * BLK]
        member = field[...].astype(jnp.bfloat16)
        solved = jnp.concatenate([table[r * coarse : (r + 1) * coarse, :] for r in range(rows)], axis=1)
        spread = mm(member, jnp.concatenate(split3(solved), axis=1))
        spread = spread[:, :span] + spread[:, span : 2 * span] + spread[:, 2 * span :]
        for s in range(sources):
            for r in range(rows):
                out[s, r * own : (r + 1) * own, :] = spread[
                    s * own : (s + 1) * own, r * BLK : (r + 1) * BLK
                ]


def merge_kernel(own, rows, groups, margin, spread, *refs):
    arrived = refs[:groups]
    kept, near, total, field = refs[groups:]
    halo = margin.shape[1]
    blocks = own + halo
    me = lax.axis_index("sub")
    summed = arrived[0][...]
    for part in arrived[1:]:
        summed = summed + part[...]
    total[...] = summed
    field[...] = spread[...]
    for r in range(rows):
        span = slice(r * own, (r + 1) * own)
        field[0, span, :] = field[0, span, :] + total[r * blocks : r * blocks + own, :]
    for k in range(halo):
        block = margin[me, k]
        owner = block // own
        where = pl.ds(block - owner * own, rows, stride=own)
        away = me ^ owner
        field[away, where, :] = field[away, where, :] + total[pl.ds(own + k, rows, stride=blocks), :]
    for e in range(kept.shape[0]):
        kept[e] = field[2 * e]
        near[e] = field[2 * e + 1]


def add_kernel(kept_in, arrived, kept, near):
    for e in range(kept.shape[0]):
        kept[e] = kept_in[2 * e] + arrived[2 * e]
        near[e] = kept_in[2 * e + 1] + arrived[2 * e + 1]


def last_kernel(own, rows, kept, arrived, out, total):
    total[...] = kept[0] + arrived[0]
    for b in range(own):
        out[:, b * BLK : (b + 1) * BLK] = total[pl.ds(b, rows, stride=own), :]


def swap(value, axis, distance):
    count = lax.axis_size(axis)
    return lax.ppermute(value, axis, [(i, i ^ distance) for i in range(count)])


def exchange(parts, axis, unit=1):
    return [parts[0]] + [swap(part, axis, d * unit) for d, part in enumerate(parts) if d > 0]


def on_device(residual, margin, aggregate, local_factor, coarse_factor):
    pairs = lax.axis_size("sub") // 2
    grp_count = lax.axis_size("grp")
    rhs, own_width = residual.shape
    own = own_width // BLK
    rows = rhs // grp_count
    halo = margin.shape[1]
    pad = 8
    begin = 2 * own * rows + pad
    f32 = jnp.float32
    sds = jax.ShapeDtypeStruct
    _, depth, width = local_factor.shape
    coarse_depth, coarse_width = coarse_factor.shape
    blocks = width // BLK
    in_hbm = functools.partial(pltpu.with_memory_space_constraint, memory_space=pltpu.HBM)
    aggregate = aggregate.reshape(1, own)
    local_factor = in_hbm(local_factor)
    coarse_factor = in_hbm(coarse_factor)

    near = swap(residual, "sub", 1)
    near_names = swap(aggregate, "sub", 1)
    outgoing = call(
        functools.partial(pack_kernel, own, rows, pad),
        [sds((begin, BLK), f32)] + [sds((begin + halo * rhs, BLK), f32)] * (pairs - 1),
        [HBM, HBM, HBM, VMEM, VMEM],
        [
            pltpu.VMEM((2, own * rhs, BLK), f32),
            pltpu.SMEM(margin.shape, jnp.int32),
            pltpu.VMEM((1, own), jnp.int32),
            pltpu.VMEM(residual.shape, f32),
            pltpu.SemaphoreType.DMA((3,)),
        ],
    )(in_hbm(margin), in_hbm(aggregate), in_hbm(residual), near_names, near)
    arrived = exchange(outgoing, "sub", 2)
    quarter = coarse_depth // 4
    tile, coarse_tile = min(256, depth // 2), min(256, quarter)
    chunk = depth // 8
    begun, local_factor, coarse_upper = call(
        functools.partial(load_kernel, chunk, tile),
        (
            sds((rhs, depth), f32),
            sds(local_factor.shape, local_factor.dtype),
            sds((quarter, coarse_width), coarse_factor.dtype),
        ),
        [HBM, HBM, HBM, pl.BlockSpec(memory_space=pl.ANY)],
        [
            pltpu.VMEM(residual.shape, f32),
            pltpu.SemaphoreType.DMA,
            pltpu.SemaphoreType.DMA((depth // chunk,)),
            pltpu.SemaphoreType.DMA((4,)),
        ],
        flops=2 * rhs * depth * own_width,
        moved=2 * depth * width + 2 * quarter * coarse_width,
    )(in_hbm(residual), local_factor, coarse_factor, arrived[0])
    chunk = quarter // 4
    *fine, coarse_middle = call(
        functools.partial(fine_kernel, own, rows, begin, chunk, tile, pairs),
        [sds((rows * blocks, BLK), f32)] * grp_count
        + [sds((quarter, coarse_width), coarse_factor.dtype)],
        [SMEM, VMEM, VMEM, HBM, VMEM] + [VMEM] * (pairs - 1),
        [pltpu.VMEM((rhs * blocks, BLK), f32), pltpu.SemaphoreType.DMA((quarter // chunk,))],
        flops=4 * rhs * depth * width,
        moved=2 * depth * width + 2 * quarter * coarse_width,
    )(margin, begun, local_factor, coarse_factor, near, *arrived[1:])
    panels = exchange(fine, "grp")
    lower = coarse_depth - 2 * quarter
    size = own * rows
    spread = call(
        functools.partial(coarse_kernel, own, rows, chunk, coarse_tile, pairs),
        sds((2 * pairs, size, BLK), f32),
        [VMEM, VMEM, HBM] + [VMEM] * pairs,
        [
            pltpu.VMEM((rows * (coarse_width // BLK), BLK), f32),
            pltpu.VMEM((lower, coarse_width), coarse_factor.dtype),
            pltpu.VMEM((rows, 2 * quarter), f32),
            pltpu.VMEM((2 * pairs * own, coarse_width // BLK), f32),
            pltpu.SemaphoreType.DMA((lower // chunk,)),
        ],
        flops=4 * rows * coarse_depth * coarse_width,
        moved=2 * coarse_depth * coarse_width,
        limit=24 * MIB,
    )(coarse_upper, coarse_middle, coarse_factor, *arrived)
    field = sds((pairs, size, BLK), f32)
    kept, crossing = call(
        functools.partial(merge_kernel, own, rows, grp_count),
        [field, field],
        [SMEM] + [VMEM] * (1 + grp_count),
        [pltpu.VMEM((rows * blocks, BLK), f32), pltpu.VMEM((2 * pairs, size, BLK), f32)],
    )(margin, spread, *panels)
    distance = 1
    while kept.shape[0] > 1:
        half = sds((kept.shape[0] // 2, size, BLK), f32)
        kept, crossing = call(add_kernel, [half, half], [VMEM, VMEM])(
            kept, swap(crossing, "sub", distance)
        )
        distance *= 2
    return call(
        functools.partial(last_kernel, own, rows),
        sds((rows, own_width), f32),
        [VMEM, VMEM],
        [pltpu.VMEM((size, BLK), f32)],
    )(kept, swap(crossing, "sub", distance))


def solution(mesh):
    placed = (P(None, "sub"), P(), P("sub"), P("sub", "grp", None), P("sub", None))
    return jax.shard_map(
        on_device, mesh=mesh, in_specs=placed, out_specs=P("grp", "sub"), check_vma=False
    )
```

```python
import functools

import jax
import jax.numpy as jnp
from jax import lax
from jax.experimental import pallas as pl
from jax.experimental.pallas import tpu as pltpu
from jax.sharding import PartitionSpec as P

BLK = 128
MIB = 1024 * 1024
VMEM = pl.BlockSpec(memory_space=pltpu.VMEM)
SMEM = pl.BlockSpec(memory_space=pltpu.SMEM)
HBM = pl.BlockSpec(memory_space=pltpu.HBM)
NT = (((1,), (1,)), ((), ()))
TN = (((0,), (0,)), ((), ()))


def call(kernel, out, specs, scratch=(), limit=12 * MIB, flops=0, moved=0, **options):
    return pl.pallas_call(
        kernel,
        out_shape=out,
        in_specs=specs,
        out_specs=jax.tree.map(lambda _: VMEM, out),
        scratch_shapes=scratch,
        compiler_params=pltpu.CompilerParams(vmem_limit_bytes=limit),
        cost_estimate=pl.CostEstimate(flops=flops, bytes_accessed=moved, transcendentals=0),
        **options,
    )


def mm(left, right, dims=(((1,), (0,)), ((), ()))):
    return lax.dot_general(left, right, dims, preferred_element_type=jnp.float32)


def split3(value):
    high = value.astype(jnp.bfloat16)
    rest = value - high.astype(jnp.float32)
    middle = rest.astype(jnp.bfloat16)
    low = (rest - middle.astype(jnp.float32)).astype(jnp.bfloat16)
    return [high, middle, low]


def stage_kernel(own, rows, residual_hbm, aggregate_hbm, residual, mine, names, block_rows, aggregate, sems):
    pairs = ((residual_hbm, residual), (aggregate_hbm, aggregate))
    copies = [pltpu.make_async_copy(a, b, sems.at[i]) for i, (a, b) in enumerate(pairs)]
    start(copies)
    for copy in copies:
        copy.wait()
    names[...] = aggregate[...].astype(jnp.float32)
    mine[...] = rows_of(residual, own, rows, block_rows)


def rows_of(residual, own, rows, block_rows):
    rhs = residual.shape[0]
    for b in range(own):
        block_rows[pl.ds(b, rhs, stride=own), :] = residual[:, b * BLK : (b + 1) * BLK]
    first = lax.axis_index("grp") * rows * own
    return block_rows[pl.ds(pl.multiple_of(first, 8), rows * own), :]


def pack_kernel(own, rows, pad, margin_hbm, residual, mine, names, near_names, near, *refs):
    *outs, away, block_rows, margin, sem = refs
    copy = pltpu.make_async_copy(margin_hbm, margin, sem)
    copy.start()
    halo = margin.shape[1]
    rhs = residual.shape[0]
    me = lax.axis_index("sub")
    size = own * rows
    both = [mine[...], rows_of(near, own, rows, block_rows)]
    labels = [names[...], near_names[...].astype(jnp.float32)]
    at = 2 * size
    for out in outs:
        out[at : at + pad, :] = jnp.zeros((pad, BLK), jnp.float32)
        for i in range(2):
            out[i * size : (i + 1) * size, :] = both[i]
            out[at + i : at + i + 1, :own] = labels[i]
    copy.wait()
    for k in range(halo):
        distance = (me ^ (margin[me, k] // own)) // 2
        away[k : k + 1, :] = jnp.full((1, BLK), distance, jnp.int32)
    for e, out in enumerate(outs):
        target = me ^ (2 * e)
        for k in range(halo):
            block = margin[target, k]
            owner = block // own
            where = pl.ds(pl.multiple_of((block - owner * own) * BLK, BLK), BLK)
            out[at + pad + k * rhs : at + pad + (k + 1) * rhs, :] = jnp.where(
                owner == me, residual[:, where], near[:, where]
            )


def panel_copies(source, target, chunk, sems, first=0):
    copies = []
    for n in range(target.shape[0] // chunk):
        span = pl.ds(first + n * chunk, chunk)
        copies.append(
            pltpu.make_async_copy(source.at[span], target.at[pl.ds(n * chunk, chunk)], sems.at[n])
        )
    return copies


def start(copies):
    for copy in copies:
        copy.start()


def first_product(factor, right, tile, turned=False):
    parts = []
    for n in range(factor.shape[0] // tile):
        rows = factor[n * tile : (n + 1) * tile, :]
        parts.append(mm(rows, right, NT).T if turned else mm(right, rows, NT))
    return jnp.concatenate(parts, axis=1)


def in_own_block(body):
    pl.when(lax.axis_index("sub") >= 0)(body)


def load_kernel(
    chunk, tile, residual, fine_hbm, coarse_hbm, after, inner, fine, coarse, sems, more
):
    depth = fine.shape[1]
    own_width = residual.shape[1]
    half = depth // 2
    each = half // chunk
    start(panel_copies(fine_hbm.at[0], fine.at[0], chunk, sems))
    late = panel_copies(coarse_hbm, coarse, coarse.shape[0] // 4, more)

    def step(n, carry):
        for i in range(each):
            span = pl.ds(pl.multiple_of(n * half + i * chunk, chunk), chunk)
            pltpu.make_async_copy(fine_hbm.at[0, span], fine.at[0, span], sems.at[n * each + i]).wait()
        pl.when(n == 0)(lambda: start(late))
        local = residual[...].astype(jnp.bfloat16)
        for i in range(half // tile):
            at = pl.multiple_of(n * half + i * tile, tile)
            rows = fine[0, pl.ds(at, tile), pl.ds(0, own_width)]
            inner[:, pl.ds(at, tile)] = mm(local, rows, NT)
        return carry

    lax.fori_loop(0, 2, step, 0)
    for copy in late:
        copy.wait()


def fine_kernel(own, rows, begin, chunk, tile, pairs, away, begun, factor, coarse_hbm, *refs):
    arrived = refs[:pairs]
    *outs, coarse, table, sems = refs[pairs:]
    done = coarse_hbm.shape[0] // 4
    copies = panel_copies(coarse_hbm, coarse, chunk, sems, done)
    start(copies)
    rhs = begun.shape[0]
    halo = away.shape[0]
    depth, width = factor.shape[1:]
    blocks = width // BLK
    group = lax.axis_index("grp")
    tiles = []
    for k in range(halo):
        span = slice(begin + k * rhs, begin + (k + 1) * rhs)
        distance = away[k : k + 1, :]
        part = arrived[0][span, :]
        for e in range(1, pairs):
            part = jnp.where(distance == e, arrived[e][span, :], part)
        tiles.append(part.astype(jnp.bfloat16))
    local = jnp.concatenate(tiles, axis=1)
    far = factor.at[0, :, pl.ds(own * BLK, halo * BLK)]
    mid = (begun[...] + first_product(far, local, tile)).astype(jnp.bfloat16)
    for n in range(width // 256):
        part = mm(mid, factor[0, :, n * 256 : (n + 1) * 256])
        for i in range(256 // BLK):
            b = n * (256 // BLK) + i
            table[pl.ds(b, rhs, stride=blocks), :] = part[:, i * BLK : (i + 1) * BLK]
    size = rows * blocks
    for d, out in enumerate(outs):
        out[...] = table[pl.ds(pl.multiple_of((group ^ d) * size, 8), size), :]

    @in_own_block
    def _():
        for copy in copies:
            copy.wait()


def coarse_kernel(own, rows, chunk, tile, pairs, margin_hbm, upper, middle, factor_hbm, *refs):
    arrived = refs[:pairs]
    out, place, table, lower, begun, field, margin, sem, sems = refs[pairs:]
    small = pltpu.make_async_copy(margin_hbm, margin, sem)
    small.start()
    done = upper.shape[0] + middle.shape[0]
    width = upper.shape[1]
    copies = panel_copies(factor_hbm, lower, chunk, sems, done)
    start(copies)
    coarse = width // BLK
    size = own * rows
    sources = 2 * pairs
    parts = [(part, i) for part in arrived for i in range(2)]
    names = jnp.concatenate(
        [part[2 * size + i : 2 * size + i + 1, :] for part, i in parts], axis=0
    ).T
    catalog = lax.broadcasted_iota(jnp.int32, (own, coarse), 1).astype(jnp.float32)
    member = jnp.concatenate(
        [(names[:own, s : s + 1] == catalog).astype(jnp.float32) for s in range(sources)], axis=0
    ).astype(jnp.bfloat16)
    whole = jnp.concatenate(
        [
            jnp.concatenate(
                [part[i * size + r * own : i * size + (r + 1) * own, :] for part, i in parts],
                axis=0,
            )
            for r in range(rows)
        ],
        axis=1,
    )
    ones = jnp.ones((own * sources, BLK), jnp.bfloat16)
    span = rows * BLK
    found = mm(member, jnp.concatenate(split3(whole) + [ones], axis=1), TN)
    sums = found[:, :span] + found[:, span : 2 * span] + found[:, 2 * span : 3 * span]
    counts = jnp.maximum(found[:, 3 * span :], 1.0)
    for r in range(rows):
        table[r * coarse : (r + 1) * coarse, :] = sums[:, r * BLK : (r + 1) * BLK] / counts
    right = jnp.concatenate(
        [table[pl.ds(j, rows, stride=coarse), :] for j in range(coarse)], axis=1
    ).astype(jnp.bfloat16)
    field[...] = member.astype(jnp.float32)
    begun[:, : upper.shape[0]] = first_product(upper, right, tile)
    begun[:, upper.shape[0] : done] = first_product(middle, right, tile, True)
    place[...] = jnp.zeros(place.shape, jnp.int32)

    @in_own_block
    def _():
        for copy in copies + [small]:
            copy.wait()
        me = lax.axis_index("sub")
        for k in range(margin.shape[1]):
            block = margin[me, k]
            owner = block // own
            row = (me ^ owner) * own + block - owner * own
            place[pl.ds(row, 1), :] = jnp.full((1, BLK), k + 1, jnp.int32)
        right = jnp.concatenate(
            [table[pl.ds(j, rows, stride=coarse), :] for j in range(coarse)], axis=1
        ).astype(jnp.bfloat16)
        half = lower.shape[0] // 2
        low = [
            first_product(lower.at[pl.ds(i * half, half)], right, tile, i == 1) for i in range(2)
        ]
        low = jnp.concatenate(low, axis=1).astype(jnp.bfloat16)
        mid = begun[...].astype(jnp.bfloat16)
        high = mid[:, : upper.shape[0]]
        mid = mid[:, upper.shape[0] :]
        for n in range(width // 256):
            where = slice(n * 256, (n + 1) * 256)
            part = mm(high, upper[:, where]) + mm(mid, middle[:, where]) + mm(low, lower[:, where])
            for i in range(256 // BLK):
                j = n * (256 // BLK) + i
                table[pl.ds(j, rows, stride=coarse), :] = part[:, i * BLK : (i + 1) * BLK]
        member = field[...].astype(jnp.bfloat16)
        solved = jnp.concatenate([table[r * coarse : (r + 1) * coarse, :] for r in range(rows)], axis=1)
        spread = mm(member, jnp.concatenate(split3(solved), axis=1))
        spread = spread[:, :span] + spread[:, span : 2 * span] + spread[:, 2 * span :]
        for s in range(sources):
            for r in range(rows):
                out[s, r * own : (r + 1) * own, :] = spread[
                    s * own : (s + 1) * own, r * BLK : (r + 1) * BLK
                ]


def merge_kernel(own, rows, groups, halo, place, spread, *refs):
    arrived = refs[:groups]
    kept, near = refs[groups:]
    blocks = own + halo
    total = arrived[0][...]
    for part in arrived[1:]:
        total = total + part[...]
    for d in range(spread.shape[0]):
        where = place[d * own : (d + 1) * own, :]
        hits = [where == k + 1 for k in range(halo)] if d else []
        out = near if d % 2 else kept
        for r in range(rows):
            span = slice(r * own, (r + 1) * own)
            field = spread[d, span, :]
            if d == 0:
                field = field + total[r * blocks : r * blocks + own, :]
            for k, hit in enumerate(hits):
                row = r * blocks + own + k
                field = field + jnp.where(hit, total[row : row + 1, :], 0.0)
            out[d // 2, span, :] = field


def add_kernel(kept, arrived, *outs):
    for e, out in enumerate(outs):
        out[...] = kept[e] + arrived[e]


def last_kernel(own, rows, *refs):
    *arrived, out, total = refs
    summed = arrived[0][...]
    for part in arrived[1:]:
        summed = summed + part[...]
    total[...] = summed
    for b in range(own):
        out[:, b * BLK : (b + 1) * BLK] = total[pl.ds(b, rows, stride=own), :]


def swap(value, axis, distance):
    count = lax.axis_size(axis)
    return lax.ppermute(value, axis, [(i, i ^ distance) for i in range(count)])


def exchange(parts, axis, unit=1):
    there = [swap(parts[d], axis, d * unit) for d in range(len(parts) - 1, 0, -1)]
    return [parts[0]] + there[::-1]


def on_device(residual, margin, aggregate, local_factor, coarse_factor):
    pairs = lax.axis_size("sub") // 2
    grp_count = lax.axis_size("grp")
    rhs, own_width = residual.shape
    own = own_width // BLK
    rows = rhs // grp_count
    halo = margin.shape[1]
    pad = 8
    begin = 2 * own * rows + pad
    f32 = jnp.float32
    sds = jax.ShapeDtypeStruct
    _, depth, width = local_factor.shape
    coarse_depth, coarse_width = coarse_factor.shape
    blocks = width // BLK
    in_hbm = functools.partial(pltpu.with_memory_space_constraint, memory_space=pltpu.HBM)
    aggregate = aggregate.reshape(1, own)
    local_factor = in_hbm(local_factor)
    coarse_factor = in_hbm(coarse_factor)

    near = swap(residual, "sub", 1)
    near_names = swap(aggregate, "sub", 1)
    held, mine, names = call(
        functools.partial(stage_kernel, own, rows),
        (sds(residual.shape, f32), sds((own * rows, BLK), f32), sds((1, own), f32)),
        [HBM, HBM],
        [
            pltpu.VMEM((own * rhs, BLK), f32),
            pltpu.VMEM((1, own), jnp.int32),
            pltpu.SemaphoreType.DMA((2,)),
        ],
        moved=8 * rhs * own_width,
    )(in_hbm(residual), in_hbm(aggregate))
    margin = in_hbm(margin)
    *outgoing, away = call(
        functools.partial(pack_kernel, own, rows, pad),
        [sds((begin + halo * rhs, BLK), f32)] * pairs + [sds((halo, BLK), jnp.int32)],
        [HBM] + [VMEM] * 5,
        [
            pltpu.VMEM((own * rhs, BLK), f32),
            pltpu.SMEM(margin.shape, jnp.int32),
            pltpu.SemaphoreType.DMA,
        ],
    )(margin, held, mine, names, near_names, near)
    arrived = exchange(outgoing, "sub", 2)
    quarter = coarse_depth // 4
    tile, coarse_tile = min(256, depth // 2), min(256, quarter)
    chunk = depth // 8
    begun, local_factor, coarse_upper = call(
        functools.partial(load_kernel, chunk, tile),
        (
            sds((rhs, depth), f32),
            sds(local_factor.shape, local_factor.dtype),
            sds((quarter, coarse_width), coarse_factor.dtype),
        ),
        [VMEM, HBM, HBM, pl.BlockSpec(memory_space=pl.ANY)],
        [
            pltpu.SemaphoreType.DMA((depth // chunk,)),
            pltpu.SemaphoreType.DMA((4,)),
        ],
        flops=2 * rhs * depth * own_width,
        moved=2 * depth * width + 2 * quarter * coarse_width,
    )(held, local_factor, coarse_factor, arrived[0])
    chunk = quarter // 4
    *fine, coarse_middle = call(
        functools.partial(fine_kernel, own, rows, begin, chunk, tile, pairs),
        [sds((rows * blocks, BLK), f32)] * grp_count
        + [sds((quarter, coarse_width), coarse_factor.dtype)],
        [VMEM, VMEM, VMEM, HBM] + [VMEM] * pairs,
        [pltpu.VMEM((rhs * blocks, BLK), f32), pltpu.SemaphoreType.DMA((quarter // chunk,))],
        flops=4 * rhs * depth * width,
        moved=2 * depth * width + 2 * quarter * coarse_width,
    )(away, begun, local_factor, coarse_factor, *arrived)
    panels = exchange(fine, "grp")
    lower = coarse_depth - 2 * quarter
    size = own * rows
    spread, place = call(
        functools.partial(coarse_kernel, own, rows, chunk, coarse_tile, pairs),
        (sds((2 * pairs, size, BLK), f32), sds((2 * pairs * own, BLK), jnp.int32)),
        [HBM, VMEM, VMEM, HBM] + [VMEM] * pairs,
        [
            pltpu.VMEM((rows * (coarse_width // BLK), BLK), f32),
            pltpu.VMEM((lower, coarse_width), coarse_factor.dtype),
            pltpu.VMEM((rows, 2 * quarter), f32),
            pltpu.VMEM((2 * pairs * own, coarse_width // BLK), f32),
            pltpu.SMEM(margin.shape, jnp.int32),
            pltpu.SemaphoreType.DMA,
            pltpu.SemaphoreType.DMA((lower // chunk,)),
        ],
        flops=4 * rows * coarse_depth * coarse_width,
        moved=2 * coarse_depth * coarse_width,
        limit=24 * MIB,
    )(margin, coarse_upper, coarse_middle, coarse_factor, *arrived)
    field = sds((pairs, size, BLK), f32)
    kept, crossing = call(
        functools.partial(merge_kernel, own, rows, grp_count, halo),
        [field, field],
        [VMEM] * (2 + grp_count),
    )(place, spread, *panels)
    back = call(add_kernel, [sds((size, BLK), f32)] * pairs, [VMEM, VMEM])(
        kept, swap(crossing, "sub", 1)
    )
    return call(
        functools.partial(last_kernel, own, rows),
        sds((rows, own_width), f32),
        [VMEM] * pairs,
        [pltpu.VMEM((size, BLK), f32)],
    )(*exchange(list(back), "sub", 2)[::-1])


def solution(mesh):
    placed = (P(None, "sub"), P(), P("sub"), P("sub", "grp", None), P("sub", None))
    return jax.shard_map(
        on_device, mesh=mesh, in_specs=placed, out_specs=P("grp", "sub"), check_vma=False
    )
```

```python
import functools

import jax
import jax.numpy as jnp
from jax import lax
from jax.experimental import pallas as pl
from jax.experimental.pallas import tpu as pltpu
from jax.sharding import PartitionSpec as P

BLK = 128
MIB = 1024 * 1024
VMEM = pl.BlockSpec(memory_space=pltpu.VMEM)
SMEM = pl.BlockSpec(memory_space=pltpu.SMEM)
HBM = pl.BlockSpec(memory_space=pltpu.HBM)
NT = (((1,), (1,)), ((), ()))
TN = (((0,), (0,)), ((), ()))


def call(kernel, out, specs, scratch=(), limit=12 * MIB, flops=0, moved=0, **options):
    return pl.pallas_call(
        kernel,
        out_shape=out,
        in_specs=specs,
        out_specs=jax.tree.map(lambda _: VMEM, out),
        scratch_shapes=scratch,
        compiler_params=pltpu.CompilerParams(vmem_limit_bytes=limit),
        cost_estimate=pl.CostEstimate(flops=flops, bytes_accessed=moved, transcendentals=0),
        **options,
    )


def mm(left, right, dims=(((1,), (0,)), ((), ()))):
    return lax.dot_general(left, right, dims, preferred_element_type=jnp.float32)


def split3(value):
    high = value.astype(jnp.bfloat16)
    rest = value - high.astype(jnp.float32)
    middle = rest.astype(jnp.bfloat16)
    low = (rest - middle.astype(jnp.float32)).astype(jnp.bfloat16)
    return [high, middle, low]


def stage_kernel(own, rows, residual_hbm, aggregate_hbm, residual, mine, names, block_rows, aggregate, sems):
    pairs = ((residual_hbm, residual), (aggregate_hbm, aggregate))
    copies = [pltpu.make_async_copy(a, b, sems.at[i]) for i, (a, b) in enumerate(pairs)]
    start(copies)
    for copy in copies:
        copy.wait()
    names[...] = aggregate[...].astype(jnp.float32)
    mine[...] = rows_of(residual, own, rows, block_rows)


def rows_of(residual, own, rows, block_rows):
    rhs = residual.shape[0]
    for b in range(own):
        block_rows[pl.ds(b, rhs, stride=own), :] = residual[:, b * BLK : (b + 1) * BLK]
    first = lax.axis_index("grp") * rows * own
    return block_rows[pl.ds(pl.multiple_of(first, 8), rows * own), :]


def pack_kernel(own, rows, pad, margin_hbm, residual, mine, names, near_names, near, *refs):
    *outs, away, block_rows, margin, sem = refs
    copy = pltpu.make_async_copy(margin_hbm, margin, sem)
    copy.start()
    halo = margin.shape[1]
    rhs = residual.shape[0]
    me = lax.axis_index("sub")
    size = own * rows
    both = [mine[...], rows_of(near, own, rows, block_rows)]
    labels = [names[...], near_names[...].astype(jnp.float32)]
    at = 2 * size
    for out in outs:
        out[at : at + pad, :] = jnp.zeros((pad, BLK), jnp.float32)
        for i in range(2):
            out[i * size : (i + 1) * size, :] = both[i]
            out[at + i : at + i + 1, :own] = labels[i]
    copy.wait()
    for k in range(halo):
        distance = (me ^ (margin[me, k] // own)) // 2
        away[k : k + 1, :] = jnp.full((1, BLK), distance, jnp.int32)
    for e, out in enumerate(outs):
        target = me ^ (2 * e)
        for k in range(halo):
            block = margin[target, k]
            owner = block // own
            where = pl.ds(pl.multiple_of((block - owner * own) * BLK, BLK), BLK)
            out[at + pad + k * rhs : at + pad + (k + 1) * rhs, :] = jnp.where(
                owner == me, residual[:, where], near[:, where]
            )


def panel_copies(source, target, chunk, sems, first=0):
    copies = []
    for n in range(target.shape[0] // chunk):
        span = pl.ds(first + n * chunk, chunk)
        copies.append(
            pltpu.make_async_copy(source.at[span], target.at[pl.ds(n * chunk, chunk)], sems.at[n])
        )
    return copies


def start(copies):
    for copy in copies:
        copy.start()


def first_product(factor, right, tile):
    tile = min(tile, factor.shape[0])
    parts = [
        mm(right, factor[n * tile : (n + 1) * tile, :], NT) for n in range(factor.shape[0] // tile)
    ]
    return jnp.concatenate(parts, axis=1)


def in_own_block(body):
    pl.when(lax.axis_index("sub") >= 0)(body)


def load_kernel(
    chunk, tile, residual, fine_hbm, coarse_hbm, after, inner, fine, coarse, sems, more
):
    depth = fine.shape[1]
    own_width = residual.shape[1]
    half = depth // 2
    each = half // chunk
    start(panel_copies(fine_hbm.at[0], fine.at[0], chunk, sems))
    late = panel_copies(coarse_hbm, coarse, coarse.shape[0] // 4, more)

    def step(n, carry):
        for i in range(each):
            span = pl.ds(pl.multiple_of(n * half + i * chunk, chunk), chunk)
            pltpu.make_async_copy(fine_hbm.at[0, span], fine.at[0, span], sems.at[n * each + i]).wait()
        pl.when(n == 0)(lambda: start(late))
        local = residual[...].astype(jnp.bfloat16)
        for i in range(half // tile):
            at = pl.multiple_of(n * half + i * tile, tile)
            rows = fine[0, pl.ds(at, tile), pl.ds(0, own_width)]
            inner[:, pl.ds(at, tile)] = mm(local, rows, NT)
        return carry

    lax.fori_loop(0, 2, step, 0)
    for copy in late:
        copy.wait()


def fine_kernel(own, rows, begin, chunk, tile, pairs, away, begun, factor, coarse_hbm, *refs):
    arrived = refs[:pairs][::-1]
    *outs, coarse, table, sems = refs[pairs:]
    done = coarse_hbm.shape[0] // 4
    copies = panel_copies(coarse_hbm, coarse, chunk, sems, done)
    start(copies)
    rhs = begun.shape[0]
    halo = away.shape[0]
    depth, width = factor.shape[1:]
    blocks = width // BLK
    group = lax.axis_index("grp")
    tiles = []
    for k in range(halo):
        span = slice(begin + k * rhs, begin + (k + 1) * rhs)
        distance = away[k : k + 1, :]
        part = arrived[0][span, :]
        for e in range(1, pairs):
            part = jnp.where(distance == e, arrived[e][span, :], part)
        tiles.append(part.astype(jnp.bfloat16))
    local = jnp.concatenate(tiles, axis=1)
    far = factor.at[0, :, pl.ds(own * BLK, halo * BLK)]
    mid = (begun[...] + first_product(far, local, tile)).astype(jnp.bfloat16)
    for n in range(width // 256):
        part = mm(mid, factor[0, :, n * 256 : (n + 1) * 256])
        for i in range(256 // BLK):
            b = n * (256 // BLK) + i
            table[pl.ds(b, rhs, stride=blocks), :] = part[:, i * BLK : (i + 1) * BLK]
    size = rows * blocks
    for d, out in enumerate(outs):
        out[...] = table[pl.ds(pl.multiple_of((group ^ d) * size, 8), size), :]

    @in_own_block
    def _():
        for copy in copies:
            copy.wait()


def coarse_kernel(own, rows, chunk, tile, pairs, margin_hbm, upper, middle, factor_hbm, *refs):
    arrived = refs[:pairs]
    out, place, table, lower, begun, field, margin, sem, sems = refs[pairs:]
    small = pltpu.make_async_copy(margin_hbm, margin, sem)
    small.start()
    done = upper.shape[0] + middle.shape[0]
    width = upper.shape[1]
    copies = panel_copies(factor_hbm, lower, chunk, sems, done)
    start(copies)
    coarse = width // BLK
    size = own * rows
    sources = 2 * pairs
    parts = [(part, i) for part in arrived for i in range(2)]
    names = jnp.concatenate(
        [part[2 * size + i : 2 * size + i + 1, :] for part, i in parts], axis=0
    ).T
    catalog = lax.broadcasted_iota(jnp.int32, (own, coarse), 1).astype(jnp.float32)
    member = jnp.concatenate(
        [(names[:own, s : s + 1] == catalog).astype(jnp.float32) for s in range(sources)], axis=0
    ).astype(jnp.bfloat16)
    whole = jnp.concatenate(
        [
            jnp.concatenate(
                [part[i * size + r * own : i * size + (r + 1) * own, :] for part, i in parts],
                axis=0,
            )
            for r in range(rows)
        ],
        axis=1,
    )
    ones = jnp.ones((own * sources, BLK), jnp.bfloat16)
    span = rows * BLK
    found = mm(member, jnp.concatenate(split3(whole) + [ones], axis=1), TN)
    sums = found[:, :span] + found[:, span : 2 * span] + found[:, 2 * span : 3 * span]
    counts = jnp.maximum(found[:, 3 * span :], 1.0)
    for r in range(rows):
        table[r * coarse : (r + 1) * coarse, :] = sums[:, r * BLK : (r + 1) * BLK] / counts
    right = jnp.concatenate(
        [table[pl.ds(j, rows, stride=coarse), :] for j in range(coarse)], axis=1
    ).astype(jnp.bfloat16)
    field[...] = member.astype(jnp.float32)
    begun[:, : upper.shape[0]] = first_product(upper, right, tile)
    begun[:, upper.shape[0] : done] = first_product(middle, right, tile)
    place[...] = jnp.zeros(place.shape, jnp.int32)

    @in_own_block
    def _():
        for copy in copies + [small]:
            copy.wait()
        me = lax.axis_index("sub")
        for k in range(margin.shape[1]):
            block = margin[me, k]
            owner = block // own
            row = (me ^ owner) * own + block - owner * own
            place[pl.ds(row, 1), :] = jnp.full((1, BLK), k + 1, jnp.int32)
        right = jnp.concatenate(
            [table[pl.ds(j, rows, stride=coarse), :] for j in range(coarse)], axis=1
        ).astype(jnp.bfloat16)
        low = first_product(lower, right, tile).astype(jnp.bfloat16)
        mid = begun[...].astype(jnp.bfloat16)
        high = mid[:, : upper.shape[0]]
        mid = mid[:, upper.shape[0] :]
        for n in range(width // 256):
            where = slice(n * 256, (n + 1) * 256)
            part = mm(high, upper[:, where]) + mm(mid, middle[:, where]) + mm(low, lower[:, where])
            for i in range(256 // BLK):
                j = n * (256 // BLK) + i
                table[pl.ds(j, rows, stride=coarse), :] = part[:, i * BLK : (i + 1) * BLK]
        member = field[...].astype(jnp.bfloat16)
        solved = jnp.concatenate([table[r * coarse : (r + 1) * coarse, :] for r in range(rows)], axis=1)
        spread = mm(member, jnp.concatenate(split3(solved), axis=1))
        spread = spread[:, :span] + spread[:, span : 2 * span] + spread[:, 2 * span :]
        for s in range(sources):
            for r in range(rows):
                out[s, r * own : (r + 1) * own, :] = spread[
                    s * own : (s + 1) * own, r * BLK : (r + 1) * BLK
                ]


def merge_kernel(own, rows, groups, halo, place, spread, *refs):
    arrived = refs[:groups]
    kept, near = refs[groups:]
    blocks = own + halo
    total = arrived[0][...]
    for part in arrived[1:]:
        total = total + part[...]
    for d in range(spread.shape[0]):
        where = place[d * own : (d + 1) * own, :]
        hits = [where == k + 1 for k in range(halo)] if d else []
        out = near if d % 2 else kept
        for r in range(rows):
            span = slice(r * own, (r + 1) * own)
            field = spread[d, span, :]
            if d == 0:
                field = field + total[r * blocks : r * blocks + own, :]
            for k, hit in enumerate(hits):
                row = r * blocks + own + k
                field = field + jnp.where(hit, total[row : row + 1, :], 0.0)
            out[d // 2, span, :] = field


def add_kernel(kept, arrived, *outs):
    for e, out in enumerate(outs):
        out[...] = kept[e] + arrived[e]


def last_kernel(own, rows, *refs):
    *arrived, out, total = refs
    summed = arrived[0][...]
    for part in arrived[1:]:
        summed = summed + part[...]
    total[...] = summed
    for b in range(own):
        out[:, b * BLK : (b + 1) * BLK] = total[pl.ds(b, rows, stride=own), :]


def swap(value, axis, distance):
    count = lax.axis_size(axis)
    return lax.ppermute(value, axis, [(i, i ^ distance) for i in range(count)])


def exchange(parts, axis, unit=1):
    there = [swap(parts[d], axis, d * unit) for d in range(len(parts) - 1, 0, -1)]
    return [parts[0]] + there[::-1]


def on_device(residual, margin, aggregate, local_factor, coarse_factor):
    pairs = lax.axis_size("sub") // 2
    grp_count = lax.axis_size("grp")
    rhs, own_width = residual.shape
    own = own_width // BLK
    rows = rhs // grp_count
    halo = margin.shape[1]
    pad = 8
    begin = 2 * own * rows + pad
    f32 = jnp.float32
    sds = jax.ShapeDtypeStruct
    _, depth, width = local_factor.shape
    coarse_depth, coarse_width = coarse_factor.shape
    blocks = width // BLK
    in_hbm = functools.partial(pltpu.with_memory_space_constraint, memory_space=pltpu.HBM)
    aggregate = aggregate.reshape(1, own)
    local_factor = in_hbm(local_factor)
    coarse_factor = in_hbm(coarse_factor)

    near = swap(residual, "sub", 1)
    near_names = swap(aggregate, "sub", 1)
    held, mine, names = call(
        functools.partial(stage_kernel, own, rows),
        (sds(residual.shape, f32), sds((own * rows, BLK), f32), sds((1, own), f32)),
        [HBM, HBM],
        [
            pltpu.VMEM((own * rhs, BLK), f32),
            pltpu.VMEM((1, own), jnp.int32),
            pltpu.SemaphoreType.DMA((2,)),
        ],
        moved=8 * rhs * own_width,
    )(in_hbm(residual), in_hbm(aggregate))
    margin = in_hbm(margin)
    *outgoing, away = call(
        functools.partial(pack_kernel, own, rows, pad),
        [sds((begin + halo * rhs, BLK), f32)] * pairs + [sds((halo, BLK), jnp.int32)],
        [HBM] + [VMEM] * 5,
        [
            pltpu.VMEM((own * rhs, BLK), f32),
            pltpu.SMEM(margin.shape, jnp.int32),
            pltpu.SemaphoreType.DMA,
        ],
    )(margin, held, mine, names, near_names, near)
    arrived = exchange(outgoing, "sub", 2)
    quarter = coarse_depth // 4
    tile = min(512, depth // 2)
    chunk = depth // 8
    begun, local_factor, coarse_upper = call(
        functools.partial(load_kernel, chunk, tile),
        (
            sds((rhs, depth), f32),
            sds(local_factor.shape, local_factor.dtype),
            sds((quarter, coarse_width), coarse_factor.dtype),
        ),
        [VMEM, HBM, HBM, pl.BlockSpec(memory_space=pl.ANY)],
        [
            pltpu.SemaphoreType.DMA((depth // chunk,)),
            pltpu.SemaphoreType.DMA((4,)),
        ],
        flops=2 * rhs * depth * own_width,
        moved=2 * depth * width + 2 * quarter * coarse_width,
    )(held, local_factor, coarse_factor, arrived[0])
    chunk = quarter // 4
    *fine, coarse_middle = call(
        functools.partial(fine_kernel, own, rows, begin, chunk, tile, pairs),
        [sds((rows * blocks, BLK), f32)] * grp_count
        + [sds((quarter, coarse_width), coarse_factor.dtype)],
        [VMEM, VMEM, VMEM, HBM] + [VMEM] * pairs,
        [pltpu.VMEM((rhs * blocks, BLK), f32), pltpu.SemaphoreType.DMA((quarter // chunk,))],
        flops=4 * rhs * depth * width,
        moved=2 * depth * width + 2 * quarter * coarse_width,
    )(away, begun, local_factor, coarse_factor, *arrived[::-1])
    panels = exchange(fine, "grp")
    lower = coarse_depth - 2 * quarter
    size = own * rows
    spread, place = call(
        functools.partial(coarse_kernel, own, rows, chunk, tile, pairs),
        (sds((2 * pairs, size, BLK), f32), sds((2 * pairs * own, BLK), jnp.int32)),
        [HBM, VMEM, VMEM, HBM] + [VMEM] * pairs,
        [
            pltpu.VMEM((rows * (coarse_width // BLK), BLK), f32),
            pltpu.VMEM((lower, coarse_width), coarse_factor.dtype),
            pltpu.VMEM((rows, 2 * quarter), f32),
            pltpu.VMEM((2 * pairs * own, coarse_width // BLK), f32),
            pltpu.SMEM(margin.shape, jnp.int32),
            pltpu.SemaphoreType.DMA,
            pltpu.SemaphoreType.DMA((lower // chunk,)),
        ],
        flops=4 * rows * coarse_depth * coarse_width,
        moved=2 * coarse_depth * coarse_width,
        limit=24 * MIB,
    )(margin, coarse_upper, coarse_middle, coarse_factor, *arrived)
    field = sds((pairs, size, BLK), f32)
    kept, crossing = call(
        functools.partial(merge_kernel, own, rows, grp_count, halo),
        [field, field],
        [VMEM] * (2 + grp_count),
    )(place, spread, *panels)
    back = call(add_kernel, [sds((size, BLK), f32)] * pairs, [VMEM, VMEM])(
        kept, swap(crossing, "sub", 1)
    )
    return call(
        functools.partial(last_kernel, own, rows),
        sds((rows, own_width), f32),
        [VMEM] * pairs,
        [pltpu.VMEM((size, BLK), f32)],
    )(*exchange(list(back), "sub", 2)[::-1])


def solution(mesh):
    placed = (P(None, "sub"), P(), P("sub"), P("sub", "grp", None), P("sub", None))
    return jax.shard_map(
        on_device, mesh=mesh, in_specs=placed, out_specs=P("grp", "sub"), check_vma=False
    )
```

```python
import functools

import jax
import jax.numpy as jnp
from jax import lax
from jax.experimental import pallas as pl
from jax.experimental.pallas import tpu as pltpu
from jax.sharding import PartitionSpec as P

BLK = 128
MIB = 1024 * 1024
VMEM = pl.BlockSpec(memory_space=pltpu.VMEM)
SMEM = pl.BlockSpec(memory_space=pltpu.SMEM)
HBM = pl.BlockSpec(memory_space=pltpu.HBM)
NT = (((1,), (1,)), ((), ()))
TN = (((0,), (0,)), ((), ()))


def call(kernel, out, specs, scratch=(), limit=12 * MIB, flops=0, moved=0, **options):
    return pl.pallas_call(
        kernel,
        out_shape=out,
        in_specs=specs,
        out_specs=jax.tree.map(lambda _: VMEM, out),
        scratch_shapes=scratch,
        compiler_params=pltpu.CompilerParams(vmem_limit_bytes=limit),
        cost_estimate=pl.CostEstimate(flops=flops, bytes_accessed=moved, transcendentals=0),
        **options,
    )


def mm(left, right, dims=(((1,), (0,)), ((), ()))):
    return lax.dot_general(left, right, dims, preferred_element_type=jnp.float32)


def split3(value):
    high = value.astype(jnp.bfloat16)
    rest = value - high.astype(jnp.float32)
    middle = rest.astype(jnp.bfloat16)
    low = (rest - middle.astype(jnp.float32)).astype(jnp.bfloat16)
    return [high, middle, low]


def stage_kernel(own, rows, residual_hbm, aggregate_hbm, residual, mine, names, block_rows, aggregate, sems):
    pairs = ((residual_hbm, residual), (aggregate_hbm, aggregate))
    copies = [pltpu.make_async_copy(a, b, sems.at[i]) for i, (a, b) in enumerate(pairs)]
    start(copies)
    for copy in copies:
        copy.wait()
    names[...] = aggregate[...].astype(jnp.float32)
    mine[...] = rows_of(residual, own, rows, block_rows)


def rows_of(residual, own, rows, block_rows):
    rhs = residual.shape[0]
    for b in range(own):
        block_rows[pl.ds(b, rhs, stride=own), :] = residual[:, b * BLK : (b + 1) * BLK]
    first = lax.axis_index("grp") * rows * own
    return block_rows[pl.ds(pl.multiple_of(first, 8), rows * own), :]


def pack_kernel(own, rows, pad, margin_hbm, residual, mine, names, near_names, near, *refs):
    *outs, away, place, block_rows, margin, sem = refs
    copy = pltpu.make_async_copy(margin_hbm, margin, sem)
    copy.start()
    halo = margin.shape[1]
    rhs = residual.shape[0]
    me = lax.axis_index("sub")
    size = own * rows
    both = [mine[...], rows_of(near, own, rows, block_rows)]
    labels = [names[...], near_names[...].astype(jnp.float32)]
    at = 2 * size
    for out in outs:
        out[at : at + pad, :] = jnp.zeros((pad, BLK), jnp.float32)
        for i in range(2):
            out[i * size : (i + 1) * size, :] = both[i]
            out[at + i : at + i + 1, :own] = labels[i]
    place[...] = jnp.zeros(place.shape, jnp.int32)
    copy.wait()
    for k in range(halo):
        block = margin[me, k]
        owner = block // own
        distance = me ^ owner
        away[k : k + 1, :] = jnp.full((1, BLK), distance // 2, jnp.int32)
        row = distance * own + block - owner * own
        place[pl.ds(row, 1), :] = jnp.full((1, BLK), k + 1, jnp.int32)
    for e, out in enumerate(outs):
        target = me ^ (2 * e)
        for k in range(halo):
            block = margin[target, k]
            owner = block // own
            where = pl.ds(pl.multiple_of((block - owner * own) * BLK, BLK), BLK)
            out[at + pad + k * rhs : at + pad + (k + 1) * rhs, :] = jnp.where(
                owner == me, residual[:, where], near[:, where]
            )


def panel_copies(source, target, chunk, sems, first=0):
    copies = []
    for n in range(target.shape[0] // chunk):
        span = pl.ds(first + n * chunk, chunk)
        copies.append(
            pltpu.make_async_copy(source.at[span], target.at[pl.ds(n * chunk, chunk)], sems.at[n])
        )
    return copies


def start(copies):
    for copy in copies:
        copy.start()


def first_product(factor, right, tile):
    tile = min(tile, factor.shape[0])
    parts = [
        mm(right, factor[n * tile : (n + 1) * tile, :], NT) for n in range(factor.shape[0] // tile)
    ]
    return jnp.concatenate(parts, axis=1)


def in_own_block(body):
    pl.when(lax.axis_index("sub") >= 0)(body)


def load_kernel(
    chunk, tile, residual, fine_hbm, coarse_hbm, after, inner, fine, coarse, sems, more
):
    depth = fine.shape[1]
    own_width = residual.shape[1]
    half = depth // 2
    each = half // chunk
    start(panel_copies(fine_hbm.at[0], fine.at[0], chunk, sems))
    late = panel_copies(coarse_hbm, coarse, coarse.shape[0] // 4, more)

    def step(n, carry):
        for i in range(each):
            span = pl.ds(pl.multiple_of(n * half + i * chunk, chunk), chunk)
            pltpu.make_async_copy(fine_hbm.at[0, span], fine.at[0, span], sems.at[n * each + i]).wait()
        pl.when(n == 0)(lambda: start(late))
        local = residual[...].astype(jnp.bfloat16)
        for i in range(half // tile):
            at = pl.multiple_of(n * half + i * tile, tile)
            rows = fine[0, pl.ds(at, tile), pl.ds(0, own_width)]
            inner[:, pl.ds(at, tile)] = mm(local, rows, NT)
        return carry

    lax.fori_loop(0, 2, step, 0)
    for copy in late:
        copy.wait()


def form_sums(own, rows, coarse, arrived, named, table):
    size = own * rows
    sources = 2 * len(arrived)
    parts = [(part, i) for part in arrived for i in range(2)]
    names = jnp.concatenate(
        [part[2 * size + i : 2 * size + i + 1, :] for part, i in parts], axis=0
    ).T
    catalog = lax.broadcasted_iota(jnp.int32, (own, coarse), 1).astype(jnp.float32)
    member = jnp.concatenate(
        [(names[:own, s : s + 1] == catalog).astype(jnp.float32) for s in range(sources)], axis=0
    ).astype(jnp.bfloat16)
    whole = jnp.concatenate(
        [
            jnp.concatenate(
                [part[i * size + r * own : i * size + (r + 1) * own, :] for part, i in parts],
                axis=0,
            )
            for r in range(rows)
        ],
        axis=1,
    )
    ones = jnp.ones((own * sources, BLK), jnp.bfloat16)
    span = rows * BLK
    found = mm(member, jnp.concatenate(split3(whole) + [ones], axis=1), TN)
    sums = found[:, :span] + found[:, span : 2 * span] + found[:, 2 * span : 3 * span]
    counts = jnp.maximum(found[:, 3 * span :], 1.0)
    for r in range(rows):
        table[r * coarse : (r + 1) * coarse, :] = sums[:, r * BLK : (r + 1) * BLK] / counts
    named[...] = member.astype(jnp.float32)


def fine_kernel(own, rows, begin, chunk, tile, pairs, away, begun, factor, coarse_hbm, *refs):
    arrived = refs[:pairs][::-1]
    *outs, coarse, named, sums, table, sems = refs[pairs:]
    done = coarse_hbm.shape[0] // 4
    copies = panel_copies(coarse_hbm, coarse, chunk, sems, done)
    start(copies)
    rhs = begun.shape[0]
    halo = away.shape[0]
    depth, width = factor.shape[1:]
    blocks = width // BLK
    group = lax.axis_index("grp")
    tiles = []
    for k in range(halo):
        span = slice(begin + k * rhs, begin + (k + 1) * rhs)
        distance = away[k : k + 1, :]
        part = arrived[0][span, :]
        for e in range(1, pairs):
            part = jnp.where(distance == e, arrived[e][span, :], part)
        tiles.append(part.astype(jnp.bfloat16))
    form_sums(own, rows, coarse.shape[1] // BLK, arrived, named, sums)
    local = jnp.concatenate(tiles, axis=1)
    far = factor.at[0, :, pl.ds(own * BLK, halo * BLK)]
    mid = (begun[...] + first_product(far, local, tile)).astype(jnp.bfloat16)
    for n in range(width // 256):
        part = mm(mid, factor[0, :, n * 256 : (n + 1) * 256])
        for i in range(256 // BLK):
            b = n * (256 // BLK) + i
            table[pl.ds(b, rhs, stride=blocks), :] = part[:, i * BLK : (i + 1) * BLK]
    size = rows * blocks
    for d, out in enumerate(outs):
        out[...] = table[pl.ds(pl.multiple_of((group ^ d) * size, 8), size), :]

    @in_own_block
    def _():
        for copy in copies:
            copy.wait()


def coarse_kernel(own, rows, chunk, tile, upper, middle, factor_hbm, member, sums, *refs):
    out, table, lower, begun, sems = refs
    done = upper.shape[0] + middle.shape[0]
    width = upper.shape[1]
    copies = panel_copies(factor_hbm, lower, chunk, sems, done)
    start(copies)
    coarse = width // BLK
    span = rows * BLK

    def right():
        parts = [sums[pl.ds(j, rows, stride=coarse), :] for j in range(coarse)]
        return jnp.concatenate(parts, axis=1).astype(jnp.bfloat16)

    first = right()
    begun[:, : upper.shape[0]] = first_product(upper, first, tile)
    begun[:, upper.shape[0] : done] = first_product(middle, first, tile)

    @in_own_block
    def _():
        for copy in copies:
            copy.wait()
        low = first_product(lower, right(), tile).astype(jnp.bfloat16)
        mid = begun[...].astype(jnp.bfloat16)
        high = mid[:, : upper.shape[0]]
        mid = mid[:, upper.shape[0] :]
        for n in range(width // 256):
            where = slice(n * 256, (n + 1) * 256)
            part = mm(high, upper[:, where]) + mm(mid, middle[:, where]) + mm(low, lower[:, where])
            for i in range(256 // BLK):
                j = n * (256 // BLK) + i
                table[pl.ds(j, rows, stride=coarse), :] = part[:, i * BLK : (i + 1) * BLK]
        solved = jnp.concatenate([table[r * coarse : (r + 1) * coarse, :] for r in range(rows)], axis=1)
        spread = mm(member[...].astype(jnp.bfloat16), jnp.concatenate(split3(solved), axis=1))
        spread = spread[:, :span] + spread[:, span : 2 * span] + spread[:, 2 * span :]
        for s in range(out.shape[0]):
            for r in range(rows):
                out[s, r * own : (r + 1) * own, :] = spread[
                    s * own : (s + 1) * own, r * BLK : (r + 1) * BLK
                ]


def merge_kernel(own, rows, groups, halo, place, spread, *refs):
    arrived = refs[:groups]
    kept, near = refs[groups:]
    blocks = own + halo
    total = arrived[0][...]
    for part in arrived[1:]:
        total = total + part[...]
    for d in range(spread.shape[0]):
        where = place[d * own : (d + 1) * own, :]
        hits = [where == k + 1 for k in range(halo)] if d else []
        out = near if d % 2 else kept
        for r in range(rows):
            span = slice(r * own, (r + 1) * own)
            field = spread[d, span, :]
            if d == 0:
                field = field + total[r * blocks : r * blocks + own, :]
            for k, hit in enumerate(hits):
                row = r * blocks + own + k
                field = field + jnp.where(hit, total[row : row + 1, :], 0.0)
            out[d // 2, span, :] = field


def add_kernel(kept, arrived, *outs):
    for e, out in enumerate(outs):
        out[...] = kept[e] + arrived[e]


def last_kernel(own, rows, *refs):
    *arrived, out, total = refs
    summed = arrived[0][...]
    for part in arrived[1:]:
        summed = summed + part[...]
    total[...] = summed
    for b in range(own):
        out[:, b * BLK : (b + 1) * BLK] = total[pl.ds(b, rows, stride=own), :]


def swap(value, axis, distance):
    count = lax.axis_size(axis)
    return lax.ppermute(value, axis, [(i, i ^ distance) for i in range(count)])


def exchange(parts, axis, unit=1):
    there = [swap(parts[d], axis, d * unit) for d in range(len(parts) - 1, 0, -1)]
    return [parts[0]] + there[::-1]


def on_device(residual, margin, aggregate, local_factor, coarse_factor):
    pairs = lax.axis_size("sub") // 2
    grp_count = lax.axis_size("grp")
    rhs, own_width = residual.shape
    own = own_width // BLK
    rows = rhs // grp_count
    halo = margin.shape[1]
    pad = 8
    begin = 2 * own * rows + pad
    f32 = jnp.float32
    sds = jax.ShapeDtypeStruct
    _, depth, width = local_factor.shape
    coarse_depth, coarse_width = coarse_factor.shape
    blocks = width // BLK
    in_hbm = functools.partial(pltpu.with_memory_space_constraint, memory_space=pltpu.HBM)
    aggregate = aggregate.reshape(1, own)
    local_factor = in_hbm(local_factor)
    coarse_factor = in_hbm(coarse_factor)

    near = swap(residual, "sub", 1)
    near_names = swap(aggregate, "sub", 1)
    held, mine, names = call(
        functools.partial(stage_kernel, own, rows),
        (sds(residual.shape, f32), sds((own * rows, BLK), f32), sds((1, own), f32)),
        [HBM, HBM],
        [
            pltpu.VMEM((own * rhs, BLK), f32),
            pltpu.VMEM((1, own), jnp.int32),
            pltpu.SemaphoreType.DMA((2,)),
        ],
        moved=8 * rhs * own_width,
    )(in_hbm(residual), in_hbm(aggregate))
    margin = in_hbm(margin)
    *outgoing, away, place = call(
        functools.partial(pack_kernel, own, rows, pad),
        [sds((begin + halo * rhs, BLK), f32)] * pairs
        + [sds((halo, BLK), jnp.int32), sds((2 * pairs * own, BLK), jnp.int32)],
        [HBM] + [VMEM] * 5,
        [
            pltpu.VMEM((own * rhs, BLK), f32),
            pltpu.SMEM(margin.shape, jnp.int32),
            pltpu.SemaphoreType.DMA,
        ],
    )(margin, held, mine, names, near_names, near)
    arrived = exchange(outgoing, "sub", 2)
    quarter = coarse_depth // 4
    tile = min(512, depth // 2)
    chunk = depth // 8
    begun, local_factor, coarse_upper = call(
        functools.partial(load_kernel, chunk, tile),
        (
            sds((rhs, depth), f32),
            sds(local_factor.shape, local_factor.dtype),
            sds((quarter, coarse_width), coarse_factor.dtype),
        ),
        [VMEM, HBM, HBM, pl.BlockSpec(memory_space=pl.ANY)],
        [
            pltpu.SemaphoreType.DMA((depth // chunk,)),
            pltpu.SemaphoreType.DMA((4,)),
        ],
        flops=2 * rhs * depth * own_width,
        moved=2 * depth * width + 2 * quarter * coarse_width,
    )(held, local_factor, coarse_factor, arrived[0])
    chunk = quarter // 4
    count = coarse_width // BLK
    *fine, coarse_middle, member, sums = call(
        functools.partial(fine_kernel, own, rows, begin, chunk, tile, pairs),
        [sds((rows * blocks, BLK), f32)] * grp_count
        + [
            sds((quarter, coarse_width), coarse_factor.dtype),
            sds((2 * pairs * own, count), f32),
            sds((rows * count, BLK), f32),
        ],
        [VMEM, VMEM, VMEM, HBM] + [VMEM] * pairs,
        [pltpu.VMEM((rhs * blocks, BLK), f32), pltpu.SemaphoreType.DMA((quarter // chunk,))],
        flops=4 * rhs * depth * width,
        moved=2 * depth * width + 2 * quarter * coarse_width,
    )(away, begun, local_factor, coarse_factor, *arrived[::-1])
    panels = exchange(fine, "grp")
    lower = coarse_depth - 2 * quarter
    size = own * rows
    spread = call(
        functools.partial(coarse_kernel, own, rows, chunk, tile),
        sds((2 * pairs, size, BLK), f32),
        [VMEM, VMEM, HBM, VMEM, VMEM],
        [
            pltpu.VMEM((rows * count, BLK), f32),
            pltpu.VMEM((lower, coarse_width), coarse_factor.dtype),
            pltpu.VMEM((rows, 2 * quarter), f32),
            pltpu.SemaphoreType.DMA((lower // chunk,)),
        ],
        flops=4 * rows * coarse_depth * coarse_width,
        moved=2 * coarse_depth * coarse_width,
        limit=24 * MIB,
    )(coarse_upper, coarse_middle, coarse_factor, member, sums)
    field = sds((pairs, size, BLK), f32)
    kept, crossing = call(
        functools.partial(merge_kernel, own, rows, grp_count, halo),
        [field, field],
        [VMEM] * (2 + grp_count),
    )(place, spread, *panels)
    back = call(add_kernel, [sds((size, BLK), f32)] * pairs, [VMEM, VMEM])(
        kept, swap(crossing, "sub", 1)
    )
    return call(
        functools.partial(last_kernel, own, rows),
        sds((rows, own_width), f32),
        [VMEM] * pairs,
        [pltpu.VMEM((size, BLK), f32)],
    )(*exchange(list(back), "sub", 2)[::-1])


def solution(mesh):
    placed = (P(None, "sub"), P(), P("sub"), P("sub", "grp", None), P("sub", None))
    return jax.shard_map(
        on_device, mesh=mesh, in_specs=placed, out_specs=P("grp", "sub"), check_vma=False
    )
```

```python
import functools

import jax
import jax.numpy as jnp
from jax import lax
from jax.experimental import pallas as pl
from jax.experimental.pallas import tpu as pltpu
from jax.sharding import PartitionSpec as P

BLK = 128
MIB = 1024 * 1024
VMEM = pl.BlockSpec(memory_space=pltpu.VMEM)
SMEM = pl.BlockSpec(memory_space=pltpu.SMEM)
HBM = pl.BlockSpec(memory_space=pltpu.HBM)
NT = (((1,), (1,)), ((), ()))
TN = (((0,), (0,)), ((), ()))


def call(kernel, out, specs, scratch=(), limit=12 * MIB, flops=0, moved=0, **options):
    return pl.pallas_call(
        kernel,
        out_shape=out,
        in_specs=specs,
        out_specs=jax.tree.map(lambda _: VMEM, out),
        scratch_shapes=scratch,
        compiler_params=pltpu.CompilerParams(vmem_limit_bytes=limit),
        cost_estimate=pl.CostEstimate(flops=flops, bytes_accessed=moved, transcendentals=0),
        **options,
    )


def mm(left, right, dims=(((1,), (0,)), ((), ()))):
    return lax.dot_general(left, right, dims, preferred_element_type=jnp.float32)


def split3(value):
    high = value.astype(jnp.bfloat16)
    rest = value - high.astype(jnp.float32)
    middle = rest.astype(jnp.bfloat16)
    low = (rest - middle.astype(jnp.float32)).astype(jnp.bfloat16)
    return [high, middle, low]


def stage_kernel(own, rows, residual_hbm, aggregate_hbm, residual, mine, names, block_rows, aggregate, sems):
    pairs = ((residual_hbm, residual), (aggregate_hbm, aggregate))
    copies = [pltpu.make_async_copy(a, b, sems.at[i]) for i, (a, b) in enumerate(pairs)]
    start(copies)
    for copy in copies:
        copy.wait()
    names[...] = aggregate[...].astype(jnp.float32)
    mine[...] = rows_of(residual, own, rows, block_rows)


def rows_of(residual, own, rows, block_rows):
    rhs = residual.shape[0]
    for b in range(own):
        block_rows[pl.ds(b, rhs, stride=own), :] = residual[:, b * BLK : (b + 1) * BLK]
    first = lax.axis_index("grp") * rows * own
    return block_rows[pl.ds(pl.multiple_of(first, 8), rows * own), :]


def pack_kernel(own, rows, pad, margin_hbm, residual, mine, names, near_names, near, *refs):
    *outs, away, place, block_rows, margin, sem = refs
    copy = pltpu.make_async_copy(margin_hbm, margin, sem)
    copy.start()
    halo = margin.shape[1]
    rhs = residual.shape[0]
    me = lax.axis_index("sub")
    size = own * rows
    both = [mine[...], rows_of(near, own, rows, block_rows)]
    labels = [names[...], near_names[...].astype(jnp.float32)]
    at = 2 * size
    for out in outs:
        out[at : at + pad, :] = jnp.zeros((pad, BLK), jnp.float32)
        for i in range(2):
            out[i * size : (i + 1) * size, :] = both[i]
            out[at + i : at + i + 1, :own] = labels[i]
    place[...] = jnp.zeros(place.shape, jnp.int32)
    copy.wait()
    for k in range(halo):
        block = margin[me, k]
        owner = block // own
        distance = me ^ owner
        away[k : k + 1, :] = jnp.full((1, BLK), distance // 2, jnp.int32)
        row = distance * own + block - owner * own
        place[pl.ds(row, 1), :] = jnp.full((1, BLK), k + 1, jnp.int32)
    for e, out in enumerate(outs):
        target = me ^ (2 * e)
        for k in range(halo):
            block = margin[target, k]
            owner = block // own
            where = pl.ds(pl.multiple_of((block - owner * own) * BLK, BLK), BLK)
            out[at + pad + k * rhs : at + pad + (k + 1) * rhs, :] = jnp.where(
                owner == me, residual[:, where], near[:, where]
            )


def panel_copies(source, target, chunk, sems, first=0):
    copies = []
    for n in range(target.shape[0] // chunk):
        span = pl.ds(first + n * chunk, chunk)
        copies.append(
            pltpu.make_async_copy(source.at[span], target.at[pl.ds(n * chunk, chunk)], sems.at[n])
        )
    return copies


def start(copies):
    for copy in copies:
        copy.start()


def first_product(factor, right, tile):
    tile = min(tile, factor.shape[0])
    parts = [
        mm(right, factor[n * tile : (n + 1) * tile, :], NT) for n in range(factor.shape[0] // tile)
    ]
    return jnp.concatenate(parts, axis=1)


def in_own_block(body):
    pl.when(lax.axis_index("sub") >= 0)(body)


def load_kernel(
    chunk, tile, residual, fine_hbm, coarse_hbm, after, inner, fine, coarse, sems, more
):
    depth = fine.shape[1]
    own_width = residual.shape[1]
    half = depth // 2
    each = half // chunk
    start(panel_copies(fine_hbm.at[0], fine.at[0], chunk, sems))
    late = panel_copies(coarse_hbm, coarse, coarse.shape[0] // 4, more)

    def step(n, carry):
        for i in range(each):
            span = pl.ds(pl.multiple_of(n * half + i * chunk, chunk), chunk)
            pltpu.make_async_copy(fine_hbm.at[0, span], fine.at[0, span], sems.at[n * each + i]).wait()
        pl.when(n == 0)(lambda: start(late))
        local = residual[...].astype(jnp.bfloat16)
        for i in range(half // tile):
            at = pl.multiple_of(n * half + i * tile, tile)
            rows = fine[0, pl.ds(at, tile), pl.ds(0, own_width)]
            inner[:, pl.ds(at, tile)] = mm(local, rows, NT)
        return carry

    lax.fori_loop(0, 2, step, 0)
    for copy in late:
        copy.wait()


def form_sums(own, rows, coarse, arrived, named, table):
    size = own * rows
    sources = 2 * len(arrived)
    parts = [(part, i) for part in arrived for i in range(2)]
    names = jnp.concatenate(
        [part[2 * size + i : 2 * size + i + 1, :] for part, i in parts], axis=0
    ).T
    catalog = lax.broadcasted_iota(jnp.int32, (own, coarse), 1).astype(jnp.float32)
    member = jnp.concatenate(
        [(names[:own, s : s + 1] == catalog).astype(jnp.float32) for s in range(sources)], axis=0
    ).astype(jnp.bfloat16)
    whole = jnp.concatenate(
        [
            jnp.concatenate(
                [part[i * size + r * own : i * size + (r + 1) * own, :] for part, i in parts],
                axis=0,
            )
            for r in range(rows)
        ],
        axis=1,
    )
    ones = jnp.ones((own * sources, BLK), jnp.bfloat16)
    span = rows * BLK
    found = mm(member, jnp.concatenate(split3(whole) + [ones], axis=1), TN)
    sums = found[:, :span] + found[:, span : 2 * span] + found[:, 2 * span : 3 * span]
    counts = jnp.maximum(found[:, 3 * span :], 1.0)
    for r in range(rows):
        table[r * coarse : (r + 1) * coarse, :] = sums[:, r * BLK : (r + 1) * BLK] / counts
    named[...] = member.astype(jnp.float32)


def fine_kernel(own, rows, begin, chunk, tile, pairs, away, begun, factor, coarse_hbm, *refs):
    arrived = refs[:pairs][::-1]
    *outs, coarse, named, sums, table, sems = refs[pairs:]
    done = coarse_hbm.shape[0] // 4
    copies = panel_copies(coarse_hbm, coarse, chunk, sems, done)
    start(copies)
    rhs = begun.shape[0]
    halo = away.shape[0]
    depth, width = factor.shape[1:]
    blocks = width // BLK
    group = lax.axis_index("grp")
    tiles = []
    for k in range(halo):
        span = slice(begin + k * rhs, begin + (k + 1) * rhs)
        distance = away[k : k + 1, :]
        part = arrived[0][span, :]
        for e in range(1, pairs):
            part = jnp.where(distance == e, arrived[e][span, :], part)
        tiles.append(part.astype(jnp.bfloat16))
    form_sums(own, rows, coarse.shape[1] // BLK, arrived, named, sums)
    local = jnp.concatenate(tiles, axis=1)
    far = factor.at[0, :, pl.ds(own * BLK, halo * BLK)]
    mid = (begun[...] + first_product(far, local, tile)).astype(jnp.bfloat16)
    for n in range(width // 256):
        part = mm(mid, factor[0, :, n * 256 : (n + 1) * 256])
        for i in range(256 // BLK):
            b = n * (256 // BLK) + i
            table[pl.ds(b, rhs, stride=blocks), :] = part[:, i * BLK : (i + 1) * BLK]
    size = rows * blocks
    for d, out in enumerate(outs):
        out[...] = table[pl.ds(pl.multiple_of((group ^ d) * size, 8), size), :]

    @in_own_block
    def _():
        for copy in copies:
            copy.wait()


def coarse_kernel(own, rows, chunk, tile, upper, middle, factor_hbm, member, sums, *refs):
    out, table, lower, sems = refs
    done = upper.shape[0] + middle.shape[0]
    width = upper.shape[1]
    copies = panel_copies(factor_hbm, lower, chunk, sems, done)
    start(copies)
    coarse = width // BLK
    span = rows * BLK

    def right():
        parts = [sums[pl.ds(j, rows, stride=coarse), :] for j in range(coarse)]
        return jnp.concatenate(parts, axis=1).astype(jnp.bfloat16)

    def second_product(mid, *panels):
        for n in range(width // 256):
            where = slice(n * 256, (n + 1) * 256)
            at = 0
            part = None
            for panel in panels:
                piece = mm(mid[:, at : at + panel.shape[0]], panel[:, where])
                part = piece if part is None else part + piece
                at += panel.shape[0]
            for i in range(256 // BLK):
                yield n * (256 // BLK) + i, part[:, i * BLK : (i + 1) * BLK]

    first = right()
    mid = [first_product(panel, first, tile) for panel in (upper, middle)]
    mid = jnp.concatenate(mid, axis=1).astype(jnp.bfloat16)
    for j, part in second_product(mid, upper, middle):
        table[pl.ds(j, rows, stride=coarse), :] = part

    @in_own_block
    def _():
        for copy in copies:
            copy.wait()
        mid = first_product(lower, right(), tile).astype(jnp.bfloat16)
        for j, part in second_product(mid, lower):
            where = pl.ds(j, rows, stride=coarse)
            table[where, :] = table[where, :] + part
        solved = jnp.concatenate([table[r * coarse : (r + 1) * coarse, :] for r in range(rows)], axis=1)
        spread = mm(member[...].astype(jnp.bfloat16), jnp.concatenate(split3(solved), axis=1))
        spread = spread[:, :span] + spread[:, span : 2 * span] + spread[:, 2 * span :]
        for s in range(out.shape[0]):
            for r in range(rows):
                out[s, r * own : (r + 1) * own, :] = spread[
                    s * own : (s + 1) * own, r * BLK : (r + 1) * BLK
                ]


def merge_kernel(own, rows, groups, halo, place, spread, *refs):
    arrived = refs[:groups]
    kept, near = refs[groups:]
    blocks = own + halo
    total = arrived[0][...]
    for part in arrived[1:]:
        total = total + part[...]
    for d in range(spread.shape[0]):
        where = place[d * own : (d + 1) * own, :]
        hits = [where == k + 1 for k in range(halo)] if d else []
        out = near if d % 2 else kept
        for r in range(rows):
            span = slice(r * own, (r + 1) * own)
            field = spread[d, span, :]
            if d == 0:
                field = field + total[r * blocks : r * blocks + own, :]
            for k, hit in enumerate(hits):
                row = r * blocks + own + k
                field = field + jnp.where(hit, total[row : row + 1, :], 0.0)
            out[d // 2, span, :] = field


def add_kernel(kept, arrived, *outs):
    for e, out in enumerate(outs):
        out[...] = kept[e] + arrived[e]


def last_kernel(own, rows, *refs):
    *arrived, out, total = refs
    summed = arrived[0][...]
    for part in arrived[1:]:
        summed = summed + part[...]
    total[...] = summed
    for b in range(own):
        out[:, b * BLK : (b + 1) * BLK] = total[pl.ds(b, rows, stride=own), :]


def swap(value, axis, distance):
    count = lax.axis_size(axis)
    return lax.ppermute(value, axis, [(i, i ^ distance) for i in range(count)])


def exchange(parts, axis, unit=1):
    there = [swap(parts[d], axis, d * unit) for d in range(len(parts) - 1, 0, -1)]
    return [parts[0]] + there[::-1]


def on_device(residual, margin, aggregate, local_factor, coarse_factor):
    pairs = lax.axis_size("sub") // 2
    grp_count = lax.axis_size("grp")
    rhs, own_width = residual.shape
    own = own_width // BLK
    rows = rhs // grp_count
    halo = margin.shape[1]
    pad = 8
    begin = 2 * own * rows + pad
    f32 = jnp.float32
    sds = jax.ShapeDtypeStruct
    _, depth, width = local_factor.shape
    coarse_depth, coarse_width = coarse_factor.shape
    blocks = width // BLK
    in_hbm = functools.partial(pltpu.with_memory_space_constraint, memory_space=pltpu.HBM)
    aggregate = aggregate.reshape(1, own)
    local_factor = in_hbm(local_factor)
    coarse_factor = in_hbm(coarse_factor)

    near = swap(residual, "sub", 1)
    near_names = swap(aggregate, "sub", 1)
    held, mine, names = call(
        functools.partial(stage_kernel, own, rows),
        (sds(residual.shape, f32), sds((own * rows, BLK), f32), sds((1, own), f32)),
        [HBM, HBM],
        [
            pltpu.VMEM((own * rhs, BLK), f32),
            pltpu.VMEM((1, own), jnp.int32),
            pltpu.SemaphoreType.DMA((2,)),
        ],
        moved=8 * rhs * own_width,
    )(in_hbm(residual), in_hbm(aggregate))
    margin = in_hbm(margin)
    *outgoing, away, place = call(
        functools.partial(pack_kernel, own, rows, pad),
        [sds((begin + halo * rhs, BLK), f32)] * pairs
        + [sds((halo, BLK), jnp.int32), sds((2 * pairs * own, BLK), jnp.int32)],
        [HBM] + [VMEM] * 5,
        [
            pltpu.VMEM((own * rhs, BLK), f32),
            pltpu.SMEM(margin.shape, jnp.int32),
            pltpu.SemaphoreType.DMA,
        ],
    )(margin, held, mine, names, near_names, near)
    arrived = exchange(outgoing, "sub", 2)
    quarter = coarse_depth // 4
    tile = min(512, depth // 2)
    chunk = depth // 8
    begun, local_factor, coarse_upper = call(
        functools.partial(load_kernel, chunk, tile),
        (
            sds((rhs, depth), f32),
            sds(local_factor.shape, local_factor.dtype),
            sds((quarter, coarse_width), coarse_factor.dtype),
        ),
        [VMEM, HBM, HBM, pl.BlockSpec(memory_space=pl.ANY)],
        [
            pltpu.SemaphoreType.DMA((depth // chunk,)),
            pltpu.SemaphoreType.DMA((4,)),
        ],
        flops=2 * rhs * depth * own_width,
        moved=2 * depth * width + 2 * quarter * coarse_width,
    )(held, local_factor, coarse_factor, arrived[0])
    chunk = quarter // 4
    count = coarse_width // BLK
    *fine, coarse_middle, member, sums = call(
        functools.partial(fine_kernel, own, rows, begin, chunk, tile, pairs),
        [sds((rows * blocks, BLK), f32)] * grp_count
        + [
            sds((quarter, coarse_width), coarse_factor.dtype),
            sds((2 * pairs * own, count), f32),
            sds((rows * count, BLK), f32),
        ],
        [VMEM, VMEM, VMEM, HBM] + [VMEM] * pairs,
        [pltpu.VMEM((rhs * blocks, BLK), f32), pltpu.SemaphoreType.DMA((quarter // chunk,))],
        flops=4 * rhs * depth * width,
        moved=2 * depth * width + 2 * quarter * coarse_width,
    )(away, begun, local_factor, coarse_factor, *arrived[::-1])
    panels = exchange(fine, "grp")
    lower = coarse_depth - 2 * quarter
    size = own * rows
    spread = call(
        functools.partial(coarse_kernel, own, rows, chunk, tile),
        sds((2 * pairs, size, BLK), f32),
        [VMEM, VMEM, HBM, VMEM, VMEM],
        [
            pltpu.VMEM((rows * count, BLK), f32),
            pltpu.VMEM((lower, coarse_width), coarse_factor.dtype),
            pltpu.SemaphoreType.DMA((lower // chunk,)),
        ],
        flops=4 * rows * coarse_depth * coarse_width,
        moved=2 * coarse_depth * coarse_width,
        limit=24 * MIB,
    )(coarse_upper, coarse_middle, coarse_factor, member, sums)
    field = sds((pairs, size, BLK), f32)
    kept, crossing = call(
        functools.partial(merge_kernel, own, rows, grp_count, halo),
        [field, field],
        [VMEM] * (2 + grp_count),
    )(place, spread, *panels)
    back = call(add_kernel, [sds((size, BLK), f32)] * pairs, [VMEM, VMEM])(
        kept, swap(crossing, "sub", 1)
    )
    return call(
        functools.partial(last_kernel, own, rows),
        sds((rows, own_width), f32),
        [VMEM] * pairs,
        [pltpu.VMEM((size, BLK), f32)],
    )(*exchange(list(back), "sub", 2)[::-1])


def solution(mesh):
    placed = (P(None, "sub"), P(), P("sub"), P("sub", "grp", None), P("sub", None))
    return jax.shard_map(
        on_device, mesh=mesh, in_specs=placed, out_specs=P("grp", "sub"), check_vma=False
    )
```

```python
import functools

import jax
import jax.numpy as jnp
from jax import lax
from jax.experimental import pallas as pl
from jax.experimental.pallas import tpu as pltpu
from jax.sharding import PartitionSpec as P

BLK = 128
MIB = 1024 * 1024
VMEM = pl.BlockSpec(memory_space=pltpu.VMEM)
SMEM = pl.BlockSpec(memory_space=pltpu.SMEM)
HBM = pl.BlockSpec(memory_space=pltpu.HBM)
NT = (((1,), (1,)), ((), ()))
TN = (((0,), (0,)), ((), ()))


def call(kernel, out, specs, scratch=(), limit=12 * MIB, flops=0, moved=0, **options):
    return pl.pallas_call(
        kernel,
        out_shape=out,
        in_specs=specs,
        out_specs=jax.tree.map(lambda _: VMEM, out),
        scratch_shapes=scratch,
        compiler_params=pltpu.CompilerParams(vmem_limit_bytes=limit),
        cost_estimate=pl.CostEstimate(flops=flops, bytes_accessed=moved, transcendentals=0),
        **options,
    )


def mm(left, right, dims=(((1,), (0,)), ((), ()))):
    return lax.dot_general(left, right, dims, preferred_element_type=jnp.float32)


def split3(value):
    high = value.astype(jnp.bfloat16)
    rest = value - high.astype(jnp.float32)
    middle = rest.astype(jnp.bfloat16)
    low = (rest - middle.astype(jnp.float32)).astype(jnp.bfloat16)
    return [high, middle, low]


def stage_kernel(own, rows, residual_hbm, aggregate_hbm, residual, mine, names, block_rows, aggregate, sems):
    pairs = ((residual_hbm, residual), (aggregate_hbm, aggregate))
    copies = [pltpu.make_async_copy(a, b, sems.at[i]) for i, (a, b) in enumerate(pairs)]
    start(copies)
    for copy in copies:
        copy.wait()
    names[...] = aggregate[...].astype(jnp.float32)
    mine[...] = rows_of(residual, own, rows, block_rows)


def rows_of(residual, own, rows, block_rows):
    rhs = residual.shape[0]
    for b in range(own):
        block_rows[pl.ds(b, rhs, stride=own), :] = residual[:, b * BLK : (b + 1) * BLK]
    first = lax.axis_index("grp") * rows * own
    return block_rows[pl.ds(pl.multiple_of(first, 8), rows * own), :]


def pack_kernel(own, rows, pad, margin_hbm, residual, mine, names, near_names, near, *refs):
    *outs, away, place, block_rows, margin, sem = refs
    copy = pltpu.make_async_copy(margin_hbm, margin, sem)
    copy.start()
    halo = margin.shape[1]
    rhs = residual.shape[0]
    me = lax.axis_index("sub")
    size = own * rows
    both = [mine[...], rows_of(near, own, rows, block_rows)]
    labels = [names[...], near_names[...].astype(jnp.float32)]
    at = 2 * size
    for out in outs:
        out[at : at + pad, :] = jnp.zeros((pad, BLK), jnp.float32)
        for i in range(2):
            out[i * size : (i + 1) * size, :] = both[i]
            out[at + i : at + i + 1, :own] = labels[i]
    place[...] = jnp.zeros(place.shape, jnp.int32)
    copy.wait()
    for k in range(halo):
        block = margin[me, k]
        owner = block // own
        distance = me ^ owner
        away[k : k + 1, :] = jnp.full((1, BLK), distance // 2, jnp.int32)
        row = distance * own + block - owner * own
        place[pl.ds(row, 1), :] = jnp.full((1, BLK), k + 1, jnp.int32)
    for e, out in enumerate(outs):
        target = me ^ (2 * e)
        for k in range(halo):
            block = margin[target, k]
            owner = block // own
            where = pl.ds(pl.multiple_of((block - owner * own) * BLK, BLK), BLK)
            out[at + pad + k * rhs : at + pad + (k + 1) * rhs, :] = jnp.where(
                owner == me, residual[:, where], near[:, where]
            )


def panel_copies(source, target, chunk, sems, first=0):
    copies = []
    for n in range(target.shape[0] // chunk):
        span = pl.ds(first + n * chunk, chunk)
        copies.append(
            pltpu.make_async_copy(source.at[span], target.at[pl.ds(n * chunk, chunk)], sems.at[n])
        )
    return copies


def start(copies):
    for copy in copies:
        copy.start()


def first_product(factor, right, tile):
    tile = min(tile, factor.shape[0])
    parts = [
        mm(right, factor[n * tile : (n + 1) * tile, :], NT) for n in range(factor.shape[0] // tile)
    ]
    return jnp.concatenate(parts, axis=1)


def in_own_block(body):
    pl.when(lax.axis_index("sub") >= 0)(body)


def load_kernel(
    chunk, tile, residual, fine_hbm, coarse_hbm, after, inner, fine, coarse, sems, more
):
    depth = fine.shape[1]
    own_width = residual.shape[1]
    half = depth // 2
    each = half // chunk
    start(panel_copies(fine_hbm.at[0], fine.at[0], chunk, sems))
    late = panel_copies(coarse_hbm, coarse, coarse.shape[0] // 4, more)

    def step(n, carry):
        for i in range(each):
            span = pl.ds(pl.multiple_of(n * half + i * chunk, chunk), chunk)
            pltpu.make_async_copy(fine_hbm.at[0, span], fine.at[0, span], sems.at[n * each + i]).wait()
        pl.when(n == 0)(lambda: start(late))
        local = residual[...].astype(jnp.bfloat16)
        for i in range(half // tile):
            at = pl.multiple_of(n * half + i * tile, tile)
            rows = fine[0, pl.ds(at, tile), pl.ds(0, own_width)]
            inner[:, pl.ds(at, tile)] = mm(local, rows, NT)
        return carry

    lax.fori_loop(0, 2, step, 0)
    for copy in late:
        copy.wait()


def form_sums(own, rows, coarse, arrived, named, table):
    size = own * rows
    sources = 2 * len(arrived)
    parts = [(part, i) for part in arrived for i in range(2)]
    names = jnp.concatenate(
        [part[2 * size + i : 2 * size + i + 1, :] for part, i in parts], axis=0
    ).T
    catalog = lax.broadcasted_iota(jnp.int32, (own, coarse), 1).astype(jnp.float32)
    member = jnp.concatenate(
        [(names[:own, s : s + 1] == catalog).astype(jnp.float32) for s in range(sources)], axis=0
    ).astype(jnp.bfloat16)
    whole = jnp.concatenate(
        [
            jnp.concatenate(
                [part[i * size + r * own : i * size + (r + 1) * own, :] for part, i in parts],
                axis=0,
            )
            for r in range(rows)
        ],
        axis=1,
    )
    ones = jnp.ones((own * sources, BLK), jnp.bfloat16)
    span = rows * BLK
    found = mm(member, jnp.concatenate(split3(whole) + [ones], axis=1), TN)
    sums = found[:, :span] + found[:, span : 2 * span] + found[:, 2 * span : 3 * span]
    counts = jnp.maximum(found[:, 3 * span :], 1.0)
    for r in range(rows):
        table[r * coarse : (r + 1) * coarse, :] = sums[:, r * BLK : (r + 1) * BLK] / counts
    rest = table.shape[0] - rows * coarse
    if rest > 0:
        table[rows * coarse :, :] = jnp.zeros((rest, BLK), jnp.float32)
    named[...] = member.astype(jnp.float32)


def fine_kernel(own, rows, begin, chunk, tile, pairs, away, begun, factor, coarse_hbm, *refs):
    arrived = refs[:pairs][::-1]
    *outs, coarse, named, sums, table, sems = refs[pairs:]
    done = coarse_hbm.shape[0] // 4
    copies = panel_copies(coarse_hbm, coarse, chunk, sems, done)
    start(copies)
    rhs = begun.shape[0]
    halo = away.shape[0]
    depth, width = factor.shape[1:]
    blocks = width // BLK
    group = lax.axis_index("grp")
    tiles = []
    for k in range(halo):
        span = slice(begin + k * rhs, begin + (k + 1) * rhs)
        distance = away[k : k + 1, :]
        part = arrived[0][span, :]
        for e in range(1, pairs):
            part = jnp.where(distance == e, arrived[e][span, :], part)
        tiles.append(part.astype(jnp.bfloat16))
    form_sums(own, rows, coarse.shape[1] // BLK, arrived, named, sums)
    local = jnp.concatenate(tiles, axis=1)
    far = factor.at[0, :, pl.ds(own * BLK, halo * BLK)]
    mid = (begun[...] + first_product(far, local, tile)).astype(jnp.bfloat16)
    for n in range(width // 256):
        part = mm(mid, factor[0, :, n * 256 : (n + 1) * 256])
        for i in range(256 // BLK):
            b = n * (256 // BLK) + i
            table[pl.ds(b, rhs, stride=blocks), :] = part[:, i * BLK : (i + 1) * BLK]
    size = rows * blocks
    for d, out in enumerate(outs):
        out[...] = table[pl.ds(pl.multiple_of((group ^ d) * size, 8), size), :]

    @in_own_block
    def _():
        for copy in copies:
            copy.wait()


def coarse_kernel(own, rows, chunk, tile, upper, middle, factor_hbm, member, sums, *refs):
    out, table, lower, begun, sems = refs
    done = upper.shape[0] + middle.shape[0]
    width = upper.shape[1]
    copies = panel_copies(factor_hbm, lower, chunk, sems, done)
    start(copies)
    coarse = width // BLK
    span = rows * BLK
    padded = table.shape[0] // coarse

    def right():
        parts = [sums[pl.ds(j, padded, stride=coarse), :] for j in range(coarse)]
        return jnp.concatenate(parts, axis=1).astype(jnp.bfloat16)

    first = right()
    begun[:, : upper.shape[0]] = first_product(upper, first, tile)
    begun[:, upper.shape[0] : done] = first_product(middle, first, tile)

    @in_own_block
    def _():
        for copy in copies:
            copy.wait()
        low = first_product(lower, right(), tile).astype(jnp.bfloat16)
        mid = begun[...].astype(jnp.bfloat16)
        high = mid[:, : upper.shape[0]]
        mid = mid[:, upper.shape[0] :]
        for n in range(width // 256):
            where = slice(n * 256, (n + 1) * 256)
            part = mm(high, upper[:, where]) + mm(mid, middle[:, where]) + mm(low, lower[:, where])
            for i in range(256 // BLK):
                j = n * (256 // BLK) + i
                table[pl.ds(j, padded, stride=coarse), :] = part[:, i * BLK : (i + 1) * BLK]
        solved = jnp.concatenate([table[r * coarse : (r + 1) * coarse, :] for r in range(rows)], axis=1)
        spread = mm(member[...].astype(jnp.bfloat16), jnp.concatenate(split3(solved), axis=1))
        spread = spread[:, :span] + spread[:, span : 2 * span] + spread[:, 2 * span :]
        for s in range(out.shape[0]):
            for r in range(rows):
                out[s, r * own : (r + 1) * own, :] = spread[
                    s * own : (s + 1) * own, r * BLK : (r + 1) * BLK
                ]


def merge_kernel(own, rows, groups, halo, place, spread, *refs):
    arrived = refs[:groups]
    kept, near = refs[groups:]
    blocks = own + halo
    total = arrived[0][...]
    for part in arrived[1:]:
        total = total + part[...]
    for d in range(spread.shape[0]):
        where = place[d * own : (d + 1) * own, :]
        hits = [where == k + 1 for k in range(halo)] if d else []
        out = near if d % 2 else kept
        for r in range(rows):
            span = slice(r * own, (r + 1) * own)
            field = spread[d, span, :]
            if d == 0:
                field = field + total[r * blocks : r * blocks + own, :]
            for k, hit in enumerate(hits):
                row = r * blocks + own + k
                field = field + jnp.where(hit, total[row : row + 1, :], 0.0)
            out[d // 2, span, :] = field


def add_kernel(kept, arrived, *outs):
    for e, out in enumerate(outs):
        out[...] = kept[e] + arrived[e]


def last_kernel(own, rows, *refs):
    *arrived, out, total = refs
    summed = arrived[0][...]
    for part in arrived[1:]:
        summed = summed + part[...]
    total[...] = summed
    for b in range(own):
        out[:, b * BLK : (b + 1) * BLK] = total[pl.ds(b, rows, stride=own), :]


def swap(value, axis, distance):
    count = lax.axis_size(axis)
    return lax.ppermute(value, axis, [(i, i ^ distance) for i in range(count)])


def exchange(parts, axis, unit=1):
    there = [swap(parts[d], axis, d * unit) for d in range(len(parts) - 1, 0, -1)]
    return [parts[0]] + there[::-1]


def on_device(residual, margin, aggregate, local_factor, coarse_factor):
    pairs = lax.axis_size("sub") // 2
    grp_count = lax.axis_size("grp")
    rhs, own_width = residual.shape
    own = own_width // BLK
    rows = rhs // grp_count
    halo = margin.shape[1]
    pad = 8
    begin = 2 * own * rows + pad
    f32 = jnp.float32
    sds = jax.ShapeDtypeStruct
    _, depth, width = local_factor.shape
    coarse_depth, coarse_width = coarse_factor.shape
    blocks = width // BLK
    in_hbm = functools.partial(pltpu.with_memory_space_constraint, memory_space=pltpu.HBM)
    aggregate = aggregate.reshape(1, own)
    local_factor = in_hbm(local_factor)
    coarse_factor = in_hbm(coarse_factor)

    near = swap(residual, "sub", 1)
    near_names = swap(aggregate, "sub", 1)
    held, mine, names = call(
        functools.partial(stage_kernel, own, rows),
        (sds(residual.shape, f32), sds((own * rows, BLK), f32), sds((1, own), f32)),
        [HBM, HBM],
        [
            pltpu.VMEM((own * rhs, BLK), f32),
            pltpu.VMEM((1, own), jnp.int32),
            pltpu.SemaphoreType.DMA((2,)),
        ],
        moved=8 * rhs * own_width,
    )(in_hbm(residual), in_hbm(aggregate))
    margin = in_hbm(margin)
    *outgoing, away, place = call(
        functools.partial(pack_kernel, own, rows, pad),
        [sds((begin + halo * rhs, BLK), f32)] * pairs
        + [sds((halo, BLK), jnp.int32), sds((2 * pairs * own, BLK), jnp.int32)],
        [HBM] + [VMEM] * 5,
        [
            pltpu.VMEM((own * rhs, BLK), f32),
            pltpu.SMEM(margin.shape, jnp.int32),
            pltpu.SemaphoreType.DMA,
        ],
    )(margin, held, mine, names, near_names, near)
    arrived = exchange(outgoing, "sub", 2)
    quarter = coarse_depth // 4
    tile = min(512, depth // 2)
    chunk = depth // 8
    begun, local_factor, coarse_upper = call(
        functools.partial(load_kernel, chunk, tile),
        (
            sds((rhs, depth), f32),
            sds(local_factor.shape, local_factor.dtype),
            sds((quarter, coarse_width), coarse_factor.dtype),
        ),
        [VMEM, HBM, HBM, pl.BlockSpec(memory_space=pl.ANY)],
        [
            pltpu.SemaphoreType.DMA((depth // chunk,)),
            pltpu.SemaphoreType.DMA((4,)),
        ],
        flops=2 * rhs * depth * own_width,
        moved=2 * depth * width + 2 * quarter * coarse_width,
    )(held, local_factor, coarse_factor, arrived[0])
    chunk = quarter // 4
    count = coarse_width // BLK
    padded = -(-rows // 8) * 8
    *fine, coarse_middle, member, sums = call(
        functools.partial(fine_kernel, own, rows, begin, chunk, tile, pairs),
        [sds((rows * blocks, BLK), f32)] * grp_count
        + [
            sds((quarter, coarse_width), coarse_factor.dtype),
            sds((2 * pairs * own, count), f32),
            sds((padded * count, BLK), f32),
        ],
        [VMEM, VMEM, VMEM, HBM] + [VMEM] * pairs,
        [pltpu.VMEM((rhs * blocks, BLK), f32), pltpu.SemaphoreType.DMA((quarter // chunk,))],
        flops=4 * rhs * depth * width,
        moved=2 * depth * width + 2 * quarter * coarse_width,
    )(away, begun, local_factor, coarse_factor, *arrived[::-1])
    panels = exchange(fine, "grp")
    lower = coarse_depth - 2 * quarter
    size = own * rows
    spread = call(
        functools.partial(coarse_kernel, own, rows, chunk, tile),
        sds((2 * pairs, size, BLK), f32),
        [VMEM, VMEM, HBM, VMEM, VMEM],
        [
            pltpu.VMEM((padded * count, BLK), f32),
            pltpu.VMEM((lower, coarse_width), coarse_factor.dtype),
            pltpu.VMEM((padded, 2 * quarter), f32),
            pltpu.SemaphoreType.DMA((lower // chunk,)),
        ],
        flops=4 * rows * coarse_depth * coarse_width,
        moved=2 * coarse_depth * coarse_width,
        limit=24 * MIB,
    )(coarse_upper, coarse_middle, coarse_factor, member, sums)
    field = sds((pairs, size, BLK), f32)
    kept, crossing = call(
        functools.partial(merge_kernel, own, rows, grp_count, halo),
        [field, field],
        [VMEM] * (2 + grp_count),
    )(place, spread, *panels)
    back = call(add_kernel, [sds((size, BLK), f32)] * pairs, [VMEM, VMEM])(
        kept, swap(crossing, "sub", 1)
    )
    return call(
        functools.partial(last_kernel, own, rows),
        sds((rows, own_width), f32),
        [VMEM] * pairs,
        [pltpu.VMEM((size, BLK), f32)],
    )(*exchange(list(back), "sub", 2)[::-1])


def solution(mesh):
    placed = (P(None, "sub"), P(), P("sub"), P("sub", "grp", None), P("sub", None))
    return jax.shard_map(
        on_device, mesh=mesh, in_specs=placed, out_specs=P("grp", "sub"), check_vma=False
    )
```

```python
import functools

import jax
import jax.numpy as jnp
from jax import lax
from jax.experimental import pallas as pl
from jax.experimental.pallas import tpu as pltpu
from jax.sharding import PartitionSpec as P

BLK = 128
MIB = 1024 * 1024
VMEM = pl.BlockSpec(memory_space=pltpu.VMEM)
SMEM = pl.BlockSpec(memory_space=pltpu.SMEM)
HBM = pl.BlockSpec(memory_space=pltpu.HBM)
NT = (((1,), (1,)), ((), ()))
TN = (((0,), (0,)), ((), ()))


def call(kernel, out, specs, scratch=(), limit=12 * MIB, flops=0, moved=0, **options):
    return pl.pallas_call(
        kernel,
        out_shape=out,
        in_specs=specs,
        out_specs=jax.tree.map(lambda _: VMEM, out),
        scratch_shapes=scratch,
        compiler_params=pltpu.CompilerParams(vmem_limit_bytes=limit),
        cost_estimate=pl.CostEstimate(flops=flops, bytes_accessed=moved, transcendentals=0),
        **options,
    )


def mm(left, right, dims=(((1,), (0,)), ((), ()))):
    return lax.dot_general(left, right, dims, preferred_element_type=jnp.float32)


def split3(value):
    high = value.astype(jnp.bfloat16)
    rest = value - high.astype(jnp.float32)
    middle = rest.astype(jnp.bfloat16)
    low = (rest - middle.astype(jnp.float32)).astype(jnp.bfloat16)
    return [high, middle, low]


def stage_kernel(
    own, rows, residual_hbm, aggregate_hbm, coarse_hbm, residual, mine, names, panel, block_rows, aggregate, sems
):
    pairs = ((residual_hbm, residual), (aggregate_hbm, aggregate))
    copies = [pltpu.make_async_copy(a, b, sems.at[i]) for i, (a, b) in enumerate(pairs)]
    start(copies)
    late = panel_copies(coarse_hbm, panel, panel.shape[0], sems.at[pl.ds(len(copies), 1)])
    start(late)
    for copy in copies:
        copy.wait()
    names[...] = aggregate[...].astype(jnp.float32)
    mine[...] = rows_of(residual, own, rows, block_rows)
    in_own_block(late[0].wait)


def rows_of(residual, own, rows, block_rows):
    rhs = residual.shape[0]
    for b in range(own):
        block_rows[pl.ds(b, rhs, stride=own), :] = residual[:, b * BLK : (b + 1) * BLK]
    first = lax.axis_index("grp") * rows * own
    return block_rows[pl.ds(pl.multiple_of(first, 8), rows * own), :]


def pack_kernel(own, rows, pad, margin_hbm, coarse_hbm, residual, mine, names, near_names, near, *refs):
    *outs, away, place, panel, block_rows, margin, sem, sems = refs
    copy = pltpu.make_async_copy(margin_hbm, margin, sem)
    copy.start()
    late = panel_copies(coarse_hbm, panel, panel.shape[0], sems, panel.shape[0])
    start(late)
    halo = margin.shape[1]
    rhs = residual.shape[0]
    me = lax.axis_index("sub")
    size = own * rows
    both = [mine[...], rows_of(near, own, rows, block_rows)]
    labels = [names[...], near_names[...].astype(jnp.float32)]
    at = 2 * size
    for out in outs:
        out[at : at + pad, :] = jnp.zeros((pad, BLK), jnp.float32)
        for i in range(2):
            out[i * size : (i + 1) * size, :] = both[i]
            out[at + i : at + i + 1, :own] = labels[i]
    place[...] = jnp.zeros(place.shape, jnp.int32)
    copy.wait()
    for k in range(halo):
        block = margin[me, k]
        owner = block // own
        distance = me ^ owner
        away[k : k + 1, :] = jnp.full((1, BLK), distance // 2, jnp.int32)
        row = distance * own + block - owner * own
        place[pl.ds(row, 1), :] = jnp.full((1, BLK), k + 1, jnp.int32)
    for e, out in enumerate(outs):
        target = me ^ (2 * e)
        for k in range(halo):
            block = margin[target, k]
            owner = block // own
            where = pl.ds(pl.multiple_of((block - owner * own) * BLK, BLK), BLK)
            out[at + pad + k * rhs : at + pad + (k + 1) * rhs, :] = jnp.where(
                owner == me, residual[:, where], near[:, where]
            )
    in_own_block(late[0].wait)


def panel_copies(source, target, chunk, sems, first=0):
    copies = []
    for n in range(target.shape[0] // chunk):
        span = pl.ds(first + n * chunk, chunk)
        copies.append(
            pltpu.make_async_copy(source.at[span], target.at[pl.ds(n * chunk, chunk)], sems.at[n])
        )
    return copies


def start(copies):
    for copy in copies:
        copy.start()


def first_product(factor, right, tile):
    tile = min(tile, factor.shape[0])
    parts = [
        mm(right, factor[n * tile : (n + 1) * tile, :], NT) for n in range(factor.shape[0] // tile)
    ]
    return jnp.concatenate(parts, axis=1)


def in_own_block(body):
    pl.when(lax.axis_index("sub") >= 0)(body)


def load_kernel(
    chunk, tile, residual, fine_hbm, coarse_hbm, after, inner, fine, coarse, sems, more
):
    depth = fine.shape[1]
    own_width = residual.shape[1]
    half = depth // 2
    each = half // chunk
    start(panel_copies(fine_hbm.at[0], fine.at[0], chunk, sems))
    late = panel_copies(coarse_hbm, coarse, coarse.shape[0] // 4, more, coarse_hbm.shape[0] // 8)

    def step(n, carry):
        for i in range(each):
            span = pl.ds(pl.multiple_of(n * half + i * chunk, chunk), chunk)
            pltpu.make_async_copy(fine_hbm.at[0, span], fine.at[0, span], sems.at[n * each + i]).wait()
        pl.when(n == 0)(lambda: start(late))
        local = residual[...].astype(jnp.bfloat16)
        for i in range(half // tile):
            at = pl.multiple_of(n * half + i * tile, tile)
            rows = fine[0, pl.ds(at, tile), pl.ds(0, own_width)]
            inner[:, pl.ds(at, tile)] = mm(local, rows, NT)
        return carry

    lax.fori_loop(0, 2, step, 0)
    for copy in late:
        copy.wait()


def form_sums(own, rows, coarse, arrived, named, table):
    size = own * rows
    sources = 2 * len(arrived)
    parts = [(part, i) for part in arrived for i in range(2)]
    names = jnp.concatenate(
        [part[2 * size + i : 2 * size + i + 1, :] for part, i in parts], axis=0
    ).T
    catalog = lax.broadcasted_iota(jnp.int32, (own, coarse), 1).astype(jnp.float32)
    member = jnp.concatenate(
        [(names[:own, s : s + 1] == catalog).astype(jnp.float32) for s in range(sources)], axis=0
    ).astype(jnp.bfloat16)
    whole = jnp.concatenate(
        [
            jnp.concatenate(
                [part[i * size + r * own : i * size + (r + 1) * own, :] for part, i in parts],
                axis=0,
            )
            for r in range(rows)
        ],
        axis=1,
    )
    ones = jnp.ones((own * sources, BLK), jnp.bfloat16)
    span = rows * BLK
    found = mm(member, jnp.concatenate(split3(whole) + [ones], axis=1), TN)
    sums = found[:, :span] + found[:, span : 2 * span] + found[:, 2 * span : 3 * span]
    counts = jnp.maximum(found[:, 3 * span :], 1.0)
    for r in range(rows):
        table[r * coarse : (r + 1) * coarse, :] = sums[:, r * BLK : (r + 1) * BLK] / counts
    named[...] = member.astype(jnp.float32)


def fine_kernel(own, rows, begin, chunk, tile, pairs, away, begun, factor, coarse_hbm, *refs):
    arrived = refs[:pairs][::-1]
    *outs, coarse, named, sums, table, sems = refs[pairs:]
    done = coarse_hbm.shape[0] // 8 + coarse.shape[0]
    copies = panel_copies(coarse_hbm, coarse, chunk, sems, done)
    start(copies)
    rhs = begun.shape[0]
    halo = away.shape[0]
    depth, width = factor.shape[1:]
    blocks = width // BLK
    group = lax.axis_index("grp")
    tiles = []
    for k in range(halo):
        span = slice(begin + k * rhs, begin + (k + 1) * rhs)
        distance = away[k : k + 1, :]
        part = arrived[0][span, :]
        for e in range(1, pairs):
            part = jnp.where(distance == e, arrived[e][span, :], part)
        tiles.append(part.astype(jnp.bfloat16))
    form_sums(own, rows, coarse.shape[1] // BLK, arrived, named, sums)
    local = jnp.concatenate(tiles, axis=1)
    far = factor.at[0, :, pl.ds(own * BLK, halo * BLK)]
    mid = (begun[...] + first_product(far, local, tile)).astype(jnp.bfloat16)
    for n in range(width // 256):
        part = mm(mid, factor[0, :, n * 256 : (n + 1) * 256])
        for i in range(256 // BLK):
            b = n * (256 // BLK) + i
            table[pl.ds(b, rhs, stride=blocks), :] = part[:, i * BLK : (i + 1) * BLK]
    size = rows * blocks
    for d, out in enumerate(outs):
        out[...] = table[pl.ds(pl.multiple_of((group ^ d) * size, 8), size), :]

    @in_own_block
    def _():
        for copy in copies:
            copy.wait()


def coarse_kernel(own, rows, chunk, tile, held, factor_hbm, member, sums, *refs):
    panels = refs[:held]
    out, table, lower, begun, sems = refs[held:]
    done = sum(panel.shape[0] for panel in panels)
    width = lower.shape[1]
    copies = panel_copies(factor_hbm, lower, chunk, sems, done)
    start(copies)
    coarse = width // BLK
    span = rows * BLK

    def right():
        parts = [sums[pl.ds(j, rows, stride=coarse), :] for j in range(coarse)]
        return jnp.concatenate(parts, axis=1).astype(jnp.bfloat16)

    first = right()
    spans = []
    at = 0
    for panel in panels:
        spans.append(slice(at, at + panel.shape[0]))
        begun[:, spans[-1]] = first_product(panel, first, tile)
        at += panel.shape[0]

    @in_own_block
    def _():
        for copy in copies:
            copy.wait()
        low = first_product(lower, right(), tile).astype(jnp.bfloat16)
        mid = begun[...].astype(jnp.bfloat16)
        mids = [mid[:, part] for part in spans]
        for n in range(width // 256):
            where = slice(n * 256, (n + 1) * 256)
            part = mm(low, lower[:, where])
            for mid, panel in zip(mids, panels):
                part = part + mm(mid, panel[:, where])
            for i in range(256 // BLK):
                j = n * (256 // BLK) + i
                table[pl.ds(j, rows, stride=coarse), :] = part[:, i * BLK : (i + 1) * BLK]
        solved = jnp.concatenate([table[r * coarse : (r + 1) * coarse, :] for r in range(rows)], axis=1)
        spread = mm(member[...].astype(jnp.bfloat16), jnp.concatenate(split3(solved), axis=1))
        spread = spread[:, :span] + spread[:, span : 2 * span] + spread[:, 2 * span :]
        for s in range(out.shape[0]):
            for r in range(rows):
                out[s, r * own : (r + 1) * own, :] = spread[
                    s * own : (s + 1) * own, r * BLK : (r + 1) * BLK
                ]


def merge_kernel(own, rows, groups, halo, place, spread, *refs):
    arrived = refs[:groups]
    kept, near = refs[groups:]
    blocks = own + halo
    total = arrived[0][...]
    for part in arrived[1:]:
        total = total + part[...]
    for d in range(spread.shape[0]):
        where = place[d * own : (d + 1) * own, :]
        hits = [where == k + 1 for k in range(halo)] if d else []
        out = near if d % 2 else kept
        for r in range(rows):
            span = slice(r * own, (r + 1) * own)
            field = spread[d, span, :]
            if d == 0:
                field = field + total[r * blocks : r * blocks + own, :]
            for k, hit in enumerate(hits):
                row = r * blocks + own + k
                field = field + jnp.where(hit, total[row : row + 1, :], 0.0)
            out[d // 2, span, :] = field


def add_kernel(kept, arrived, *outs):
    for e, out in enumerate(outs):
        out[...] = kept[e] + arrived[e]


def last_kernel(own, rows, *refs):
    *arrived, out, total = refs
    summed = arrived[0][...]
    for part in arrived[1:]:
        summed = summed + part[...]
    total[...] = summed
    for b in range(own):
        out[:, b * BLK : (b + 1) * BLK] = total[pl.ds(b, rows, stride=own), :]


def swap(value, axis, distance):
    count = lax.axis_size(axis)
    return lax.ppermute(value, axis, [(i, i ^ distance) for i in range(count)])


def exchange(parts, axis, unit=1):
    there = [swap(parts[d], axis, d * unit) for d in range(len(parts) - 1, 0, -1)]
    return [parts[0]] + there[::-1]


def on_device(residual, margin, aggregate, local_factor, coarse_factor):
    pairs = lax.axis_size("sub") // 2
    grp_count = lax.axis_size("grp")
    rhs, own_width = residual.shape
    own = own_width // BLK
    rows = rhs // grp_count
    halo = margin.shape[1]
    pad = 8
    begin = 2 * own * rows + pad
    f32 = jnp.float32
    sds = jax.ShapeDtypeStruct
    _, depth, width = local_factor.shape
    coarse_depth, coarse_width = coarse_factor.shape
    blocks = width // BLK
    in_hbm = functools.partial(pltpu.with_memory_space_constraint, memory_space=pltpu.HBM)
    aggregate = aggregate.reshape(1, own)
    local_factor = in_hbm(local_factor)
    coarse_factor = in_hbm(coarse_factor)

    near = swap(residual, "sub", 1)
    near_names = swap(aggregate, "sub", 1)
    piece = sds((coarse_depth // 16, coarse_width), coarse_factor.dtype)
    held, mine, names, first_piece = call(
        functools.partial(stage_kernel, own, rows),
        (sds(residual.shape, f32), sds((own * rows, BLK), f32), sds((1, own), f32), piece),
        [HBM, HBM, HBM],
        [
            pltpu.VMEM((own * rhs, BLK), f32),
            pltpu.VMEM((1, own), jnp.int32),
            pltpu.SemaphoreType.DMA((3,)),
        ],
        moved=8 * rhs * own_width,
    )(in_hbm(residual), in_hbm(aggregate), coarse_factor)
    margin = in_hbm(margin)
    *outgoing, away, place, second_piece = call(
        functools.partial(pack_kernel, own, rows, pad),
        [sds((begin + halo * rhs, BLK), f32)] * pairs
        + [sds((halo, BLK), jnp.int32), sds((2 * pairs * own, BLK), jnp.int32), piece],
        [HBM, HBM] + [VMEM] * 5,
        [
            pltpu.VMEM((own * rhs, BLK), f32),
            pltpu.SMEM(margin.shape, jnp.int32),
            pltpu.SemaphoreType.DMA,
            pltpu.SemaphoreType.DMA((1,)),
        ],
    )(margin, coarse_factor, held, mine, names, near_names, near)
    arrived = exchange(outgoing, "sub", 2)
    quarter = coarse_depth // 4
    tile = min(512, depth // 2)
    chunk = depth // 8
    begun, local_factor, coarse_upper = call(
        functools.partial(load_kernel, chunk, tile),
        (
            sds((rhs, depth), f32),
            sds(local_factor.shape, local_factor.dtype),
            sds((quarter, coarse_width), coarse_factor.dtype),
        ),
        [VMEM, HBM, HBM, pl.BlockSpec(memory_space=pl.ANY)],
        [
            pltpu.SemaphoreType.DMA((depth // chunk,)),
            pltpu.SemaphoreType.DMA((4,)),
        ],
        flops=2 * rhs * depth * own_width,
        moved=2 * depth * width + 2 * quarter * coarse_width,
    )(held, local_factor, coarse_factor, arrived[0])
    chunk = quarter // 4
    count = coarse_width // BLK
    *fine, coarse_middle, member, sums = call(
        functools.partial(fine_kernel, own, rows, begin, chunk, tile, pairs),
        [sds((rows * blocks, BLK), f32)] * grp_count
        + [
            sds((quarter, coarse_width), coarse_factor.dtype),
            sds((2 * pairs * own, count), f32),
            sds((rows * count, BLK), f32),
        ],
        [VMEM, VMEM, VMEM, HBM] + [VMEM] * pairs,
        [pltpu.VMEM((rhs * blocks, BLK), f32), pltpu.SemaphoreType.DMA((quarter // chunk,))],
        flops=4 * rhs * depth * width,
        moved=2 * depth * width + 2 * quarter * coarse_width,
    )(away, begun, local_factor, coarse_factor, *arrived[::-1])
    panels = exchange(fine, "grp")
    panels_held = (first_piece, second_piece, coarse_upper, coarse_middle)
    done = sum(panel.shape[0] for panel in panels_held)
    lower = coarse_depth - done
    size = own * rows
    spread = call(
        functools.partial(coarse_kernel, own, rows, chunk, tile, len(panels_held)),
        sds((2 * pairs, size, BLK), f32),
        [HBM, VMEM, VMEM] + [VMEM] * len(panels_held),
        [
            pltpu.VMEM((rows * count, BLK), f32),
            pltpu.VMEM((lower, coarse_width), coarse_factor.dtype),
            pltpu.VMEM((rows, done), f32),
            pltpu.SemaphoreType.DMA((lower // chunk,)),
        ],
        flops=4 * rows * coarse_depth * coarse_width,
        moved=2 * coarse_depth * coarse_width,
        limit=24 * MIB,
    )(coarse_factor, member, sums, *panels_held)
    field = sds((pairs, size, BLK), f32)
    kept, crossing = call(
        functools.partial(merge_kernel, own, rows, grp_count, halo),
        [field, field],
        [VMEM] * (2 + grp_count),
    )(place, spread, *panels)
    back = call(add_kernel, [sds((size, BLK), f32)] * pairs, [VMEM, VMEM])(
        kept, swap(crossing, "sub", 1)
    )
    return call(
        functools.partial(last_kernel, own, rows),
        sds((rows, own_width), f32),
        [VMEM] * pairs,
        [pltpu.VMEM((size, BLK), f32)],
    )(*exchange(list(back), "sub", 2)[::-1])


def solution(mesh):
    placed = (P(None, "sub"), P(), P("sub"), P("sub", "grp", None), P("sub", None))
    return jax.shard_map(
        on_device, mesh=mesh, in_specs=placed, out_specs=P("grp", "sub"), check_vma=False
    )
```

```python
import functools

import jax
import jax.numpy as jnp
from jax import lax
from jax.experimental import pallas as pl
from jax.experimental.pallas import tpu as pltpu
from jax.sharding import PartitionSpec as P

BLK = 128
MIB = 1024 * 1024
VMEM = pl.BlockSpec(memory_space=pltpu.VMEM)
SMEM = pl.BlockSpec(memory_space=pltpu.SMEM)
HBM = pl.BlockSpec(memory_space=pltpu.HBM)
NT = (((1,), (1,)), ((), ()))
TN = (((0,), (0,)), ((), ()))


def call(kernel, out, specs, scratch=(), limit=12 * MIB, flops=0, moved=0, **options):
    return pl.pallas_call(
        kernel,
        out_shape=out,
        in_specs=specs,
        out_specs=jax.tree.map(lambda _: VMEM, out),
        scratch_shapes=scratch,
        compiler_params=pltpu.CompilerParams(vmem_limit_bytes=limit),
        cost_estimate=pl.CostEstimate(flops=flops, bytes_accessed=moved, transcendentals=0),
        **options,
    )


def mm(left, right, dims=(((1,), (0,)), ((), ()))):
    return lax.dot_general(left, right, dims, preferred_element_type=jnp.float32)


def split3(value):
    high = value.astype(jnp.bfloat16)
    rest = value - high.astype(jnp.float32)
    middle = rest.astype(jnp.bfloat16)
    low = (rest - middle.astype(jnp.float32)).astype(jnp.bfloat16)
    return [high, middle, low]


def stage_kernel(own, rows, residual_hbm, aggregate_hbm, residual, mine, names, block_rows, aggregate, sems):
    pairs = ((residual_hbm, residual), (aggregate_hbm, aggregate))
    copies = [pltpu.make_async_copy(a, b, sems.at[i]) for i, (a, b) in enumerate(pairs)]
    start(copies)
    for copy in copies:
        copy.wait()
    names[...] = aggregate[...].astype(jnp.float32)
    mine[...] = rows_of(residual, own, rows, block_rows)


def rows_of(residual, own, rows, block_rows):
    rhs = residual.shape[0]
    for b in range(own):
        block_rows[pl.ds(b, rhs, stride=own), :] = residual[:, b * BLK : (b + 1) * BLK]
    first = lax.axis_index("grp") * rows * own
    return block_rows[pl.ds(pl.multiple_of(first, 8), rows * own), :]


def pack_kernel(own, rows, pad, margin_hbm, residual, mine, names, near_names, near, *refs):
    *outs, away, place, block_rows, margin, sem = refs
    copy = pltpu.make_async_copy(margin_hbm, margin, sem)
    copy.start()
    halo = margin.shape[1]
    rhs = residual.shape[0]
    me = lax.axis_index("sub")
    size = own * rows
    both = [mine[...], rows_of(near, own, rows, block_rows)]
    labels = [names[...], near_names[...].astype(jnp.float32)]
    at = 2 * size
    for out in outs:
        out[at : at + pad, :] = jnp.zeros((pad, BLK), jnp.float32)
        for i in range(2):
            out[i * size : (i + 1) * size, :] = both[i]
            out[at + i : at + i + 1, :own] = labels[i]
    place[...] = jnp.zeros(place.shape, jnp.int32)
    copy.wait()
    for k in range(halo):
        block = margin[me, k]
        owner = block // own
        distance = me ^ owner
        away[k : k + 1, :] = jnp.full((1, BLK), distance // 2, jnp.int32)
        row = distance * own + block - owner * own
        place[pl.ds(row, 1), :] = jnp.full((1, BLK), k + 1, jnp.int32)
    for e, out in enumerate(outs):
        target = me ^ (2 * e)
        for k in range(halo):
            block = margin[target, k]
            owner = block // own
            where = pl.ds(pl.multiple_of((block - owner * own) * BLK, BLK), BLK)
            out[at + pad + k * rhs : at + pad + (k + 1) * rhs, :] = jnp.where(
                owner == me, residual[:, where], near[:, where]
            )


def panel_copies(source, target, chunk, sems, first=0):
    copies = []
    for n in range(target.shape[0] // chunk):
        span = pl.ds(first + n * chunk, chunk)
        copies.append(
            pltpu.make_async_copy(source.at[span], target.at[pl.ds(n * chunk, chunk)], sems.at[n])
        )
    return copies


def start(copies):
    for copy in copies:
        copy.start()


def first_product(factor, right, tile):
    tile = min(tile, factor.shape[0])
    parts = [
        mm(right, factor[n * tile : (n + 1) * tile, :], NT) for n in range(factor.shape[0] // tile)
    ]
    return jnp.concatenate(parts, axis=1)


def in_own_block(body):
    pl.when(lax.axis_index("sub") >= 0)(body)


def load_kernel(
    chunk, tile, residual, fine_hbm, coarse_hbm, after, inner, fine, coarse, sems, more
):
    depth = fine.shape[1]
    own_width = residual.shape[1]
    half = depth // 2
    each = half // chunk
    start(panel_copies(fine_hbm.at[0], fine.at[0], chunk, sems))
    quarter = coarse.shape[0] // 4
    late = panel_copies(coarse_hbm, coarse.at[pl.ds(0, quarter)], quarter // 4, more)

    def step(n, carry):
        for i in range(each):
            span = pl.ds(pl.multiple_of(n * half + i * chunk, chunk), chunk)
            pltpu.make_async_copy(fine_hbm.at[0, span], fine.at[0, span], sems.at[n * each + i]).wait()
        pl.when(n == 0)(lambda: start(late))
        local = residual[...].astype(jnp.bfloat16)
        for i in range(half // tile):
            at = pl.multiple_of(n * half + i * tile, tile)
            rows = fine[0, pl.ds(at, tile), pl.ds(0, own_width)]
            inner[:, pl.ds(at, tile)] = mm(local, rows, NT)
        return carry

    lax.fori_loop(0, 2, step, 0)
    for copy in late:
        copy.wait()


def form_sums(own, rows, coarse, arrived, named, table):
    size = own * rows
    sources = 2 * len(arrived)
    parts = [(part, i) for part in arrived for i in range(2)]
    names = jnp.concatenate(
        [part[2 * size + i : 2 * size + i + 1, :] for part, i in parts], axis=0
    ).T
    catalog = lax.broadcasted_iota(jnp.int32, (own, coarse), 1).astype(jnp.float32)
    member = jnp.concatenate(
        [(names[:own, s : s + 1] == catalog).astype(jnp.float32) for s in range(sources)], axis=0
    ).astype(jnp.bfloat16)
    whole = jnp.concatenate(
        [
            jnp.concatenate(
                [part[i * size + r * own : i * size + (r + 1) * own, :] for part, i in parts],
                axis=0,
            )
            for r in range(rows)
        ],
        axis=1,
    )
    ones = jnp.ones((own * sources, BLK), jnp.bfloat16)
    span = rows * BLK
    found = mm(member, jnp.concatenate(split3(whole) + [ones], axis=1), TN)
    sums = found[:, :span] + found[:, span : 2 * span] + found[:, 2 * span : 3 * span]
    counts = jnp.maximum(found[:, 3 * span :], 1.0)
    for r in range(rows):
        table[r * coarse : (r + 1) * coarse, :] = sums[:, r * BLK : (r + 1) * BLK] / counts
    named[...] = member.astype(jnp.float32)


def fine_kernel(own, rows, begin, chunk, tile, pairs, away, begun, factor, coarse_hbm, given, *refs):
    arrived = refs[:pairs][::-1]
    *outs, coarse, named, sums, table, sems = refs[pairs:]
    quarter = coarse.shape[0] // 4
    copies = panel_copies(coarse_hbm, coarse.at[pl.ds(quarter, quarter)], chunk, sems, quarter)
    start(copies)
    rhs = begun.shape[0]
    halo = away.shape[0]
    depth, width = factor.shape[1:]
    blocks = width // BLK
    group = lax.axis_index("grp")
    tiles = []
    for k in range(halo):
        span = slice(begin + k * rhs, begin + (k + 1) * rhs)
        distance = away[k : k + 1, :]
        part = arrived[0][span, :]
        for e in range(1, pairs):
            part = jnp.where(distance == e, arrived[e][span, :], part)
        tiles.append(part.astype(jnp.bfloat16))
    form_sums(own, rows, coarse.shape[1] // BLK, arrived, named, sums)
    local = jnp.concatenate(tiles, axis=1)
    far = factor.at[0, :, pl.ds(own * BLK, halo * BLK)]
    mid = (begun[...] + first_product(far, local, tile)).astype(jnp.bfloat16)
    for n in range(width // 256):
        part = mm(mid, factor[0, :, n * 256 : (n + 1) * 256])
        for i in range(256 // BLK):
            b = n * (256 // BLK) + i
            table[pl.ds(b, rhs, stride=blocks), :] = part[:, i * BLK : (i + 1) * BLK]
    size = rows * blocks
    for d, out in enumerate(outs):
        out[...] = table[pl.ds(pl.multiple_of((group ^ d) * size, 8), size), :]

    @in_own_block
    def _():
        for copy in copies:
            copy.wait()


def coarse_kernel(own, rows, chunk, tile, given, factor_hbm, member, sums, out, factor, table, begun, sems):
    depth, width = factor.shape
    done = depth // 2
    held, lower = factor.at[pl.ds(0, done)], factor.at[pl.ds(done, depth - done)]
    copies = panel_copies(factor_hbm, lower, chunk, sems, done)
    start(copies)
    coarse = width // BLK
    span = rows * BLK

    def right():
        parts = [sums[pl.ds(j, rows, stride=coarse), :] for j in range(coarse)]
        return jnp.concatenate(parts, axis=1).astype(jnp.bfloat16)

    first = right()
    begun[:, :done] = first_product(held, first, tile)

    @in_own_block
    def _():
        for copy in copies:
            copy.wait()
        begun[:, done:] = first_product(lower, right(), tile)
        mid = begun[...].astype(jnp.bfloat16)
        for n in range(width // 256):
            where = slice(n * 256, (n + 1) * 256)
            part = mm(mid, factor[:, where])
            for i in range(256 // BLK):
                j = n * (256 // BLK) + i
                table[pl.ds(j, rows, stride=coarse), :] = part[:, i * BLK : (i + 1) * BLK]
        solved = jnp.concatenate([table[r * coarse : (r + 1) * coarse, :] for r in range(rows)], axis=1)
        spread = mm(member[...].astype(jnp.bfloat16), jnp.concatenate(split3(solved), axis=1))
        spread = spread[:, :span] + spread[:, span : 2 * span] + spread[:, 2 * span :]
        for s in range(out.shape[0]):
            for r in range(rows):
                out[s, r * own : (r + 1) * own, :] = spread[
                    s * own : (s + 1) * own, r * BLK : (r + 1) * BLK
                ]


def merge_kernel(own, rows, groups, halo, place, spread, *refs):
    arrived = refs[:groups]
    kept, near = refs[groups:]
    blocks = own + halo
    total = arrived[0][...]
    for part in arrived[1:]:
        total = total + part[...]
    for d in range(spread.shape[0]):
        where = place[d * own : (d + 1) * own, :]
        hits = [where == k + 1 for k in range(halo)] if d else []
        out = near if d % 2 else kept
        for r in range(rows):
            span = slice(r * own, (r + 1) * own)
            field = spread[d, span, :]
            if d == 0:
                field = field + total[r * blocks : r * blocks + own, :]
            for k, hit in enumerate(hits):
                row = r * blocks + own + k
                field = field + jnp.where(hit, total[row : row + 1, :], 0.0)
            out[d // 2, span, :] = field


def add_kernel(kept, arrived, *outs):
    for e, out in enumerate(outs):
        out[...] = kept[e] + arrived[e]


def last_kernel(own, rows, *refs):
    *arrived, out, total = refs
    summed = arrived[0][...]
    for part in arrived[1:]:
        summed = summed + part[...]
    total[...] = summed
    for b in range(own):
        out[:, b * BLK : (b + 1) * BLK] = total[pl.ds(b, rows, stride=own), :]


def swap(value, axis, distance):
    count = lax.axis_size(axis)
    return lax.ppermute(value, axis, [(i, i ^ distance) for i in range(count)])


def exchange(parts, axis, unit=1):
    there = [swap(parts[d], axis, d * unit) for d in range(len(parts) - 1, 0, -1)]
    return [parts[0]] + there[::-1]


def on_device(residual, margin, aggregate, local_factor, coarse_factor):
    pairs = lax.axis_size("sub") // 2
    grp_count = lax.axis_size("grp")
    rhs, own_width = residual.shape
    own = own_width // BLK
    rows = rhs // grp_count
    halo = margin.shape[1]
    pad = 8
    begin = 2 * own * rows + pad
    f32 = jnp.float32
    sds = jax.ShapeDtypeStruct
    _, depth, width = local_factor.shape
    coarse_depth, coarse_width = coarse_factor.shape
    blocks = width // BLK
    in_hbm = functools.partial(pltpu.with_memory_space_constraint, memory_space=pltpu.HBM)
    aggregate = aggregate.reshape(1, own)
    local_factor = in_hbm(local_factor)
    coarse_factor = in_hbm(coarse_factor)

    near = swap(residual, "sub", 1)
    near_names = swap(aggregate, "sub", 1)
    held, mine, names = call(
        functools.partial(stage_kernel, own, rows),
        (sds(residual.shape, f32), sds((own * rows, BLK), f32), sds((1, own), f32)),
        [HBM, HBM],
        [
            pltpu.VMEM((own * rhs, BLK), f32),
            pltpu.VMEM((1, own), jnp.int32),
            pltpu.SemaphoreType.DMA((2,)),
        ],
        moved=8 * rhs * own_width,
    )(in_hbm(residual), in_hbm(aggregate))
    margin = in_hbm(margin)
    *outgoing, away, place = call(
        functools.partial(pack_kernel, own, rows, pad),
        [sds((begin + halo * rhs, BLK), f32)] * pairs
        + [sds((halo, BLK), jnp.int32), sds((2 * pairs * own, BLK), jnp.int32)],
        [HBM] + [VMEM] * 5,
        [
            pltpu.VMEM((own * rhs, BLK), f32),
            pltpu.SMEM(margin.shape, jnp.int32),
            pltpu.SemaphoreType.DMA,
        ],
    )(margin, held, mine, names, near_names, near)
    arrived = exchange(outgoing, "sub", 2)
    quarter = coarse_depth // 4
    tile = min(512, depth // 2)
    chunk = depth // 8
    coarse_held = sds(coarse_factor.shape, coarse_factor.dtype)
    begun, local_factor, coarse_part = call(
        functools.partial(load_kernel, chunk, tile),
        (
            sds((rhs, depth), f32),
            sds(local_factor.shape, local_factor.dtype),
            coarse_held,
        ),
        [VMEM, HBM, HBM, pl.BlockSpec(memory_space=pl.ANY)],
        [
            pltpu.SemaphoreType.DMA((depth // chunk,)),
            pltpu.SemaphoreType.DMA((4,)),
        ],
        flops=2 * rhs * depth * own_width,
        moved=2 * depth * width + 2 * quarter * coarse_width,
    )(held, local_factor, coarse_factor, arrived[0])
    chunk = quarter // 4
    count = coarse_width // BLK
    *fine, coarse_part, member, sums = call(
        functools.partial(fine_kernel, own, rows, begin, chunk, tile, pairs),
        [sds((rows * blocks, BLK), f32)] * grp_count
        + [
            coarse_held,
            sds((2 * pairs * own, count), f32),
            sds((rows * count, BLK), f32),
        ],
        [VMEM, VMEM, VMEM, HBM, VMEM] + [VMEM] * pairs,
        [pltpu.VMEM((rhs * blocks, BLK), f32), pltpu.SemaphoreType.DMA((quarter // chunk,))],
        flops=4 * rhs * depth * width,
        moved=2 * depth * width + 2 * quarter * coarse_width,
        input_output_aliases={4: grp_count},
    )(away, begun, local_factor, coarse_factor, coarse_part, *arrived[::-1])
    panels = exchange(fine, "grp")
    lower = coarse_depth - 2 * quarter
    size = own * rows
    spread, _ = call(
        functools.partial(coarse_kernel, own, rows, chunk, tile),
        (sds((2 * pairs, size, BLK), f32), coarse_held),
        [VMEM, HBM, VMEM, VMEM],
        [
            pltpu.VMEM((rows * count, BLK), f32),
            pltpu.VMEM((rows, coarse_depth), f32),
            pltpu.SemaphoreType.DMA((lower // chunk,)),
        ],
        flops=4 * rows * coarse_depth * coarse_width,
        moved=2 * coarse_depth * coarse_width,
        input_output_aliases={0: 1},
    )(coarse_part, coarse_factor, member, sums)
    field = sds((pairs, size, BLK), f32)
    kept, crossing = call(
        functools.partial(merge_kernel, own, rows, grp_count, halo),
        [field, field],
        [VMEM] * (2 + grp_count),
    )(place, spread, *panels)
    back = call(add_kernel, [sds((size, BLK), f32)] * pairs, [VMEM, VMEM])(
        kept, swap(crossing, "sub", 1)
    )
    return call(
        functools.partial(last_kernel, own, rows),
        sds((rows, own_width), f32),
        [VMEM] * pairs,
        [pltpu.VMEM((size, BLK), f32)],
    )(*exchange(list(back), "sub", 2)[::-1])


def solution(mesh):
    placed = (P(None, "sub"), P(), P("sub"), P("sub", "grp", None), P("sub", None))
    return jax.shard_map(
        on_device, mesh=mesh, in_specs=placed, out_specs=P("grp", "sub"), check_vma=False
    )
```

```python
import functools

import jax
import jax.numpy as jnp
from jax import lax
from jax.experimental import pallas as pl
from jax.experimental.pallas import tpu as pltpu
from jax.sharding import PartitionSpec as P

BLK = 128
MIB = 1024 * 1024
VMEM = pl.BlockSpec(memory_space=pltpu.VMEM)
SMEM = pl.BlockSpec(memory_space=pltpu.SMEM)
HBM = pl.BlockSpec(memory_space=pltpu.HBM)
NT = (((1,), (1,)), ((), ()))
TN = (((0,), (0,)), ((), ()))


def call(kernel, out, specs, scratch=(), limit=12 * MIB, flops=0, moved=0, **options):
    return pl.pallas_call(
        kernel,
        out_shape=out,
        in_specs=specs,
        out_specs=jax.tree.map(lambda _: VMEM, out),
        scratch_shapes=scratch,
        compiler_params=pltpu.CompilerParams(vmem_limit_bytes=limit),
        cost_estimate=pl.CostEstimate(flops=flops, bytes_accessed=moved, transcendentals=0),
        **options,
    )


def mm(left, right, dims=(((1,), (0,)), ((), ()))):
    return lax.dot_general(left, right, dims, preferred_element_type=jnp.float32)


def split3(value):
    high = value.astype(jnp.bfloat16)
    rest = value - high.astype(jnp.float32)
    middle = rest.astype(jnp.bfloat16)
    low = (rest - middle.astype(jnp.float32)).astype(jnp.bfloat16)
    return [high, middle, low]


def stage_kernel(own, rows, residual_hbm, aggregate_hbm, residual, mine, names, block_rows, aggregate, sems):
    pairs = ((residual_hbm, residual), (aggregate_hbm, aggregate))
    copies = [pltpu.make_async_copy(a, b, sems.at[i]) for i, (a, b) in enumerate(pairs)]
    start(copies)
    for copy in copies:
        copy.wait()
    names[...] = aggregate[...].astype(jnp.float32)
    mine[...] = rows_of(residual, own, rows, block_rows)


def rows_of(residual, own, rows, block_rows):
    rhs = residual.shape[0]
    for b in range(own):
        block_rows[pl.ds(b, rhs, stride=own), :] = residual[:, b * BLK : (b + 1) * BLK]
    first = lax.axis_index("grp") * rows * own
    return block_rows[pl.ds(pl.multiple_of(first, 8), rows * own), :]


def pack_kernel(own, rows, pad, margin_hbm, residual, mine, names, near_names, near, *refs):
    *outs, away, place, block_rows, margin, sem = refs
    copy = pltpu.make_async_copy(margin_hbm, margin, sem)
    copy.start()
    halo = margin.shape[1]
    rhs = residual.shape[0]
    me = lax.axis_index("sub")
    size = own * rows
    both = [mine[...], rows_of(near, own, rows, block_rows)]
    labels = [names[...], near_names[...].astype(jnp.float32)]
    at = 2 * size
    for out in outs:
        out[at : at + pad, :] = jnp.zeros((pad, BLK), jnp.float32)
        for i in range(2):
            out[i * size : (i + 1) * size, :] = both[i]
            out[at + i : at + i + 1, :own] = labels[i]
    place[...] = jnp.zeros(place.shape, jnp.int32)
    copy.wait()
    for k in range(halo):
        block = margin[me, k]
        owner = block // own
        distance = me ^ owner
        away[k : k + 1, :] = jnp.full((1, BLK), distance // 2, jnp.int32)
        row = distance * own + block - owner * own
        place[pl.ds(row, 1), :] = jnp.full((1, BLK), k + 1, jnp.int32)
    for e, out in enumerate(outs):
        target = me ^ (2 * e)
        for k in range(halo):
            block = margin[target, k]
            owner = block // own
            where = pl.ds(pl.multiple_of((block - owner * own) * BLK, BLK), BLK)
            out[at + pad + k * rhs : at + pad + (k + 1) * rhs, :] = jnp.where(
                owner == me, residual[:, where], near[:, where]
            )


def panel_copies(source, target, chunk, sems, first=0):
    copies = []
    for n in range(target.shape[0] // chunk):
        span = pl.ds(first + n * chunk, chunk)
        copies.append(
            pltpu.make_async_copy(source.at[span], target.at[pl.ds(n * chunk, chunk)], sems.at[n])
        )
    return copies


def start(copies):
    for copy in copies:
        copy.start()


def first_product(factor, right, tile):
    depth = factor.shape[0]
    parts = [
        mm(right, factor[at : min(at + tile, depth), :], NT) for at in range(0, depth, tile)
    ]
    return jnp.concatenate(parts, axis=1)


def in_own_block(body):
    pl.when(lax.axis_index("sub") >= 0)(body)


def load_kernel(
    chunk, tile, residual, fine_hbm, coarse_hbm, after, inner, fine, coarse, sems, more
):
    depth = fine.shape[1]
    own_width = residual.shape[1]
    half = depth // 2
    each = half // chunk
    start(panel_copies(fine_hbm.at[0], fine.at[0], chunk, sems))
    quarter = coarse.shape[0] // 4
    late = panel_copies(coarse_hbm, coarse.at[pl.ds(0, quarter)], quarter // 4, more)

    def step(n, carry):
        for i in range(each):
            span = pl.ds(pl.multiple_of(n * half + i * chunk, chunk), chunk)
            pltpu.make_async_copy(fine_hbm.at[0, span], fine.at[0, span], sems.at[n * each + i]).wait()
        pl.when(n == 0)(lambda: start(late))
        local = residual[...].astype(jnp.bfloat16)
        for i in range(half // tile):
            at = pl.multiple_of(n * half + i * tile, tile)
            rows = fine[0, pl.ds(at, tile), pl.ds(0, own_width)]
            inner[:, pl.ds(at, tile)] = mm(local, rows, NT)
        return carry

    lax.fori_loop(0, 2, step, 0)
    for copy in late:
        copy.wait()


def form_sums(own, rows, coarse, arrived, named, table):
    size = own * rows
    sources = 2 * len(arrived)
    parts = [(part, i) for part in arrived for i in range(2)]
    names = jnp.concatenate(
        [part[2 * size + i : 2 * size + i + 1, :] for part, i in parts], axis=0
    ).T
    catalog = lax.broadcasted_iota(jnp.int32, (own, coarse), 1).astype(jnp.float32)
    member = jnp.concatenate(
        [(names[:own, s : s + 1] == catalog).astype(jnp.float32) for s in range(sources)], axis=0
    ).astype(jnp.bfloat16)
    whole = jnp.concatenate(
        [
            jnp.concatenate(
                [part[i * size + r * own : i * size + (r + 1) * own, :] for part, i in parts],
                axis=0,
            )
            for r in range(rows)
        ],
        axis=1,
    )
    ones = jnp.ones((own * sources, BLK), jnp.bfloat16)
    span = rows * BLK
    found = mm(member, jnp.concatenate(split3(whole) + [ones], axis=1), TN)
    sums = found[:, :span] + found[:, span : 2 * span] + found[:, 2 * span : 3 * span]
    counts = jnp.maximum(found[:, 3 * span :], 1.0)
    for r in range(rows):
        table[r * coarse : (r + 1) * coarse, :] = sums[:, r * BLK : (r + 1) * BLK] / counts
    named[...] = member.astype(jnp.float32)


def fine_kernel(own, rows, begin, chunk, tile, pairs, away, begun, factor, coarse_hbm, given, *refs):
    arrived = refs[:pairs][::-1]
    *outs, coarse, named, sums, table, sems = refs[pairs:]
    first = coarse.shape[0] // 4
    copies = panel_copies(
        coarse_hbm, coarse.at[pl.ds(first, sems.shape[0] * chunk)], chunk, sems, first
    )
    start(copies)
    rhs = begun.shape[0]
    halo = away.shape[0]
    depth, width = factor.shape[1:]
    blocks = width // BLK
    group = lax.axis_index("grp")
    tiles = []
    for k in range(halo):
        span = slice(begin + k * rhs, begin + (k + 1) * rhs)
        distance = away[k : k + 1, :]
        part = arrived[0][span, :]
        for e in range(1, pairs):
            part = jnp.where(distance == e, arrived[e][span, :], part)
        tiles.append(part.astype(jnp.bfloat16))
    form_sums(own, rows, coarse.shape[1] // BLK, arrived, named, sums)
    local = jnp.concatenate(tiles, axis=1)
    far = factor.at[0, :, pl.ds(own * BLK, halo * BLK)]
    mid = (begun[...] + first_product(far, local, tile)).astype(jnp.bfloat16)
    for n in range(width // 256):
        part = mm(mid, factor[0, :, n * 256 : (n + 1) * 256])
        for i in range(256 // BLK):
            b = n * (256 // BLK) + i
            table[pl.ds(b, rhs, stride=blocks), :] = part[:, i * BLK : (i + 1) * BLK]
    size = rows * blocks
    for d, out in enumerate(outs):
        out[...] = table[pl.ds(pl.multiple_of((group ^ d) * size, 8), size), :]

    @in_own_block
    def _():
        for copy in copies:
            copy.wait()


def coarse_kernel(own, rows, chunk, tile, given, factor_hbm, member, sums, out, factor, table, begun, sems):
    depth, width = factor.shape
    done = depth - sems.shape[0] * chunk
    held, lower = factor.at[pl.ds(0, done)], factor.at[pl.ds(done, depth - done)]
    copies = panel_copies(factor_hbm, lower, chunk, sems, done)
    start(copies)
    coarse = width // BLK
    span = rows * BLK

    def right():
        parts = [sums[pl.ds(j, rows, stride=coarse), :] for j in range(coarse)]
        return jnp.concatenate(parts, axis=1).astype(jnp.bfloat16)

    first = right()
    begun[:, :done] = first_product(held, first, tile)

    @in_own_block
    def _():
        for copy in copies:
            copy.wait()
        begun[:, done:] = first_product(lower, right(), tile)
        mid = begun[...].astype(jnp.bfloat16)
        for n in range(width // 256):
            where = slice(n * 256, (n + 1) * 256)
            part = mm(mid, factor[:, where])
            for i in range(256 // BLK):
                j = n * (256 // BLK) + i
                table[pl.ds(j, rows, stride=coarse), :] = part[:, i * BLK : (i + 1) * BLK]
        solved = jnp.concatenate([table[r * coarse : (r + 1) * coarse, :] for r in range(rows)], axis=1)
        spread = mm(member[...].astype(jnp.bfloat16), jnp.concatenate(split3(solved), axis=1))
        spread = spread[:, :span] + spread[:, span : 2 * span] + spread[:, 2 * span :]
        for s in range(out.shape[0]):
            for r in range(rows):
                out[s, r * own : (r + 1) * own, :] = spread[
                    s * own : (s + 1) * own, r * BLK : (r + 1) * BLK
                ]


def merge_kernel(own, rows, groups, halo, place, spread, *refs):
    arrived = refs[:groups]
    kept, near = refs[groups:]
    blocks = own + halo
    total = arrived[0][...]
    for part in arrived[1:]:
        total = total + part[...]
    for d in range(spread.shape[0]):
        where = place[d * own : (d + 1) * own, :]
        hits = [where == k + 1 for k in range(halo)] if d else []
        out = near if d % 2 else kept
        for r in range(rows):
            span = slice(r * own, (r + 1) * own)
            field = spread[d, span, :]
            if d == 0:
                field = field + total[r * blocks : r * blocks + own, :]
            for k, hit in enumerate(hits):
                row = r * blocks + own + k
                field = field + jnp.where(hit, total[row : row + 1, :], 0.0)
            out[d // 2, span, :] = field


def add_kernel(kept, arrived, *outs):
    for e, out in enumerate(outs):
        out[...] = kept[e] + arrived[e]


def last_kernel(own, rows, *refs):
    *arrived, out, total = refs
    summed = arrived[0][...]
    for part in arrived[1:]:
        summed = summed + part[...]
    total[...] = summed
    for b in range(own):
        out[:, b * BLK : (b + 1) * BLK] = total[pl.ds(b, rows, stride=own), :]


def swap(value, axis, distance):
    count = lax.axis_size(axis)
    return lax.ppermute(value, axis, [(i, i ^ distance) for i in range(count)])


def exchange(parts, axis, unit=1):
    there = [swap(parts[d], axis, d * unit) for d in range(len(parts) - 1, 0, -1)]
    return [parts[0]] + there[::-1]


def on_device(residual, margin, aggregate, local_factor, coarse_factor):
    pairs = lax.axis_size("sub") // 2
    grp_count = lax.axis_size("grp")
    rhs, own_width = residual.shape
    own = own_width // BLK
    rows = rhs // grp_count
    halo = margin.shape[1]
    pad = 8
    begin = 2 * own * rows + pad
    f32 = jnp.float32
    sds = jax.ShapeDtypeStruct
    _, depth, width = local_factor.shape
    coarse_depth, coarse_width = coarse_factor.shape
    blocks = width // BLK
    in_hbm = functools.partial(pltpu.with_memory_space_constraint, memory_space=pltpu.HBM)
    aggregate = aggregate.reshape(1, own)
    local_factor = in_hbm(local_factor)
    coarse_factor = in_hbm(coarse_factor)

    near = swap(residual, "sub", 1)
    near_names = swap(aggregate, "sub", 1)
    held, mine, names = call(
        functools.partial(stage_kernel, own, rows),
        (sds(residual.shape, f32), sds((own * rows, BLK), f32), sds((1, own), f32)),
        [HBM, HBM],
        [
            pltpu.VMEM((own * rhs, BLK), f32),
            pltpu.VMEM((1, own), jnp.int32),
            pltpu.SemaphoreType.DMA((2,)),
        ],
        moved=8 * rhs * own_width,
    )(in_hbm(residual), in_hbm(aggregate))
    margin = in_hbm(margin)
    *outgoing, away, place = call(
        functools.partial(pack_kernel, own, rows, pad),
        [sds((begin + halo * rhs, BLK), f32)] * pairs
        + [sds((halo, BLK), jnp.int32), sds((2 * pairs * own, BLK), jnp.int32)],
        [HBM] + [VMEM] * 5,
        [
            pltpu.VMEM((own * rhs, BLK), f32),
            pltpu.SMEM(margin.shape, jnp.int32),
            pltpu.SemaphoreType.DMA,
        ],
    )(margin, held, mine, names, near_names, near)
    arrived = exchange(outgoing, "sub", 2)
    quarter = coarse_depth // 4
    tile = min(512, depth // 2)
    chunk = depth // 8
    coarse_held = sds(coarse_factor.shape, coarse_factor.dtype)
    begun, local_factor, coarse_part = call(
        functools.partial(load_kernel, chunk, tile),
        (
            sds((rhs, depth), f32),
            sds(local_factor.shape, local_factor.dtype),
            coarse_held,
        ),
        [VMEM, HBM, HBM, pl.BlockSpec(memory_space=pl.ANY)],
        [
            pltpu.SemaphoreType.DMA((depth // chunk,)),
            pltpu.SemaphoreType.DMA((4,)),
        ],
        flops=2 * rhs * depth * own_width,
        moved=2 * depth * width + 2 * quarter * coarse_width,
    )(held, local_factor, coarse_factor, arrived[0])
    chunk = quarter // 4
    middle = 6 * chunk
    count = coarse_width // BLK
    *fine, coarse_part, member, sums = call(
        functools.partial(fine_kernel, own, rows, begin, chunk, tile, pairs),
        [sds((rows * blocks, BLK), f32)] * grp_count
        + [
            coarse_held,
            sds((2 * pairs * own, count), f32),
            sds((rows * count, BLK), f32),
        ],
        [VMEM, VMEM, VMEM, HBM, VMEM] + [VMEM] * pairs,
        [pltpu.VMEM((rhs * blocks, BLK), f32), pltpu.SemaphoreType.DMA((middle // chunk,))],
        flops=4 * rhs * depth * width,
        moved=2 * depth * width + 2 * middle * coarse_width,
        input_output_aliases={4: grp_count},
    )(away, begun, local_factor, coarse_factor, coarse_part, *arrived[::-1])
    panels = exchange(fine, "grp")
    lower = coarse_depth - quarter - middle
    size = own * rows
    spread, _ = call(
        functools.partial(coarse_kernel, own, rows, chunk, tile),
        (sds((2 * pairs, size, BLK), f32), coarse_held),
        [VMEM, HBM, VMEM, VMEM],
        [
            pltpu.VMEM((rows * count, BLK), f32),
            pltpu.VMEM((rows, coarse_depth), f32),
            pltpu.SemaphoreType.DMA((lower // chunk,)),
        ],
        flops=4 * rows * coarse_depth * coarse_width,
        moved=2 * coarse_depth * coarse_width,
        input_output_aliases={0: 1},
    )(coarse_part, coarse_factor, member, sums)
    field = sds((pairs, size, BLK), f32)
    kept, crossing = call(
        functools.partial(merge_kernel, own, rows, grp_count, halo),
        [field, field],
        [VMEM] * (2 + grp_count),
    )(place, spread, *panels)
    back = call(add_kernel, [sds((size, BLK), f32)] * pairs, [VMEM, VMEM])(
        kept, swap(crossing, "sub", 1)
    )
    return call(
        functools.partial(last_kernel, own, rows),
        sds((rows, own_width), f32),
        [VMEM] * pairs,
        [pltpu.VMEM((size, BLK), f32)],
    )(*exchange(list(back), "sub", 2)[::-1])


def solution(mesh):
    placed = (P(None, "sub"), P(), P("sub"), P("sub", "grp", None), P("sub", None))
    return jax.shard_map(
        on_device, mesh=mesh, in_specs=placed, out_specs=P("grp", "sub"), check_vma=False
    )
```

```python
import functools

import jax
import jax.numpy as jnp
from jax import lax
from jax.experimental import pallas as pl
from jax.experimental.pallas import tpu as pltpu
from jax.sharding import PartitionSpec as P

BLK = 128
MIB = 1024 * 1024
VMEM = pl.BlockSpec(memory_space=pltpu.VMEM)
SMEM = pl.BlockSpec(memory_space=pltpu.SMEM)
HBM = pl.BlockSpec(memory_space=pltpu.HBM)
NT = (((1,), (1,)), ((), ()))
TN = (((0,), (0,)), ((), ()))


def call(kernel, out, specs, scratch=(), limit=12 * MIB, flops=0, moved=0, **options):
    return pl.pallas_call(
        kernel,
        out_shape=out,
        in_specs=specs,
        out_specs=jax.tree.map(lambda _: VMEM, out),
        scratch_shapes=scratch,
        compiler_params=pltpu.CompilerParams(vmem_limit_bytes=limit),
        cost_estimate=pl.CostEstimate(flops=flops, bytes_accessed=moved, transcendentals=0),
        **options,
    )


def mm(left, right, dims=(((1,), (0,)), ((), ()))):
    return lax.dot_general(left, right, dims, preferred_element_type=jnp.float32)


def split3(value):
    high = value.astype(jnp.bfloat16)
    rest = value - high.astype(jnp.float32)
    middle = rest.astype(jnp.bfloat16)
    low = (rest - middle.astype(jnp.float32)).astype(jnp.bfloat16)
    return [high, middle, low]


def stage_kernel(own, rows, residual_hbm, aggregate_hbm, residual, mine, names, block_rows, aggregate, sems):
    pairs = ((residual_hbm, residual), (aggregate_hbm, aggregate))
    copies = [pltpu.make_async_copy(a, b, sems.at[i]) for i, (a, b) in enumerate(pairs)]
    start(copies)
    for copy in copies:
        copy.wait()
    names[...] = aggregate[...].astype(jnp.float32)
    mine[...] = rows_of(residual, own, rows, block_rows)


def rows_of(residual, own, rows, block_rows):
    rhs = residual.shape[0]
    for b in range(own):
        block_rows[pl.ds(b, rhs, stride=own), :] = residual[:, b * BLK : (b + 1) * BLK]
    first = lax.axis_index("grp") * rows * own
    return block_rows[pl.ds(pl.multiple_of(first, 8), rows * own), :]


def pack_kernel(own, rows, pad, margin_hbm, residual, mine, names, near_names, near, *refs):
    *outs, away, place, block_rows, margin, sem = refs
    copy = pltpu.make_async_copy(margin_hbm, margin, sem)
    copy.start()
    halo = margin.shape[1]
    rhs = residual.shape[0]
    me = lax.axis_index("sub")
    size = own * rows
    both = [mine[...], rows_of(near, own, rows, block_rows)]
    labels = [names[...], near_names[...].astype(jnp.float32)]
    at = 2 * size
    for out in outs:
        out[at : at + pad, :] = jnp.zeros((pad, BLK), jnp.float32)
        for i in range(2):
            out[i * size : (i + 1) * size, :] = both[i]
            out[at + i : at + i + 1, :own] = labels[i]
    place[...] = jnp.zeros(place.shape, jnp.int32)
    copy.wait()
    for k in range(halo):
        block = margin[me, k]
        owner = block // own
        distance = me ^ owner
        away[k : k + 1, :] = jnp.full((1, BLK), distance // 2, jnp.int32)
        row = distance * own + block - owner * own
        place[pl.ds(row, 1), :] = jnp.full((1, BLK), k + 1, jnp.int32)
    for e, out in enumerate(outs):
        target = me ^ (2 * e)
        for k in range(halo):
            block = margin[target, k]
            owner = block // own
            where = pl.ds(pl.multiple_of((block - owner * own) * BLK, BLK), BLK)
            out[at + pad + k * rhs : at + pad + (k + 1) * rhs, :] = jnp.where(
                owner == me, residual[:, where], near[:, where]
            )


def panel_copies(source, target, chunk, sems, first=0):
    copies = []
    for n in range(target.shape[0] // chunk):
        span = pl.ds(first + n * chunk, chunk)
        copies.append(
            pltpu.make_async_copy(source.at[span], target.at[pl.ds(n * chunk, chunk)], sems.at[n])
        )
    return copies


def start(copies):
    for copy in copies:
        copy.start()


def first_product(factor, right, tile):
    depth = factor.shape[0]
    parts = [
        mm(right, factor[at : min(at + tile, depth), :], NT) for at in range(0, depth, tile)
    ]
    return jnp.concatenate(parts, axis=1)


def in_own_block(body):
    pl.when(lax.axis_index("sub") >= 0)(body)


def load_kernel(
    chunk, tile, residual, fine_hbm, coarse_hbm, after, inner, fine, coarse, sems, more
):
    depth = fine.shape[1]
    own_width = residual.shape[1]
    half = depth // 2
    each = half // chunk
    start(panel_copies(fine_hbm.at[0], fine.at[0], chunk, sems))
    quarter = coarse.shape[0] // 4
    late = panel_copies(coarse_hbm, coarse.at[pl.ds(0, quarter)], quarter // 4, more)

    def step(n, carry):
        for i in range(each):
            span = pl.ds(pl.multiple_of(n * half + i * chunk, chunk), chunk)
            pltpu.make_async_copy(fine_hbm.at[0, span], fine.at[0, span], sems.at[n * each + i]).wait()
        pl.when(n == 0)(lambda: start(late))
        local = residual[...].astype(jnp.bfloat16)
        for i in range(half // tile):
            at = pl.multiple_of(n * half + i * tile, tile)
            rows = fine[0, pl.ds(at, tile), pl.ds(0, own_width)]
            inner[:, pl.ds(at, tile)] = mm(local, rows, NT)
        return carry

    lax.fori_loop(0, 2, step, 0)
    for copy in late:
        copy.wait()


def form_sums(own, rows, coarse, arrived, named, table):
    size = own * rows
    sources = 2 * len(arrived)
    parts = [(part, i) for part in arrived for i in range(2)]
    names = jnp.concatenate(
        [part[2 * size + i : 2 * size + i + 1, :] for part, i in parts], axis=0
    ).T
    catalog = lax.broadcasted_iota(jnp.int32, (own, coarse), 1).astype(jnp.float32)
    member = jnp.concatenate(
        [(names[:own, s : s + 1] == catalog).astype(jnp.float32) for s in range(sources)], axis=0
    ).astype(jnp.bfloat16)
    whole = jnp.concatenate(
        [
            jnp.concatenate(
                [part[i * size + r * own : i * size + (r + 1) * own, :] for part, i in parts],
                axis=0,
            )
            for r in range(rows)
        ],
        axis=1,
    )
    ones = jnp.ones((own * sources, BLK), jnp.bfloat16)
    span = rows * BLK
    found = mm(member, jnp.concatenate(split3(whole) + [ones], axis=1), TN)
    sums = found[:, :span] + found[:, span : 2 * span] + found[:, 2 * span : 3 * span]
    counts = jnp.maximum(found[:, 3 * span :], 1.0)
    for r in range(rows):
        table[r * coarse : (r + 1) * coarse, :] = sums[:, r * BLK : (r + 1) * BLK] / counts
    named[...] = member.astype(jnp.float32)


def fine_kernel(own, rows, begin, chunk, tile, pairs, away, begun, factor, coarse_hbm, given, *refs):
    arrived = refs[:pairs][::-1]
    *outs, coarse, named, sums, table, sems = refs[pairs:]
    first = coarse.shape[0] // 4
    copies = panel_copies(
        coarse_hbm, coarse.at[pl.ds(first, sems.shape[0] * chunk)], chunk, sems, first
    )
    start(copies)
    rhs = begun.shape[0]
    halo = away.shape[0]
    depth, width = factor.shape[1:]
    blocks = width // BLK
    group = lax.axis_index("grp")
    tiles = []
    for k in range(halo):
        span = slice(begin + k * rhs, begin + (k + 1) * rhs)
        distance = away[k : k + 1, :]
        part = arrived[0][span, :]
        for e in range(1, pairs):
            part = jnp.where(distance == e, arrived[e][span, :], part)
        tiles.append(part.astype(jnp.bfloat16))
    form_sums(own, rows, coarse.shape[1] // BLK, arrived, named, sums)
    local = jnp.concatenate(tiles, axis=1)
    far = factor.at[0, :, pl.ds(own * BLK, halo * BLK)]
    mid = (begun[...] + first_product(far, local, tile)).astype(jnp.bfloat16)
    for n in range(width // 256):
        part = mm(mid, factor[0, :, n * 256 : (n + 1) * 256])
        for i in range(256 // BLK):
            b = n * (256 // BLK) + i
            table[pl.ds(b, rhs, stride=blocks), :] = part[:, i * BLK : (i + 1) * BLK]
    size = rows * blocks
    for d, out in enumerate(outs):
        out[...] = table[pl.ds(pl.multiple_of((group ^ d) * size, 8), size), :]

    @in_own_block
    def _():
        for copy in copies:
            copy.wait()


def coarse_kernel(own, rows, chunk, tile, given, factor_hbm, member, sums, out, factor, table, begun, sems):
    depth, width = factor.shape
    done = depth - sems.shape[0] * chunk
    held, lower = factor.at[pl.ds(0, done)], factor.at[pl.ds(done, depth - done)]
    copies = panel_copies(factor_hbm, lower, chunk, sems, done)
    start(copies)
    coarse = width // BLK
    span = rows * BLK

    def right():
        parts = [sums[pl.ds(j, rows, stride=coarse), :] for j in range(coarse)]
        return jnp.concatenate(parts, axis=1).astype(jnp.bfloat16)

    first = right()
    begun[:, :done] = first_product(held, first, tile)

    @in_own_block
    def _():
        for copy in copies:
            copy.wait()
        begun[:, done:] = first_product(lower, right(), tile)
        mid = begun[...].astype(jnp.bfloat16)
        for n in range(width // 256):
            where = slice(n * 256, (n + 1) * 256)
            part = mm(mid, factor[:, where])
            for i in range(256 // BLK):
                j = n * (256 // BLK) + i
                table[pl.ds(j, rows, stride=coarse), :] = part[:, i * BLK : (i + 1) * BLK]
        solved = jnp.concatenate([table[r * coarse : (r + 1) * coarse, :] for r in range(rows)], axis=1)
        spread = mm(member[...].astype(jnp.bfloat16), jnp.concatenate(split3(solved), axis=1))
        spread = spread[:, :span] + spread[:, span : 2 * span] + spread[:, 2 * span :]
        for s in range(out.shape[0]):
            for r in range(rows):
                out[s, r * own : (r + 1) * own, :] = spread[
                    s * own : (s + 1) * own, r * BLK : (r + 1) * BLK
                ]


def merge_kernel(own, rows, groups, halo, place, spread, *refs):
    arrived = refs[:groups]
    kept, near = refs[groups:]
    blocks = own + halo
    total = arrived[0][...]
    for part in arrived[1:]:
        total = total + part[...]
    for d in range(spread.shape[0]):
        where = place[d * own : (d + 1) * own, :]
        hits = [where == k + 1 for k in range(halo)] if d else []
        out = near if d % 2 else kept
        for r in range(rows):
            span = slice(r * own, (r + 1) * own)
            field = spread[d, span, :]
            if d == 0:
                field = field + total[r * blocks : r * blocks + own, :]
            for k, hit in enumerate(hits):
                row = r * blocks + own + k
                field = field + jnp.where(hit, total[row : row + 1, :], 0.0)
            out[d // 2, span, :] = field


def add_kernel(kept, arrived, *outs):
    for e, out in enumerate(outs):
        out[...] = kept[e] + arrived[e]


def last_kernel(own, rows, *refs):
    *arrived, out, total = refs
    summed = arrived[0][...]
    for part in arrived[1:]:
        summed = summed + part[...]
    total[...] = summed
    for b in range(own):
        out[:, b * BLK : (b + 1) * BLK] = total[pl.ds(b, rows, stride=own), :]


def swap(value, axis, distance):
    count = lax.axis_size(axis)
    return lax.ppermute(value, axis, [(i, i ^ distance) for i in range(count)])


def exchange(parts, axis, unit=1):
    there = [swap(parts[d], axis, d * unit) for d in range(len(parts) - 1, 0, -1)]
    return [parts[0]] + there[::-1]


def on_device(residual, margin, aggregate, local_factor, coarse_factor):
    pairs = lax.axis_size("sub") // 2
    grp_count = lax.axis_size("grp")
    rhs, own_width = residual.shape
    own = own_width // BLK
    rows = rhs // grp_count
    halo = margin.shape[1]
    pad = 8
    begin = 2 * own * rows + pad
    f32 = jnp.float32
    sds = jax.ShapeDtypeStruct
    _, depth, width = local_factor.shape
    coarse_depth, coarse_width = coarse_factor.shape
    blocks = width // BLK
    in_hbm = functools.partial(pltpu.with_memory_space_constraint, memory_space=pltpu.HBM)
    aggregate = aggregate.reshape(1, own)
    local_factor = in_hbm(local_factor)
    coarse_factor = in_hbm(coarse_factor)

    near = swap(residual, "sub", 1)
    near_names = swap(aggregate, "sub", 1)
    held, mine, names = call(
        functools.partial(stage_kernel, own, rows),
        (sds(residual.shape, f32), sds((own * rows, BLK), f32), sds((1, own), f32)),
        [HBM, HBM],
        [
            pltpu.VMEM((own * rhs, BLK), f32),
            pltpu.VMEM((1, own), jnp.int32),
            pltpu.SemaphoreType.DMA((2,)),
        ],
        moved=8 * rhs * own_width,
    )(in_hbm(residual), in_hbm(aggregate))
    margin = in_hbm(margin)
    *outgoing, away, place = call(
        functools.partial(pack_kernel, own, rows, pad),
        [sds((begin + halo * rhs, BLK), f32)] * pairs
        + [sds((halo, BLK), jnp.int32), sds((2 * pairs * own, BLK), jnp.int32)],
        [HBM] + [VMEM] * 5,
        [
            pltpu.VMEM((own * rhs, BLK), f32),
            pltpu.SMEM(margin.shape, jnp.int32),
            pltpu.SemaphoreType.DMA,
        ],
    )(margin, held, mine, names, near_names, near)
    arrived = exchange(outgoing, "sub", 2)
    quarter = coarse_depth // 4
    tile = min(512, depth // 2)
    chunk = depth // 8
    coarse_held = sds(coarse_factor.shape, coarse_factor.dtype)
    begun, local_factor, coarse_part = call(
        functools.partial(load_kernel, chunk, tile),
        (
            sds((rhs, depth), f32),
            sds(local_factor.shape, local_factor.dtype),
            coarse_held,
        ),
        [VMEM, HBM, HBM, pl.BlockSpec(memory_space=pl.ANY)],
        [
            pltpu.SemaphoreType.DMA((depth // chunk,)),
            pltpu.SemaphoreType.DMA((4,)),
        ],
        flops=2 * rhs * depth * own_width,
        moved=2 * depth * width + 2 * quarter * coarse_width,
    )(held, local_factor, coarse_factor, arrived[0])
    chunk = quarter // 4
    middle = 2 * chunk
    count = coarse_width // BLK
    *fine, coarse_part, member, sums = call(
        functools.partial(fine_kernel, own, rows, begin, chunk, tile, pairs),
        [sds((rows * blocks, BLK), f32)] * grp_count
        + [
            coarse_held,
            sds((2 * pairs * own, count), f32),
            sds((rows * count, BLK), f32),
        ],
        [VMEM, VMEM, VMEM, HBM, VMEM] + [VMEM] * pairs,
        [pltpu.VMEM((rhs * blocks, BLK), f32), pltpu.SemaphoreType.DMA((middle // chunk,))],
        flops=4 * rhs * depth * width,
        moved=2 * depth * width + 2 * middle * coarse_width,
        input_output_aliases={4: grp_count},
    )(away, begun, local_factor, coarse_factor, coarse_part, *arrived[::-1])
    panels = exchange(fine, "grp")
    lower = coarse_depth - quarter - middle
    size = own * rows
    spread, _ = call(
        functools.partial(coarse_kernel, own, rows, chunk, tile),
        (sds((2 * pairs, size, BLK), f32), coarse_held),
        [VMEM, HBM, VMEM, VMEM],
        [
            pltpu.VMEM((rows * count, BLK), f32),
            pltpu.VMEM((rows, coarse_depth), f32),
            pltpu.SemaphoreType.DMA((lower // chunk,)),
        ],
        flops=4 * rows * coarse_depth * coarse_width,
        moved=2 * coarse_depth * coarse_width,
        input_output_aliases={0: 1},
    )(coarse_part, coarse_factor, member, sums)
    field = sds((pairs, size, BLK), f32)
    kept, crossing = call(
        functools.partial(merge_kernel, own, rows, grp_count, halo),
        [field, field],
        [VMEM] * (2 + grp_count),
    )(place, spread, *panels)
    back = call(add_kernel, [sds((size, BLK), f32)] * pairs, [VMEM, VMEM])(
        kept, swap(crossing, "sub", 1)
    )
    return call(
        functools.partial(last_kernel, own, rows),
        sds((rows, own_width), f32),
        [VMEM] * pairs,
        [pltpu.VMEM((size, BLK), f32)],
    )(*exchange(list(back), "sub", 2)[::-1])


def solution(mesh):
    placed = (P(None, "sub"), P(), P("sub"), P("sub", "grp", None), P("sub", None))
    return jax.shard_map(
        on_device, mesh=mesh, in_specs=placed, out_specs=P("grp", "sub"), check_vma=False
    )
```

```python
import functools

import jax
import jax.numpy as jnp
from jax import lax
from jax.experimental import pallas as pl
from jax.experimental.pallas import tpu as pltpu
from jax.sharding import PartitionSpec as P

BLK = 128
MIB = 1024 * 1024
VMEM = pl.BlockSpec(memory_space=pltpu.VMEM)
SMEM = pl.BlockSpec(memory_space=pltpu.SMEM)
HBM = pl.BlockSpec(memory_space=pltpu.HBM)
NT = (((1,), (1,)), ((), ()))
TN = (((0,), (0,)), ((), ()))


def call(kernel, out, specs, scratch=(), limit=12 * MIB, flops=0, moved=0, **options):
    return pl.pallas_call(
        kernel,
        out_shape=out,
        in_specs=specs,
        out_specs=jax.tree.map(lambda _: VMEM, out),
        scratch_shapes=scratch,
        compiler_params=pltpu.CompilerParams(vmem_limit_bytes=limit),
        cost_estimate=pl.CostEstimate(flops=flops, bytes_accessed=moved, transcendentals=0),
        **options,
    )


def mm(left, right, dims=(((1,), (0,)), ((), ()))):
    return lax.dot_general(left, right, dims, preferred_element_type=jnp.float32)


def split3(value):
    high = value.astype(jnp.bfloat16)
    rest = value - high.astype(jnp.float32)
    middle = rest.astype(jnp.bfloat16)
    low = (rest - middle.astype(jnp.float32)).astype(jnp.bfloat16)
    return [high, middle, low]


def stage_kernel(own, rows, residual_hbm, aggregate_hbm, residual, mine, names, block_rows, aggregate, sems):
    pairs = ((residual_hbm, residual), (aggregate_hbm, aggregate))
    copies = [pltpu.make_async_copy(a, b, sems.at[i]) for i, (a, b) in enumerate(pairs)]
    start(copies)
    for copy in copies:
        copy.wait()
    names[...] = aggregate[...].astype(jnp.float32)
    mine[...] = rows_of(residual, own, rows, block_rows)


def rows_of(residual, own, rows, block_rows):
    rhs = residual.shape[0]
    for b in range(own):
        block_rows[pl.ds(b, rhs, stride=own), :] = residual[:, b * BLK : (b + 1) * BLK]
    first = lax.axis_index("grp") * rows * own
    return block_rows[pl.ds(pl.multiple_of(first, 8), rows * own), :]


def pack_kernel(own, rows, pad, margin_hbm, residual, mine, names, near_names, near, *refs):
    *outs, away, place, block_rows, margin, sem = refs
    copy = pltpu.make_async_copy(margin_hbm, margin, sem)
    copy.start()
    halo = margin.shape[1]
    rhs = residual.shape[0]
    me = lax.axis_index("sub")
    size = own * rows
    both = [mine[...], rows_of(near, own, rows, block_rows)]
    labels = [names[...], near_names[...].astype(jnp.float32)]
    at = 2 * size
    for out in outs:
        out[at : at + pad, :] = jnp.zeros((pad, BLK), jnp.float32)
        for i in range(2):
            out[i * size : (i + 1) * size, :] = both[i]
            out[at + i : at + i + 1, :own] = labels[i]
    place[...] = jnp.zeros(place.shape, jnp.int32)
    copy.wait()
    for k in range(halo):
        block = margin[me, k]
        owner = block // own
        distance = me ^ owner
        away[k : k + 1, :] = jnp.full((1, BLK), distance // 2, jnp.int32)
        row = distance * own + block - owner * own
        place[pl.ds(row, 1), :] = jnp.full((1, BLK), k + 1, jnp.int32)
    for e, out in enumerate(outs):
        target = me ^ (2 * e)
        for k in range(halo):
            block = margin[target, k]
            owner = block // own
            where = pl.ds(pl.multiple_of((block - owner * own) * BLK, BLK), BLK)
            out[at + pad + k * rhs : at + pad + (k + 1) * rhs, :] = jnp.where(
                owner == me, residual[:, where], near[:, where]
            )


def panel_copies(source, target, chunk, sems, first=0):
    copies = []
    for n in range(target.shape[0] // chunk):
        span = pl.ds(first + n * chunk, chunk)
        copies.append(
            pltpu.make_async_copy(source.at[span], target.at[pl.ds(n * chunk, chunk)], sems.at[n])
        )
    return copies


def start(copies):
    for copy in copies:
        copy.start()


def first_product(factor, right, tile):
    tile = min(tile, factor.shape[0])
    parts = [
        mm(right, factor[n * tile : (n + 1) * tile, :], NT) for n in range(factor.shape[0] // tile)
    ]
    return jnp.concatenate(parts, axis=1)


def in_own_block(body):
    pl.when(lax.axis_index("sub") >= 0)(body)


def load_kernel(
    chunk, tile, residual, fine_hbm, coarse_hbm, after, inner, fine, coarse, sems, more
):
    depth = fine.shape[1]
    own_width = residual.shape[1]
    half = depth // 2
    each = half // chunk
    start(panel_copies(fine_hbm.at[0], fine.at[0], chunk, sems))
    quarter = coarse.shape[0] // 4
    late = panel_copies(coarse_hbm, coarse.at[pl.ds(0, quarter)], quarter // 4, more)

    def step(n, carry):
        for i in range(each):
            span = pl.ds(pl.multiple_of(n * half + i * chunk, chunk), chunk)
            pltpu.make_async_copy(fine_hbm.at[0, span], fine.at[0, span], sems.at[n * each + i]).wait()
        pl.when(n == 0)(lambda: start(late))
        local = residual[...].astype(jnp.bfloat16)
        for i in range(half // tile):
            at = pl.multiple_of(n * half + i * tile, tile)
            rows = fine[0, pl.ds(at, tile), pl.ds(0, own_width)]
            inner[:, pl.ds(at, tile)] = mm(local, rows, NT)
        return carry

    lax.fori_loop(0, 2, step, 0)
    for copy in late:
        copy.wait()


def form_sums(own, rows, coarse, arrived, named, table):
    size = own * rows
    sources = 2 * len(arrived)
    parts = [(part, i) for part in arrived for i in range(2)]
    names = jnp.concatenate(
        [part[2 * size + i : 2 * size + i + 1, :] for part, i in parts], axis=0
    ).T
    catalog = lax.broadcasted_iota(jnp.int32, (own, coarse), 1).astype(jnp.float32)
    member = jnp.concatenate(
        [(names[:own, s : s + 1] == catalog).astype(jnp.float32) for s in range(sources)], axis=0
    ).astype(jnp.bfloat16)
    whole = jnp.concatenate(
        [
            jnp.concatenate(
                [part[i * size + r * own : i * size + (r + 1) * own, :] for part, i in parts],
                axis=0,
            )
            for r in range(rows)
        ],
        axis=1,
    )
    ones = jnp.ones((own * sources, BLK), jnp.bfloat16)
    span = rows * BLK
    found = mm(member, jnp.concatenate(split3(whole) + [ones], axis=1), TN)
    sums = found[:, :span] + found[:, span : 2 * span] + found[:, 2 * span : 3 * span]
    counts = jnp.maximum(found[:, 3 * span :], 1.0)
    for r in range(rows):
        table[r * coarse : (r + 1) * coarse, :] = sums[:, r * BLK : (r + 1) * BLK] / counts
    named[...] = member.astype(jnp.float32)


def fine_kernel(own, rows, begin, chunk, tile, pairs, away, begun, factor, coarse_hbm, given, *refs):
    arrived = refs[:pairs][::-1]
    *outs, coarse, named, sums, table, sems = refs[pairs:]
    quarter = coarse.shape[0] // 4
    copies = panel_copies(coarse_hbm, coarse.at[pl.ds(quarter, quarter)], chunk, sems, quarter)
    start(copies)
    rhs = begun.shape[0]
    halo = away.shape[0]
    depth, width = factor.shape[1:]
    blocks = width // BLK
    group = lax.axis_index("grp")
    tiles = []
    for k in range(halo):
        span = slice(begin + k * rhs, begin + (k + 1) * rhs)
        distance = away[k : k + 1, :]
        part = arrived[0][span, :]
        for e in range(1, pairs):
            part = jnp.where(distance == e, arrived[e][span, :], part)
        tiles.append(part.astype(jnp.bfloat16))
    form_sums(own, rows, coarse.shape[1] // BLK, arrived, named, sums)
    local = jnp.concatenate(tiles, axis=1)
    far = factor.at[0, :, pl.ds(own * BLK, halo * BLK)]
    mid = (begun[...] + first_product(far, local, tile)).astype(jnp.bfloat16)
    for n in range(width // 256):
        part = mm(mid, factor[0, :, n * 256 : (n + 1) * 256])
        for i in range(256 // BLK):
            b = n * (256 // BLK) + i
            table[pl.ds(b, rhs, stride=blocks), :] = part[:, i * BLK : (i + 1) * BLK]
    size = rows * blocks
    for d, out in enumerate(outs):
        out[...] = table[pl.ds(pl.multiple_of((group ^ d) * size, 8), size), :]

    @in_own_block
    def _():
        for copy in copies:
            copy.wait()


def coarse_kernel(own, rows, chunk, tile, given, factor_hbm, member, sums, out, factor, table, begun, sems):
    depth, width = factor.shape
    done = depth // 2
    held, lower = factor.at[pl.ds(0, done)], factor.at[pl.ds(done, depth - done)]
    copies = panel_copies(factor_hbm, lower, chunk, sems, done)
    start(copies)
    coarse = width // BLK
    span = rows * BLK

    def right():
        parts = [sums[pl.ds(j, rows, stride=coarse), :] for j in range(coarse)]
        return jnp.concatenate(parts, axis=1).astype(jnp.bfloat16)

    first = right()
    begun[:, :done] = first_product(held, first, tile)

    @in_own_block
    def _():
        for copy in copies:
            copy.wait()
        begun[:, done:] = first_product(lower, right(), tile)
        mid = begun[...].astype(jnp.bfloat16)
        for n in range(width // 256):
            where = slice(n * 256, (n + 1) * 256)
            part = mm(mid, factor[:, where])
            for i in range(256 // BLK):
                j = n * (256 // BLK) + i
                table[pl.ds(j, rows, stride=coarse), :] = part[:, i * BLK : (i + 1) * BLK]
        solved = jnp.concatenate([table[r * coarse : (r + 1) * coarse, :] for r in range(rows)], axis=1)
        spread = mm(member[...].astype(jnp.bfloat16), jnp.concatenate(split3(solved), axis=1))
        spread = spread[:, :span] + spread[:, span : 2 * span] + spread[:, 2 * span :]
        for s in range(out.shape[0]):
            for r in range(rows):
                out[s, r * own : (r + 1) * own, :] = spread[
                    s * own : (s + 1) * own, r * BLK : (r + 1) * BLK
                ]


def merge_kernel(own, rows, groups, halo, place, spread, *refs):
    arrived = refs[:groups]
    kept, near = refs[groups:]
    blocks = own + halo
    total = arrived[0][...]
    for part in arrived[1:]:
        total = total + part[...]
    for d in range(spread.shape[0]):
        where = place[d * own : (d + 1) * own, :]
        hits = [where == k + 1 for k in range(halo)] if d else []
        out = near if d % 2 else kept
        for r in range(rows):
            span = slice(r * own, (r + 1) * own)
            field = spread[d, span, :]
            if d == 0:
                field = field + total[r * blocks : r * blocks + own, :]
            for k, hit in enumerate(hits):
                row = r * blocks + own + k
                field = field + jnp.where(hit, total[row : row + 1, :], 0.0)
            out[d // 2, span, :] = field


def add_kernel(kept, arrived, *outs):
    for e, out in enumerate(outs):
        out[...] = kept[e] + arrived[e]


def last_kernel(own, rows, *refs):
    *arrived, out, total = refs
    summed = arrived[0][...]
    for part in arrived[1:]:
        summed = summed + part[...]
    total[...] = summed
    for b in range(own):
        out[:, b * BLK : (b + 1) * BLK] = total[pl.ds(b, rows, stride=own), :]


def swap(value, axis, distance):
    count = lax.axis_size(axis)
    return lax.ppermute(value, axis, [(i, i ^ distance) for i in range(count)])


def exchange(parts, axis, unit=1):
    there = [swap(parts[d], axis, d * unit) for d in range(len(parts) - 1, 0, -1)]
    return [parts[0]] + there[::-1]


def on_device(residual, margin, aggregate, local_factor, coarse_factor):
    pairs = lax.axis_size("sub") // 2
    grp_count = lax.axis_size("grp")
    rhs, own_width = residual.shape
    own = own_width // BLK
    rows = rhs // grp_count
    halo = margin.shape[1]
    pad = 8
    begin = 2 * own * rows + pad
    f32 = jnp.float32
    sds = jax.ShapeDtypeStruct
    _, depth, width = local_factor.shape
    coarse_depth, coarse_width = coarse_factor.shape
    blocks = width // BLK
    in_hbm = functools.partial(pltpu.with_memory_space_constraint, memory_space=pltpu.HBM)
    aggregate = aggregate.reshape(1, own)
    local_factor = in_hbm(local_factor)
    coarse_factor = in_hbm(coarse_factor)

    near = swap(residual, "sub", 1)
    near_names = swap(aggregate, "sub", 1)
    held, mine, names = call(
        functools.partial(stage_kernel, own, rows),
        (sds(residual.shape, f32), sds((own * rows, BLK), f32), sds((1, own), f32)),
        [HBM, HBM],
        [
            pltpu.VMEM((own * rhs, BLK), f32),
            pltpu.VMEM((1, own), jnp.int32),
            pltpu.SemaphoreType.DMA((2,)),
        ],
        moved=8 * rhs * own_width,
    )(in_hbm(residual), in_hbm(aggregate))
    margin = in_hbm(margin)
    *outgoing, away, place = call(
        functools.partial(pack_kernel, own, rows, pad),
        [sds((begin + halo * rhs, BLK), f32)] * pairs
        + [sds((halo, BLK), jnp.int32), sds((2 * pairs * own, BLK), jnp.int32)],
        [HBM] + [VMEM] * 5,
        [
            pltpu.VMEM((own * rhs, BLK), f32),
            pltpu.SMEM(margin.shape, jnp.int32),
            pltpu.SemaphoreType.DMA,
        ],
    )(margin, held, mine, names, near_names, near)
    arrived = exchange(outgoing, "sub", 2)
    quarter = coarse_depth // 4
    tile = min(512, depth // 2)
    chunk = depth // 8
    coarse_held = sds(coarse_factor.shape, coarse_factor.dtype)
    begun, local_factor, coarse_part = call(
        functools.partial(load_kernel, chunk, tile),
        (
            sds((rhs, depth), f32),
            sds(local_factor.shape, local_factor.dtype),
            coarse_held,
        ),
        [VMEM, HBM, HBM, pl.BlockSpec(memory_space=pl.ANY)],
        [
            pltpu.SemaphoreType.DMA((depth // chunk,)),
            pltpu.SemaphoreType.DMA((4,)),
        ],
        flops=2 * rhs * depth * own_width,
        moved=2 * depth * width + 2 * quarter * coarse_width,
    )(held, local_factor, coarse_factor, arrived[0])
    chunk = max(16, quarter // 8)
    count = coarse_width // BLK
    *fine, coarse_part, member, sums = call(
        functools.partial(fine_kernel, own, rows, begin, chunk, tile, pairs),
        [sds((rows * blocks, BLK), f32)] * grp_count
        + [
            coarse_held,
            sds((2 * pairs * own, count), f32),
            sds((rows * count, BLK), f32),
        ],
        [VMEM, VMEM, VMEM, HBM, VMEM] + [VMEM] * pairs,
        [pltpu.VMEM((rhs * blocks, BLK), f32), pltpu.SemaphoreType.DMA((quarter // chunk,))],
        flops=4 * rhs * depth * width,
        moved=2 * depth * width + 2 * quarter * coarse_width,
        input_output_aliases={4: grp_count},
    )(away, begun, local_factor, coarse_factor, coarse_part, *arrived[::-1])
    panels = exchange(fine, "grp")
    lower = coarse_depth - 2 * quarter
    size = own * rows
    spread, _ = call(
        functools.partial(coarse_kernel, own, rows, chunk, tile),
        (sds((2 * pairs, size, BLK), f32), coarse_held),
        [VMEM, HBM, VMEM, VMEM],
        [
            pltpu.VMEM((rows * count, BLK), f32),
            pltpu.VMEM((rows, coarse_depth), f32),
            pltpu.SemaphoreType.DMA((lower // chunk,)),
        ],
        flops=4 * rows * coarse_depth * coarse_width,
        moved=2 * coarse_depth * coarse_width,
        input_output_aliases={0: 1},
    )(coarse_part, coarse_factor, member, sums)
    field = sds((pairs, size, BLK), f32)
    kept, crossing = call(
        functools.partial(merge_kernel, own, rows, grp_count, halo),
        [field, field],
        [VMEM] * (2 + grp_count),
    )(place, spread, *panels)
    back = call(add_kernel, [sds((size, BLK), f32)] * pairs, [VMEM, VMEM])(
        kept, swap(crossing, "sub", 1)
    )
    return call(
        functools.partial(last_kernel, own, rows),
        sds((rows, own_width), f32),
        [VMEM] * pairs,
        [pltpu.VMEM((size, BLK), f32)],
    )(*exchange(list(back), "sub", 2)[::-1])


def solution(mesh):
    placed = (P(None, "sub"), P(), P("sub"), P("sub", "grp", None), P("sub", None))
    return jax.shard_map(
        on_device, mesh=mesh, in_specs=placed, out_specs=P("grp", "sub"), check_vma=False
    )
```

```python
import functools

import jax
import jax.numpy as jnp
from jax import lax
from jax.experimental import pallas as pl
from jax.experimental.pallas import tpu as pltpu
from jax.sharding import PartitionSpec as P

BLK = 128
MIB = 1024 * 1024
VMEM = pl.BlockSpec(memory_space=pltpu.VMEM)
SMEM = pl.BlockSpec(memory_space=pltpu.SMEM)
HBM = pl.BlockSpec(memory_space=pltpu.HBM)
NT = (((1,), (1,)), ((), ()))
TN = (((0,), (0,)), ((), ()))


def call(kernel, out, specs, scratch=(), limit=12 * MIB, flops=0, moved=0, **options):
    return pl.pallas_call(
        kernel,
        out_shape=out,
        in_specs=specs,
        out_specs=jax.tree.map(lambda _: VMEM, out),
        scratch_shapes=scratch,
        compiler_params=pltpu.CompilerParams(vmem_limit_bytes=limit),
        cost_estimate=pl.CostEstimate(flops=flops, bytes_accessed=moved, transcendentals=0),
        **options,
    )


def mm(left, right, dims=(((1,), (0,)), ((), ()))):
    return lax.dot_general(left, right, dims, preferred_element_type=jnp.float32)


def split3(value):
    high = value.astype(jnp.bfloat16)
    rest = value - high.astype(jnp.float32)
    middle = rest.astype(jnp.bfloat16)
    low = (rest - middle.astype(jnp.float32)).astype(jnp.bfloat16)
    return [high, middle, low]


def stage_kernel(own, rows, residual_hbm, aggregate_hbm, residual, mine, names, block_rows, aggregate, sems):
    pairs = ((residual_hbm, residual), (aggregate_hbm, aggregate))
    copies = [pltpu.make_async_copy(a, b, sems.at[i]) for i, (a, b) in enumerate(pairs)]
    start(copies)
    for copy in copies:
        copy.wait()
    names[...] = aggregate[...].astype(jnp.float32)
    mine[...] = rows_of(residual, own, rows, block_rows)


def rows_of(residual, own, rows, block_rows):
    rhs = residual.shape[0]
    for b in range(own):
        block_rows[pl.ds(b, rhs, stride=own), :] = residual[:, b * BLK : (b + 1) * BLK]
    first = lax.axis_index("grp") * rows * own
    return block_rows[pl.ds(pl.multiple_of(first, 8), rows * own), :]


def pack_kernel(own, rows, pad, margin_hbm, residual, mine, names, near_names, near, *refs):
    *outs, away, place, block_rows, margin, sem = refs
    copy = pltpu.make_async_copy(margin_hbm, margin, sem)
    copy.start()
    halo = margin.shape[1]
    rhs = residual.shape[0]
    me = lax.axis_index("sub")
    size = own * rows
    both = [mine[...], rows_of(near, own, rows, block_rows)]
    labels = [names[...], near_names[...].astype(jnp.float32)]
    at = 2 * size
    for out in outs:
        out[at : at + pad, :] = jnp.zeros((pad, BLK), jnp.float32)
        for i in range(2):
            out[i * size : (i + 1) * size, :] = both[i]
            out[at + i : at + i + 1, :own] = labels[i]
    place[...] = jnp.zeros(place.shape, jnp.int32)
    copy.wait()
    for k in range(halo):
        block = margin[me, k]
        owner = block // own
        distance = me ^ owner
        away[k : k + 1, :] = jnp.full((1, BLK), distance // 2, jnp.int32)
        row = distance * own + block - owner * own
        place[pl.ds(row, 1), :] = jnp.full((1, BLK), k + 1, jnp.int32)
    for e, out in enumerate(outs):
        target = me ^ (2 * e)
        for k in range(halo):
            block = margin[target, k]
            owner = block // own
            where = pl.ds(pl.multiple_of((block - owner * own) * BLK, BLK), BLK)
            out[at + pad + k * rhs : at + pad + (k + 1) * rhs, :] = jnp.where(
                owner == me, residual[:, where], near[:, where]
            )


def panel_copies(source, target, chunk, sems, first=0):
    copies = []
    for n in range(target.shape[0] // chunk):
        span = pl.ds(first + n * chunk, chunk)
        copies.append(
            pltpu.make_async_copy(source.at[span], target.at[pl.ds(n * chunk, chunk)], sems.at[n])
        )
    return copies


def start(copies):
    for copy in copies:
        copy.start()


def first_product(factor, right, tile):
    tile = min(tile, factor.shape[0])
    parts = [
        mm(right, factor[n * tile : (n + 1) * tile, :], NT) for n in range(factor.shape[0] // tile)
    ]
    return jnp.concatenate(parts, axis=1)


def in_own_block(body):
    pl.when(lax.axis_index("sub") >= 0)(body)


def load_kernel(
    chunk, tile, residual, fine_hbm, coarse_hbm, after, inner, fine, coarse, sems, more
):
    depth = fine.shape[1]
    own_width = residual.shape[1]
    half = depth // 2
    each = half // chunk
    start(panel_copies(fine_hbm.at[0], fine.at[0], chunk, sems))
    quarter = coarse.shape[0] // 4
    late = panel_copies(coarse_hbm, coarse.at[pl.ds(0, quarter)], quarter // 4, more)

    def step(n, carry):
        for i in range(each):
            span = pl.ds(pl.multiple_of(n * half + i * chunk, chunk), chunk)
            pltpu.make_async_copy(fine_hbm.at[0, span], fine.at[0, span], sems.at[n * each + i]).wait()
        pl.when(n == 0)(lambda: start(late))
        local = residual[...].astype(jnp.bfloat16)
        for i in range(half // tile):
            at = pl.multiple_of(n * half + i * tile, tile)
            rows = fine[0, pl.ds(at, tile), pl.ds(0, own_width)]
            inner[:, pl.ds(at, tile)] = mm(local, rows, NT)
        return carry

    lax.fori_loop(0, 2, step, 0)
    for copy in late:
        copy.wait()


def form_sums(own, rows, coarse, arrived, named, table):
    size = own * rows
    sources = 2 * len(arrived)
    parts = [(part, i) for part in arrived for i in range(2)]
    names = jnp.concatenate(
        [part[2 * size + i : 2 * size + i + 1, :] for part, i in parts], axis=0
    ).T
    catalog = lax.broadcasted_iota(jnp.int32, (own, coarse), 1).astype(jnp.float32)
    member = jnp.concatenate(
        [(names[:own, s : s + 1] == catalog).astype(jnp.float32) for s in range(sources)], axis=0
    ).astype(jnp.bfloat16)
    whole = jnp.concatenate(
        [
            jnp.concatenate(
                [part[i * size + r * own : i * size + (r + 1) * own, :] for part, i in parts],
                axis=0,
            )
            for r in range(rows)
        ],
        axis=1,
    )
    ones = jnp.ones((own * sources, BLK), jnp.bfloat16)
    span = rows * BLK
    found = mm(member, jnp.concatenate(split3(whole) + [ones], axis=1), TN)
    sums = found[:, :span] + found[:, span : 2 * span] + found[:, 2 * span : 3 * span]
    counts = jnp.maximum(found[:, 3 * span :], 1.0)
    for r in range(rows):
        table[r * coarse : (r + 1) * coarse, :] = sums[:, r * BLK : (r + 1) * BLK] / counts
    named[...] = member.astype(jnp.float32)


def fine_kernel(own, rows, begin, chunk, tile, pairs, away, begun, factor, coarse_hbm, given, *refs):
    arrived = refs[:pairs][::-1]
    *outs, coarse, named, sums, table, sems = refs[pairs:]
    quarter = coarse.shape[0] // 4
    copies = panel_copies(coarse_hbm, coarse.at[pl.ds(quarter, quarter)], chunk, sems, quarter)
    start(copies)
    rhs = begun.shape[0]
    halo = away.shape[0]
    depth, width = factor.shape[1:]
    blocks = width // BLK
    group = lax.axis_index("grp")
    tiles = []
    for k in range(halo):
        span = slice(begin + k * rhs, begin + (k + 1) * rhs)
        distance = away[k : k + 1, :]
        part = arrived[0][span, :]
        for e in range(1, pairs):
            part = jnp.where(distance == e, arrived[e][span, :], part)
        tiles.append(part.astype(jnp.bfloat16))
    form_sums(own, rows, coarse.shape[1] // BLK, arrived, named, sums)
    local = jnp.concatenate(tiles, axis=1)
    far = factor.at[0, :, pl.ds(own * BLK, halo * BLK)]
    mid = (begun[...] + first_product(far, local, tile)).astype(jnp.bfloat16)
    for n in range(width // 256):
        part = mm(mid, factor[0, :, n * 256 : (n + 1) * 256])
        for i in range(256 // BLK):
            b = n * (256 // BLK) + i
            table[pl.ds(b, rhs, stride=blocks), :] = part[:, i * BLK : (i + 1) * BLK]
    size = rows * blocks
    for d, out in enumerate(outs):
        out[...] = table[pl.ds(pl.multiple_of((group ^ d) * size, 8), size), :]

    @in_own_block
    def _():
        for copy in copies:
            copy.wait()


def coarse_kernel(own, rows, chunk, tile, given, factor_hbm, member, sums, out, factor, table, begun, sems):
    depth, width = factor.shape
    done = depth // 2
    held, lower = factor.at[pl.ds(0, done)], factor.at[pl.ds(done, depth - done)]
    copies = panel_copies(factor_hbm, lower, chunk, sems, done)
    start(copies)
    coarse = width // BLK
    span = rows * BLK

    def right():
        parts = [sums[pl.ds(j, rows, stride=coarse), :] for j in range(coarse)]
        return jnp.concatenate(parts, axis=1).astype(jnp.bfloat16)

    first = right()
    begun[:, :done] = first_product(held, first, tile)

    @in_own_block
    def _():
        for copy in copies:
            copy.wait()
        begun[:, done:] = first_product(lower, right(), tile)
        mid = begun[...].astype(jnp.bfloat16)
        for n in range(width // 256):
            where = slice(n * 256, (n + 1) * 256)
            part = mm(mid, factor[:, where])
            for i in range(256 // BLK):
                j = n * (256 // BLK) + i
                table[pl.ds(j, rows, stride=coarse), :] = part[:, i * BLK : (i + 1) * BLK]
        solved = jnp.concatenate([table[r * coarse : (r + 1) * coarse, :] for r in range(rows)], axis=1)
        spread = mm(member[...].astype(jnp.bfloat16), jnp.concatenate(split3(solved), axis=1))
        spread = spread[:, :span] + spread[:, span : 2 * span] + spread[:, 2 * span :]
        for s in range(out.shape[0]):
            for r in range(rows):
                out[s, r * own : (r + 1) * own, :] = spread[
                    s * own : (s + 1) * own, r * BLK : (r + 1) * BLK
                ]


def merge_kernel(own, rows, groups, halo, place, spread, *refs):
    arrived = refs[:groups]
    kept, near = refs[groups:]
    blocks = own + halo
    total = arrived[0][...]
    for part in arrived[1:]:
        total = total + part[...]
    for d in range(spread.shape[0]):
        where = place[d * own : (d + 1) * own, :]
        hits = [where == k + 1 for k in range(halo)] if d else []
        out = near if d % 2 else kept
        for r in range(rows):
            span = slice(r * own, (r + 1) * own)
            field = spread[d, span, :]
            if d == 0:
                field = field + total[r * blocks : r * blocks + own, :]
            for k, hit in enumerate(hits):
                row = r * blocks + own + k
                field = field + jnp.where(hit, total[row : row + 1, :], 0.0)
            out[d // 2, span, :] = field


def add_kernel(kept, arrived, *outs):
    for e, out in enumerate(outs):
        out[...] = kept[e] + arrived[e]


def last_kernel(own, rows, *refs):
    *arrived, out, total = refs
    summed = arrived[0][...]
    for part in arrived[1:]:
        summed = summed + part[...]
    total[...] = summed
    for b in range(own):
        out[:, b * BLK : (b + 1) * BLK] = total[pl.ds(b, rows, stride=own), :]


def swap(value, axis, distance):
    count = lax.axis_size(axis)
    return lax.ppermute(value, axis, [(i, i ^ distance) for i in range(count)])


def exchange(parts, axis, unit=1):
    there = [swap(parts[d], axis, d * unit) for d in range(len(parts) - 1, 0, -1)]
    return [parts[0]] + there[::-1]


def on_device(residual, margin, aggregate, local_factor, coarse_factor):
    pairs = lax.axis_size("sub") // 2
    grp_count = lax.axis_size("grp")
    rhs, own_width = residual.shape
    own = own_width // BLK
    rows = rhs // grp_count
    halo = margin.shape[1]
    pad = 8
    begin = 2 * own * rows + pad
    f32 = jnp.float32
    sds = jax.ShapeDtypeStruct
    _, depth, width = local_factor.shape
    coarse_depth, coarse_width = coarse_factor.shape
    blocks = width // BLK
    in_hbm = functools.partial(pltpu.with_memory_space_constraint, memory_space=pltpu.HBM)
    aggregate = aggregate.reshape(1, own)
    local_factor = in_hbm(local_factor)
    coarse_factor = in_hbm(coarse_factor)

    near = swap(residual, "sub", 1)
    near_names = swap(aggregate, "sub", 1)
    held, mine, names = call(
        functools.partial(stage_kernel, own, rows),
        (sds(residual.shape, f32), sds((own * rows, BLK), f32), sds((1, own), f32)),
        [HBM, HBM],
        [
            pltpu.VMEM((own * rhs, BLK), f32),
            pltpu.VMEM((1, own), jnp.int32),
            pltpu.SemaphoreType.DMA((2,)),
        ],
        moved=8 * rhs * own_width,
    )(in_hbm(residual), in_hbm(aggregate))
    margin = in_hbm(margin)
    *outgoing, away, place = call(
        functools.partial(pack_kernel, own, rows, pad),
        [sds((begin + halo * rhs, BLK), f32)] * pairs
        + [sds((halo, BLK), jnp.int32), sds((2 * pairs * own, BLK), jnp.int32)],
        [HBM] + [VMEM] * 5,
        [
            pltpu.VMEM((own * rhs, BLK), f32),
            pltpu.SMEM(margin.shape, jnp.int32),
            pltpu.SemaphoreType.DMA,
        ],
    )(margin, held, mine, names, near_names, near)
    arrived = exchange(outgoing, "sub", 2)
    quarter = coarse_depth // 4
    tile = min(512, depth // 2)
    chunk = depth // 8
    coarse_held = sds(coarse_factor.shape, coarse_factor.dtype)
    begun, local_factor, coarse_part = call(
        functools.partial(load_kernel, chunk, tile),
        (
            sds((rhs, depth), f32),
            sds(local_factor.shape, local_factor.dtype),
            coarse_held,
        ),
        [VMEM, HBM, HBM, pl.BlockSpec(memory_space=pl.ANY)],
        [
            pltpu.SemaphoreType.DMA((depth // chunk,)),
            pltpu.SemaphoreType.DMA((4,)),
        ],
        flops=2 * rhs * depth * own_width,
        moved=2 * depth * width + 2 * quarter * coarse_width,
    )(held, local_factor, coarse_factor, arrived[0])
    chunk = quarter // 4
    count = coarse_width // BLK
    *fine, coarse_part, member, sums = call(
        functools.partial(fine_kernel, own, rows, begin, chunk, tile, pairs),
        [sds((rows * blocks, BLK), f32)] * grp_count
        + [
            coarse_held,
            sds((2 * pairs * own, count), f32),
            sds((rows * count, BLK), f32),
        ],
        [VMEM, VMEM, VMEM, HBM, VMEM] + [VMEM] * pairs,
        [pltpu.VMEM((rhs * blocks, BLK), f32), pltpu.SemaphoreType.DMA((quarter // chunk,))],
        flops=4 * rhs * depth * width,
        moved=2 * depth * width + 2 * quarter * coarse_width,
        input_output_aliases={4: grp_count},
    )(away, begun, local_factor, coarse_factor, coarse_part, *arrived[::-1])
    panels = exchange(fine, "grp")
    lower = coarse_depth - 2 * quarter
    size = own * rows
    spread, _ = call(
        functools.partial(coarse_kernel, own, rows, chunk, tile),
        (sds((2 * pairs, size, BLK), f32), coarse_held),
        [VMEM, HBM, VMEM, VMEM],
        [
            pltpu.VMEM((rows * count, BLK), f32),
            pltpu.VMEM((rows, coarse_depth), f32),
            pltpu.SemaphoreType.DMA((lower // chunk,)),
        ],
        flops=4 * rows * coarse_depth * coarse_width,
        moved=2 * coarse_depth * coarse_width,
        input_output_aliases={0: 1},
    )(coarse_part, coarse_factor, member, sums)
    field = sds((pairs, size, BLK), f32)
    kept, crossing = call(
        functools.partial(merge_kernel, own, rows, grp_count, halo),
        [field, field],
        [VMEM] * (2 + grp_count),
    )(place, spread, *panels[::-1])
    back = call(add_kernel, [sds((size, BLK), f32)] * pairs, [VMEM, VMEM])(
        kept, swap(crossing, "sub", 1)
    )
    return call(
        functools.partial(last_kernel, own, rows),
        sds((rows, own_width), f32),
        [VMEM] * pairs,
        [pltpu.VMEM((size, BLK), f32)],
    )(*exchange(list(back), "sub", 2)[::-1])


def solution(mesh):
    placed = (P(None, "sub"), P(), P("sub"), P("sub", "grp", None), P("sub", None))
    return jax.shard_map(
        on_device, mesh=mesh, in_specs=placed, out_specs=P("grp", "sub"), check_vma=False
    )
```
